128 devices in a mesh: ctx: 64 (over x, z, y), fsdp: 2 (over core).
Axes of the slice: x: 4, y: 4, z: 4, core: 2. Of those that a mesh axis runs over, the one named last changes fastest.
Arguments:
- tokens: bfloat16 [2, 16384, 640], P('fsdp', 'ctx'), may hold values from -6 to 6
- positions: int32 [2, 16384], P('fsdp'), may hold values from 0 to 20479, as said below
- gain_attn: bfloat16 [640], P('fsdp'), may hold values from 0.25 to 1.75
- w_query: bfloat16 [640, 1024], P(None, 'fsdp'), may hold values from -0.25 to 0.25
- w_key: bfloat16 [640, 256], P(None, 'fsdp'), may hold values from -0.25 to 0.25
- w_value: bfloat16 [640, 256], P(None, 'fsdp'), may hold values from -0.25 to 0.25
- w_out: bfloat16 [1024, 640], P('fsdp'), may hold values from -1 to 1
- gain_ffn: bfloat16 [640], P('fsdp'), may hold values from 0.25 to 1.75
- w_gate: bfloat16 [640, 2048], P(None, 'fsdp'), may hold values from -0.25 to 0.25
- w_up: bfloat16 [640, 2048], P(None, 'fsdp'), may hold values from -0.25 to 0.25
- w_down: bfloat16 [2048, 640], P('fsdp'), may hold values from -0.125 to 0.125
- grad_out: bfloat16 [2, 16384, 640], P('fsdp', 'ctx'), may hold values from -6 to 6
Outputs:
- output: bfloat16 [2, 16384, 640], P('fsdp', 'ctx')
- grad_tokens: float32 [2, 16384, 640], P('fsdp', 'ctx')
- grad_gain_attn: float32 [640], P('fsdp')
- grad_w_query: float32 [640, 1024], P(None, 'fsdp')
- grad_w_key: float32 [640, 256], P(None, 'fsdp')
- grad_w_value: float32 [640, 256], P(None, 'fsdp')
- grad_w_out: float32 [1024, 640], P('fsdp')
- grad_gain_ffn: float32 [640], P('fsdp')
- grad_w_gate: float32 [640, 2048], P(None, 'fsdp')
- grad_w_up: float32 [640, 2048], P(None, 'fsdp')
- grad_w_down: float32 [2048, 640], P('fsdp')
The draws below stay inside these ranges and needn't reach their ends.
Inputs may be any that keep to these rules, and one draw needn't show every extreme that they name: Along each sequence the positions start at 0 and rise by 1 or 2 from each token to the next, by 2 at exactly 4096 of the steps.
All inputs are finite; a program needn't handle non-finite values.
Results may differ from the reference program's by a relative error of at most 0.018.
Values may be sent and summed in bfloat16 or wider, within the bound.
No kernel may reach another device: no remote copies, remote signals or barrier semaphores. Data moves between devices by JAX's collectives and lax.ppermute only.
A program may use at most 128 MiB of HBM per device.

```python
import math
import jax
import jax.numpy as jnp
from jax import lax

D = 640
HEADS = 4
HEAD = 256
FF = 2048
WINDOW = 512
SEQS = 2
LENGTH = 16384


def draw_positions(key, part):
    key = jax.random.fold_in(key, 7)
    step_count = LENGTH - 1
    order = jnp.broadcast_to(jnp.arange(step_count, dtype=jnp.int32), (SEQS, step_count))
    shuffled = jax.random.permutation(key, order, axis=1, independent=True)
    step_size = jnp.where(shuffled < LENGTH // 4, 2, 1).astype(jnp.int32)
    step_size = jnp.concatenate([jnp.zeros((SEQS, 1), jnp.int32), step_size], axis=1)
    return jnp.cumsum(step_size, axis=1).astype(jnp.int32)


def block_levels(stream_key, dims, split, smallest, high):
    def one(position, blocks):
        steps = jax.random.uniform(jax.random.fold_in(jax.random.fold_in(stream_key, 6), position), (blocks,), jnp.float32, smallest / len(split), high / len(split))
        return jnp.repeat(jnp.exp(steps), dims[position] // blocks).reshape((-1,) + (1,) * (len(dims) - position - 1))

    loudness = one(*split[0])
    for cut in split[1:]:
        loudness = loudness * one(*cut)
    return loudness


def scatter_about(rng, shape, spread, bound, cuts=(), kind=jnp.bfloat16):
    array = jax.random.normal(rng, shape, jnp.float32) * spread
    if len(cuts) > 0:
        array = block_levels(rng, shape, cuts, -0.22, 0.18) * array
    return jnp.clip(array, min=-bound, max=bound).astype(kind)


def setup_inputs(seed: int = 0) -> dict:
    key_list = jax.random.split(jax.random.key(seed), 13)
    return {
        "tokens": scatter_about(key_list[0], (SEQS, LENGTH, D), 1.0, 6.0, ((0, 2), (1, 64))),
        "positions": draw_positions(jax.random.fold_in(key_list[12], 71), 0),
        "gain_attn": jnp.clip(1.0 + 0.15 * jax.random.normal(key_list[2], (D,), jnp.float32), 0.25, 1.75).astype(jnp.bfloat16),
        "w_query": scatter_about(key_list[3], (D, HEADS * HEAD), D ** -0.5, 0.25, ((1, 2),)),
        "w_key": scatter_about(key_list[4], (D, HEAD), D ** -0.5, 0.25, ((1, 2),)),
        "w_value": scatter_about(key_list[5], (D, HEAD), D ** -0.5, 0.25, ((1, 2),)),
        "w_out": scatter_about(key_list[6], (HEADS * HEAD, D), (HEADS * HEAD // 32) ** -0.5, 1.0, ((0, 2),)),
        "gain_ffn": jnp.clip(1.0 + 0.15 * jax.random.normal(key_list[7], (D,), jnp.float32), 0.25, 1.75).astype(jnp.bfloat16),
        "w_gate": scatter_about(key_list[8], (D, FF), D ** -0.5, 0.25, ((1, 2),)),
        "w_up": scatter_about(key_list[9], (D, FF), D ** -0.5, 0.25, ((1, 2),)),
        "w_down": scatter_about(key_list[10], (FF, D), FF ** -0.5, 0.125, ((0, 2),)),
        "grad_out": scatter_about(key_list[11], (SEQS, LENGTH, D), 1.0, 6.0, ((0, 2), (1, 64))),
    }


@jax.custom_vjp
def low(v):
    return lax.optimization_barrier(v.astype(jnp.bfloat16)).astype(jnp.float32)

@jax.custom_vjp
def low_back(v):
    return v

def low_keep(v):
    return (low(v), None)

def low_pass(kept, grad):
    return (grad,)

def back_keep(v):
    return (v, None)

def back_low(kept, grad):
    return (low(grad),)
low.defvjp(low_keep, low_pass)
low_back.defvjp(back_keep, back_low)
epsilon = 1e-06
rope_base = 10000.0
highest = lax.Precision.HIGHEST

def rms_scale(values, gain_vec):
    return values * lax.rsqrt(lax.optimization_barrier(jnp.mean(values * values, axis=-1, keepdims=True)) + epsilon) * gain_vec

def rope_angles(token_pos):
    half_size = HEAD // 2
    frequency = rope_base ** (-(jnp.arange(half_size, dtype=jnp.float32) * 2.0 / HEAD))
    return token_pos.astype(jnp.float32)[:, None] * frequency[None, :]

def rotate(values, angles):
    half_size = values.shape[-1] // 2
    first_half = values[..., :half_size]
    second_half = values[..., half_size:]
    cosine = jnp.cos(angles)
    sine_part = jnp.sin(angles)
    return jnp.concatenate([first_half * cosine - second_half * sine_part, second_half * cosine + first_half * sine_part], axis=-1)

def attend(queries, key_rows, values, token_pos):
    block_rows = math.gcd(LENGTH, 512)
    block_count = LENGTH // block_rows
    key_pad = jnp.concatenate([jnp.zeros((WINDOW, HEAD), key_rows.dtype), key_rows], axis=0)
    value_pad = jnp.concatenate([jnp.zeros((WINDOW, HEAD), values.dtype), values], axis=0)
    pos_pad = jnp.concatenate([jnp.full((WINDOW,), -2 * WINDOW, jnp.int32), token_pos.astype(jnp.int32)])

    @jax.checkpoint
    def one_block(block_id):
        row_start = (block_id * block_rows).astype(jnp.int32)
        query_blk = lax.dynamic_slice_in_dim(queries, row_start, block_rows, 0)
        key_blk = lax.dynamic_slice_in_dim(key_pad, row_start, block_rows + WINDOW, 0)
        value_blk = lax.dynamic_slice_in_dim(value_pad, row_start, block_rows + WINDOW, 0)
        query_pos = lax.dynamic_slice_in_dim(token_pos.astype(jnp.int32), row_start, block_rows, 0)
        key_pos = lax.dynamic_slice_in_dim(pos_pad, row_start, block_rows + WINDOW, 0)
        distance = query_pos[:, None] - key_pos[None, :]
        allowed = (distance >= 0) & (distance < WINDOW)
        scores = low_back(jnp.einsum('thd,kd->htk', query_blk, key_blk, precision=highest))
        scores = jnp.where(allowed[None], scores, -1e+30)
        top_score = lax.optimization_barrier(jnp.max(scores, axis=-1, keepdims=True))
        exp_scores = jnp.exp(scores - top_score)
        attn_probs = low(exp_scores / lax.optimization_barrier(jnp.sum(exp_scores, axis=-1, keepdims=True)))
        mixed_vals = jnp.einsum('htk,kd->thd', attn_probs, value_blk, precision=highest)
        return mixed_vals.reshape(block_rows, HEADS * HEAD)
    blocks = lax.map(one_block, jnp.arange(block_count, dtype=jnp.int32))
    return blocks.reshape(LENGTH, HEADS * HEAD)

def forward(tokens_f, gain_attn, w_query, w_key, w_value, w_out, gain_ffn, w_gate, w_up, w_down, token_pos):
    angles = rope_angles(token_pos)
    normed = low(rms_scale(tokens_f, gain_attn))
    queries = low_back(jnp.dot(normed, w_query, precision=highest)).reshape(LENGTH, HEADS, HEAD)
    key_rows = low_back(jnp.dot(normed, w_key, precision=highest))
    values = low_back(low(jnp.dot(normed, w_value, precision=highest)))
    queries = low(rotate(queries, angles[:, None, :]) * HEAD ** (-0.5))
    key_rows = low(rotate(key_rows, angles))
    context = low_back(low(attend(queries, key_rows, values, token_pos)))
    after_attn = tokens_f + low_back(jnp.dot(context, w_out, precision=highest))
    normed_ffn = low(rms_scale(after_attn, gain_ffn))
    gate_proj = low_back(jnp.dot(normed_ffn, w_gate, precision=highest))
    up_proj = low_back(jnp.dot(normed_ffn, w_up, precision=highest))
    hidden = low(jax.nn.gelu(gate_proj, approximate=True) * up_proj)
    return after_attn + low_back(jnp.dot(hidden, w_down, precision=highest))

def reference(tokens, positions, gain_attn, w_query, w_key, w_value, w_out, gain_ffn, w_gate, w_up, w_down, grad_out):
    params = tuple((weight_in.astype(jnp.float32) for weight_in in (gain_attn, w_query, w_key, w_value, w_out, gain_ffn, w_gate, w_up, w_down)))

    def one_sequence(totals, inputs):
        seq_tokens, seq_pos, seq_grad = inputs

        def run_block(tokens_f, *weights):
            return forward(tokens_f, *weights, seq_pos)
        output, pullback = jax.vjp(run_block, seq_tokens.astype(jnp.float32), *params)
        grad_list = pullback(seq_grad.astype(jnp.float32))
        totals = tuple((acc_grad + new_grad for acc_grad, new_grad in zip(totals, grad_list[1:])))
        return (totals, (output.astype(jnp.bfloat16), grad_list[0]))
    zero_grads = tuple((jnp.zeros(weight_in.shape, jnp.float32) for weight_in in params))
    totals, (outputs, grad_tokens) = lax.scan(one_sequence, zero_grads, (tokens, positions, grad_out))
    return (outputs, grad_tokens, totals[0], totals[1], totals[2], totals[3], totals[4], totals[5], totals[6], totals[7], totals[8])
```

```python
import functools

import jax
import jax.numpy as jnp
from jax import lax
from jax.experimental import pallas as pl
from jax.experimental.pallas import tpu as pltpu
from jax.sharding import PartitionSpec as P

D = 640
HEADS = 4
HEAD = 256
FF = 2048
WINDOW = 512
HALF = HEAD // 2
MINE = 2 * HEAD

epsilon = 1e-06
rope_base = 10000.0
neg_fill = -1e30
score_scale = HEAD ** (-0.5)
gelu_c = 0.7978845608028654
gelu_k = 0.044715

F32 = jnp.float32
BF16 = jnp.bfloat16
MIB = 1024 * 1024


def swap(x):
    return lax.ppermute(x, "fsdp", [(0, 1), (1, 0)])


def chip_pairs(move):
    pairs = []
    for x in range(4):
        for z in range(4):
            for y in range(4):
                for c in range(2):
                    tx, tz, ty = move(x, z, y, c)
                    target = (((tx % 4) * 4 + tz % 4) * 4 + ty % 4) * 2 + c
                    pairs.append((((x * 4 + z) * 4 + y) * 2 + c, target))
    return pairs


def shift_first(by):
    return chip_pairs(lambda x, z, y, c: (x + by, z, y) if c == 0 else (x, z, y + by))


def shift_second(by):
    return chip_pairs(lambda x, z, y, c: (x, z, y + by) if c == 0 else (x + by, z, y))


def shift_z(by):
    return chip_pairs(lambda x, z, y, c: (x, z + by, y))


def to_peers(parts, shift):
    return [
        lax.ppermute(part, ("ctx", "fsdp"), shift(by)) for part, by in zip(parts, (2, 1, -1))
    ]


def passed_along(shard, by):
    peers = lax.axis_size("ctx")
    pairs = [(i, i + by) for i in range(peers) if 0 <= i + by < peers]
    return lax.ppermute(shard, "ctx", pairs)


def dot(a, b):
    return lax.dot_general(a, b, (((1,), (0,)), ((), ())), preferred_element_type=F32)


def dot_nt(a, b):
    return lax.dot_general(a, b, (((1,), (1,)), ((), ())), preferred_element_type=F32)


def dot_tn(a, b):
    return lax.dot_general(a, b, (((0,), (0,)), ((), ())), preferred_element_type=F32)


def call(name, body, outs, ins, scalars=0, flops=0, vmem=56):
    smem = pl.BlockSpec(memory_space=pltpu.SMEM)
    whole = pl.BlockSpec(memory_space=pltpu.VMEM)
    moved = sum(x.size * x.dtype.itemsize for x in ins)
    shapes = [jax.ShapeDtypeStruct(s, t) for s, t in outs]
    moved += sum(x.size * x.dtype.itemsize for x in shapes)
    return pl.pallas_call(
        body,
        out_shape=shapes,
        in_specs=[smem] * scalars + [whole] * (len(ins) - scalars),
        out_specs=[whole] * len(outs),
        compiler_params=pltpu.CompilerParams(vmem_limit_bytes=vmem * MIB),
        cost_estimate=pl.CostEstimate(flops=flops, bytes_accessed=moved, transcendentals=0),
        name=name,
    )(*ins)


def inv_rms(x):
    return lax.rsqrt(jnp.mean(x * x, axis=-1, keepdims=True) + epsilon)


def rotate_pair(a, b, c, s):
    return a * c - b * s, b * c + a * s


def query_body(tok, gain, wq_m, wq_o, cos, sin, normed, query):
    x = tok[...].astype(F32)
    n = (x * inv_rms(x) * gain[...]).astype(BF16)
    normed[...] = n
    c, s = cos[2 * 256 :, :], sin[2 * 256 :, :]
    for half, w in enumerate((wq_m, wq_o)):
        raw = dot(n, w[...])
        for head in range(2):
            a = raw[:, head * HEAD : head * HEAD + HALF]
            b = raw[:, head * HEAD + HALF : (head + 1) * HEAD]
            ra, rb = rotate_pair(a, b, c, s)
            at = half * MINE + head * HEAD
            query[:, at : at + HALF] = (ra * score_scale).astype(BF16)
            query[:, at + HALF : at + HEAD] = (rb * score_scale).astype(BF16)


def allowed_pairs(pos_col, pos_row):
    distance = pos_col[...] - pos_row[...]
    return (distance >= 0) & (distance < WINDOW)


def attend_body(
    tok, far_two, far_one, normed, gain, query, wkv, wo_m, wo_o, gain_two, cos, sin, pos_col,
    pos_row, normed_far, kv, context, lse, after, normed_two,
):
    for i, far in enumerate((far_two, far_one)):
        x = far[...].astype(F32)
        normed_far[i * 256 : (i + 1) * 256, :] = (x * inv_rms(x) * gain[...]).astype(BF16)
    for rows, n in ((slice(0, 512), normed_far), (slice(512, 768), normed)):
        raw = dot(n[...], wkv[...])
        ka, kb = rotate_pair(raw[:, :HALF], raw[:, HALF:HEAD], cos[rows, :], sin[rows, :])
        kv[rows, :HALF] = ka.astype(BF16)
        kv[rows, HALF:HEAD] = kb.astype(BF16)
        kv[rows, HEAD:] = raw[:, HEAD:].astype(BF16)
    ok = allowed_pairs(pos_col, pos_row)
    for head in range(HEADS):
        cols = slice(head * HEAD, (head + 1) * HEAD)
        scores = jnp.where(ok, dot_nt(query[:, cols], kv[:, :HEAD]), neg_fill)
        top = jnp.max(scores, axis=-1, keepdims=True)
        exps = jnp.exp(scores - top)
        total = jnp.sum(exps, axis=-1, keepdims=True)
        lse[:, head * 128 : (head + 1) * 128] = jnp.broadcast_to(top + jnp.log(total), (256, 128))
        probs = (exps * (1.0 / total)).astype(BF16)
        context[:, cols] = dot(probs, kv[:, HEAD:]).astype(BF16)
    h = tok[...].astype(F32) + (
        dot(context[:, :MINE], wo_m[...]) + dot(context[:, MINE:], wo_o[...])
    )
    after[...] = h
    normed_two[...] = (h * inv_rms(h) * gain_two[...]).astype(BF16)


FFN_STEP = 512


def ffn_body(
    after, normed_two, gain_two, wg_m, wg_o, wu_m, wu_o, wd_m, wd_o, gy,
    out, hid_m, hid_o, dg_m, dg_o, du_m, du_o, grad_after, grad_after_low, grad_gain,
):
    n = normed_two[...]
    y = gy[...]
    total = None
    grad_n = None
    for wg, wu, wd, hid, dg, du in (
        (wg_o, wu_o, wd_o, hid_o, dg_o, du_o),
        (wg_m, wu_m, wd_m, hid_m, dg_m, du_m),
    ):
        for at in range(0, FF // 2, FFN_STEP):
            cols = slice(at, at + FFN_STEP)
            gate = dot(n, wg[:, cols])
            up = dot(n, wu[:, cols])
            grad_hidden = dot_nt(y, wd[cols, :])
            square = gate * gate
            t = jnp.tanh(gelu_c * gate * (1.0 + gelu_k * square))
            one_t = 0.5 + 0.5 * t
            act = gate * one_t
            slope = one_t + 0.5 * gate * (1.0 - t * t) * (gelu_c * (1.0 + 3.0 * gelu_k * square))
            hidden = (act * up).astype(BF16)
            grad_gate = (grad_hidden * up * slope).astype(BF16)
            grad_up = (grad_hidden * act).astype(BF16)
            hid[:, cols] = hidden
            dg[:, cols] = grad_gate
            du[:, cols] = grad_up
            part = dot(hidden, wd[cols, :])
            total = part if total is None else total + part
            part = dot_nt(grad_gate, wg[:, cols]) + dot_nt(grad_up, wu[:, cols])
            grad_n = part if grad_n is None else grad_n + part
    h = after[...]
    out[...] = (h + total).astype(BF16)
    r = inv_rms(h)
    dn = grad_n * gain_two[...]
    grad_gain[...] = jnp.sum(grad_n * h * r, axis=0, keepdims=True)
    ga = y.astype(F32) + r * dn - h * (r * r * r * jnp.mean(dn * h, axis=-1, keepdims=True))
    grad_after[...] = ga
    grad_after_low[...] = ga.astype(BF16)


ORDER = (0, 2, 1, 3)
F_ROWS = 4480
A_ROWS = 1024


def place(i, by):
    return lax.rem(i + by, 4)


def ffn_grads_body(
    where, hid_m, hid_r, dg_m, dg_r, du_m, du_r, n, n_r, gy, gy_r, ctx, ctx_r, ga, ga_r, *outs
):
    first = where[1]
    for out, by in zip(outs, ORDER):
        j = place(first, by)
        cols = pl.ds(pl.multiple_of(j * 256, 256), 256)
        for at, left, right in ((0, dg_m, dg_r), (1280, du_m, du_r)):
            g = dot_tn(n[...], left[:, cols]) + dot_tn(n_r[...], right[:, cols])
            out[at : at + 640, :] = g[:, :128].astype(BF16)
            out[at + 640 : at + 1280, :] = g[:, 128:].astype(BF16)
        g = dot_tn(hid_m[:, cols], gy[...]) + dot_tn(hid_r[:, cols], gy_r[...])
        for b in range(5):
            out[2560 + b * 256 : 2816 + b * 256, :] = g[:, b * 128 : (b + 1) * 128].astype(BF16)
        cols = pl.ds(pl.multiple_of(j * 128, 128), 128)
        g = dot_tn(ctx[:, cols], ga[...]) + dot_tn(ctx_r[:, cols], ga_r[...])
        for b in range(5):
            out[3840 + b * 128 : 3968 + b * 128, :] = g[:, b * 128 : (b + 1) * 128].astype(BF16)


def attend_grad_body(
    where, query, kv, lse, ga_low, wo_m, wo_o, cos, sin, pos_col, pos_row,
    dq_m, dq_o, dkv, dkv_m, dkv_o,
):
    ok = allowed_pairs(pos_col, pos_row)
    ga = ga_low[...]
    grad_k = None
    grad_v = None
    c, s = cos[512:, :], sin[512:, :]
    for half, wo, dq in ((1, wo_o, dq_o), (0, wo_m, dq_m)):
        grad_context = dot_nt(ga, wo[...]).astype(BF16)
        for head in range(2):
            cols = slice(half * MINE + head * HEAD, half * MINE + (head + 1) * HEAD)
            q = query[:, cols]
            gc = grad_context[:, head * HEAD : (head + 1) * HEAD]
            which = half * 2 + head
            scores = jnp.where(ok, dot_nt(q, kv[:, :HEAD]), neg_fill)
            probs = jnp.exp(scores - lse[:, which * 128 : which * 128 + 1])
            part = dot_tn(probs.astype(BF16), gc)
            grad_v = part if grad_v is None else grad_v + part
            grad_probs = dot_nt(gc, kv[:, HEAD:])
            row_dot = jnp.sum(grad_probs * probs, axis=-1, keepdims=True)
            grad_scores = (probs * (grad_probs - row_dot)).astype(BF16)
            gq = dot(grad_scores, kv[:, :HEAD]) * score_scale
            a, b = rotate_pair(gq[:, :HALF], gq[:, HALF:], c, -s)
            dq[:, head * HEAD : head * HEAD + HALF] = a.astype(BF16)
            dq[:, head * HEAD + HALF : (head + 1) * HEAD] = b.astype(BF16)
            part = dot_tn(grad_scores, q)
            grad_k = part if grad_k is None else grad_k + part
    a, b = rotate_pair(grad_k[:, :HALF], grad_k[:, HALF:], cos[...], -sin[...])
    dkv[:, :HALF] = a.astype(BF16)
    dkv[:, HALF:HEAD] = b.astype(BF16)
    dkv[:, HEAD:] = grad_v.astype(BF16)
    even = where[0] == 0
    dkv_m[:, :HALF] = jnp.where(even, a, b).astype(BF16)
    dkv_o[:, :HALF] = jnp.where(even, b, a).astype(BF16)
    va, vb = grad_v[:, :HALF], grad_v[:, HALF:]
    dkv_m[:, HALF:] = jnp.where(even, va, vb).astype(BF16)
    dkv_o[:, HALF:] = jnp.where(even, vb, va).astype(BF16)


def attend_gain_body(
    tok, far_two, far_one, dq_m, dq_o, dkv, wq_m, wq_o, wkv, grad_normed, grad_gain,
):
    gn = dot_nt(dq_m[...], wq_m[...]) + dot_nt(dq_o[...], wq_o[...])
    gn = gn + dot_nt(dkv[512:, :], wkv[...])
    grad_normed[...] = gn
    x = tok[...].astype(F32)
    total = jnp.sum(gn * x * inv_rms(x), axis=0, keepdims=True)
    for i, far in enumerate((far_two, far_one)):
        g = dot_nt(dkv[i * 256 : (i + 1) * 256, :], wkv[...])
        x = far[...].astype(F32)
        total = total + jnp.sum(g * x * inv_rms(x), axis=0, keepdims=True)
    grad_gain[...] = total


def attend_grads_body(
    where, n, n_far, n_r, n_far_r, dq_m, dq_r, dkv_m, dkv_r, gains, *outs
):
    first = where[1]
    gk = dot_tn(n[...], dkv_m[512:, :]) + dot_tn(n_far[...], dkv_m[:512, :])
    gk = gk + dot_tn(n_r[...], dkv_r[512:, :]) + dot_tn(n_far_r[...], dkv_r[:512, :])
    gk = gk.astype(BF16)
    pieces = []
    for at in range(4):
        pieces.append((gk[at * 160 : (at + 1) * 160, :128], gk[at * 160 : (at + 1) * 160, 128:]))
    for out, by in zip(outs, ORDER):
        j = place(first, by)
        cols = pl.ds(pl.multiple_of(j * 128, 128), 128)
        g = dot_tn(n[...], dq_m[:, cols]) + dot_tn(n_r[...], dq_r[:, cols])
        out[:640, :] = g.astype(BF16)
        out[960:, :] = gains[...]
        for at in range(4):

            @pl.when(j == at)
            def _(out=out, at=at):
                out[640:800, :] = pieces[at][0]
                out[800:960, :] = pieces[at][1]


def token_grad_body(tok, gain, grad_after, grad_normed, back_one, back_two, wkv, out):
    back = (back_one[...].astype(F32) + back_two[...].astype(F32)).astype(BF16)
    gn = grad_normed[...] + dot_nt(back, wkv[...])
    x = tok[...].astype(F32)
    r = inv_rms(x)
    dm = gn * gain[...]
    out[...] = grad_after[...] + r * dm - x * (
        r * r * r * jnp.mean(dm * x, axis=-1, keepdims=True)
    )


def split_sum_body(slot, rows, where, own, r_two, r_one, r_minus, *outs):
    second = where[slot]
    for out, by in zip(outs, ORDER):
        j = place(second, by)
        at = pl.ds(pl.multiple_of(j * rows, rows), rows)
        total = (own[at, :].astype(F32) + r_two[at, :].astype(F32)) + (
            r_one[at, :].astype(F32) + r_minus[at, :].astype(F32)
        )
        out[...] = total.astype(BF16)


def sum_body(own, r_two, r_one, r_minus, out):
    total = (own[...].astype(F32) + r_two[...].astype(F32)) + (
        r_one[...].astype(F32) + r_minus[...].astype(F32)
    )
    out[...] = total.astype(BF16)


def join_body(slot, rows, where, own, r_two, r_one, r_minus, out):
    index = where[slot]
    for ref, by in ((own, 0), (r_two, 2), (r_one, 3), (r_minus, 1)):
        j = place(index, by)
        out[pl.ds(pl.multiple_of(j * rows, rows), rows), :] = ref[...]


def summed(name, chunks, where):
    rows = chunks[0].shape[0]
    part = rows // 4
    got = to_peers(chunks[1:], shift_first)
    parts = call(
        name + "_split", functools.partial(split_sum_body, 2, part),
        [((part, 128), BF16)] * 4, [where, chunks[0], *got], scalars=1,
    )
    got = to_peers(parts[1:], shift_second)
    mine = call(name + "_sum2", sum_body, [((part, 128), BF16)], [parts[0], *got])[0]
    got = to_peers([mine] * 3, shift_z)
    mine = call(name + "_sum3", sum_body, [((part, 128), BF16)], [mine, *got])[0]
    got = to_peers([mine] * 3, shift_second)
    whole = call(
        name + "_join", functools.partial(join_body, 2, part),
        [((rows, 128), BF16)], [where, mine, *got], scalars=1,
    )[0]
    return [whole, *to_peers([whole] * 3, shift_first)]


def ffn_spread_body(where, own, r_two, r_one, r_minus, gate, up, down, out):
    first = where[1]
    for ref, by in ((own, 0), (r_two, 2), (r_one, 3), (r_minus, 1)):
        j = place(first, by)
        for at, target in ((0, gate), (1280, up)):
            for b in range(2):
                cols = pl.ds(pl.multiple_of(j * 256 + b * 128, 128), 128)
                target[:, cols] = ref[at + b * 640 : at + (b + 1) * 640, :].astype(F32)
        rows = pl.ds(pl.multiple_of(j * 256, 256), 256)
        for b in range(5):
            down[rows, b * 128 : (b + 1) * 128] = ref[
                2560 + b * 256 : 2816 + b * 256, :
            ].astype(F32)
        rows = pl.ds(pl.multiple_of(j * 128, 128), 128)
        for b in range(5):
            out[rows, b * 128 : (b + 1) * 128] = ref[3840 + b * 128 : 3968 + b * 128, :].astype(F32)


def attend_spread_body(where, own, r_two, r_one, r_minus, query, key, value, gains):
    first = where[1]
    for ref, by in ((own, 0), (r_two, 2), (r_one, 3), (r_minus, 1)):
        j = place(first, by)
        query[:, pl.ds(pl.multiple_of(j * 128, 128), 128)] = ref[:640, :].astype(F32)
        rows = pl.ds(pl.multiple_of(j * 160, 160), 160)
        key[rows, :] = ref[640:800, :].astype(F32)
        value[rows, :] = ref[800:960, :].astype(F32)
    gains[...] = own[960:, :].astype(F32)


def local(
    tokens, positions, gain_attn, w_query, w_key, w_value, w_out, gain_ffn, w_gate, w_up, w_down,
    grad_out,
):
    tok = tokens[0]
    gy = grad_out[0]
    rows = tok.shape[0]
    ctx = lax.axis_index("ctx")
    core = lax.axis_index("fsdp")
    x_at, y_at = ctx // 16, ctx % 4
    where = jnp.stack(
        [core, jnp.where(core == 0, x_at, y_at), jnp.where(core == 0, y_at, x_at)]
    ).astype(jnp.int32)
    even = core == 0

    far_one = passed_along(tok, 1)
    far_two = passed_along(tok, 2)
    query_other = swap(w_query)
    key_other, value_other = swap(w_key), swap(w_value)
    gains = jnp.concatenate([gain_attn, gain_ffn]).reshape(1, D)
    gains_other = swap(gains)
    out_other = swap(w_out)
    gate_other, up_other, down_other = swap(w_gate), swap(w_up), swap(w_down)
    gy_r = swap(gy)

    low = jnp.where(even, gains, gains_other)
    high = jnp.where(even, gains_other, gains)
    half_d = D // 2
    gain_one = jnp.concatenate([low[:, :half_d], high[:, :half_d]], axis=1).astype(F32)
    gain_two = jnp.concatenate([low[:, half_d:], high[:, half_d:]], axis=1).astype(F32)
    wkv = jnp.concatenate(
        [
            jnp.where(even, w_key, key_other),
            jnp.where(even, key_other, w_key),
            jnp.where(even, w_value, value_other),
            jnp.where(even, value_other, w_value),
        ],
        axis=1,
    )

    seq_pos = positions[0]
    key_pos = lax.dynamic_slice_in_dim(
        jnp.concatenate([jnp.full((2 * rows,), -2 * WINDOW, jnp.int32), seq_pos]), ctx * rows,
        3 * rows,
    )
    pos_col = key_pos[2 * rows :].reshape(rows, 1)
    pos_row = key_pos.reshape(1, 3 * rows)
    frequency = rope_base ** (-(jnp.arange(HALF, dtype=F32) * 2.0 / HEAD))
    angles = key_pos.astype(F32)[:, None] * frequency[None, :]
    cos, sin = jnp.cos(angles), jnp.sin(angles)

    normed, query = call(
        "query", query_body, [((rows, D), BF16), ((rows, HEADS * HEAD), BF16)],
        [tok, gain_one, w_query, query_other, cos, sin], flops=2 * rows * D * 1024,
    )
    normed_far, kv, context, lse, after, normed_two = call(
        "attend", attend_body,
        [
            ((2 * rows, D), BF16), ((3 * rows, 2 * HEAD), BF16), ((rows, HEADS * HEAD), BF16),
            ((rows, 512), F32), ((rows, D), F32), ((rows, D), BF16),
        ],
        [
            tok, far_two, far_one, normed, gain_one, query, wkv, w_out, out_other, gain_two, cos,
            sin, pos_col, pos_row,
        ],
        flops=2 * rows * 768 * 256 * 12,
    )
    out, hid_m, hid_o, dg_m, dg_o, du_m, du_o, grad_after, ga_low, grad_gain_two = call(
        "ffn", ffn_body,
        [((rows, D), BF16)]
        + [((rows, FF // 2), BF16)] * 6
        + [((rows, D), F32), ((rows, D), BF16), ((1, D), F32)],
        [after, normed_two, gain_two, w_gate, gate_other, w_up, up_other, w_down, down_other, gy],
        flops=12 * rows * D * FF,
    )
    normed_r, normed_far_r, normed_two_r = swap(normed), swap(normed_far), swap(normed_two)
    ctx_r = swap(context[:, MINE:])
    hid_r, dg_r, du_r, ga_r = swap(hid_o), swap(dg_o), swap(du_o), swap(ga_low)
    chunks = call(
        "ffn_grads", ffn_grads_body, [((F_ROWS, 128), BF16)] * 4,
        [
            where, hid_m, hid_r, dg_m, dg_r, du_m, du_r, normed_two, normed_two_r, gy, gy_r,
            context, ctx_r, ga_low, ga_r,
        ],
        scalars=1, flops=4 * rows * D * 3584,
    )
    ffn_sums = summed("f", chunks, where)

    dq_m, dq_o, dkv, dkv_m, dkv_o = call(
        "attend_grad", attend_grad_body,
        [
            ((rows, MINE), BF16), ((rows, MINE), BF16), ((3 * rows, 2 * HEAD), BF16),
            ((3 * rows, HEAD), BF16), ((3 * rows, HEAD), BF16),
        ],
        [where, query, kv, lse, ga_low, w_out, out_other, cos, sin, pos_col, pos_row],
        scalars=1, flops=2 * rows * 768 * 256 * 22,
    )
    dq_r, dkv_r = swap(dq_o), swap(dkv_o)
    grad_normed, grad_gain_one = call(
        "attend_gain", attend_gain_body, [((rows, D), F32), ((1, D), F32)],
        [tok, far_two, far_one, dq_m, dq_o, dkv, w_query, query_other, wkv],
        flops=2 * rows * D * 2560,
    )
    grad_gains = jnp.concatenate([grad_gain_one, grad_gain_two], axis=1).reshape(4, half_d)
    gains_m = jnp.where(even, grad_gains[0::2], grad_gains[1::2])
    gains_o = jnp.where(even, grad_gains[1::2], grad_gains[0::2])
    gain_sum = gains_m + swap(gains_o)
    gain_rows = jnp.pad(gain_sum.reshape(-1, 128), ((0, 59), (0, 0))).astype(BF16)
    chunks = call(
        "attend_grads", attend_grads_body, [((A_ROWS, 128), BF16)] * 4,
        [where, normed, normed_far, normed_r, normed_far_r, dq_m, dq_r, dkv_m, dkv_r, gain_rows],
        scalars=1, flops=4 * rows * D * 1280,
    )
    attend_sums = summed("a", chunks, where)

    back_one = passed_along(dkv[rows : 2 * rows], -1)
    back_two = passed_along(dkv[:rows], -2)
    grad_tokens = call(
        "token_grad", token_grad_body, [((rows, D), F32)],
        [tok, gain_one, grad_after, grad_normed, back_one, back_two, wkv],
        flops=2 * rows * D * 512,
    )[0]

    g_query, g_key, g_value, g_gains = call(
        "a_spread", attend_spread_body,
        [((D, MINE), F32), ((D, HALF), F32), ((D, HALF), F32), ((64, 128), F32)],
        [where, *attend_sums], scalars=1,
    )
    g_gate, g_up, g_down, g_out = call(
        "f_spread", ffn_spread_body,
        [((D, FF // 2), F32), ((D, FF // 2), F32), ((FF // 2, D), F32), ((MINE, D), F32)],
        [where, *ffn_sums], scalars=1,
    )
    g_gains = g_gains[:5].reshape(2, half_d)
    return (
        out[None], grad_tokens[None], g_gains[0], g_query, g_key, g_value, g_out, g_gains[1],
        g_gate, g_up, g_down,
    )


def solution(mesh):
    tokens = P("fsdp", "ctx", None)
    columns, rows = P(None, "fsdp"), P("fsdp", None)
    in_specs = (
        tokens, P("fsdp", None), P("fsdp"), columns, columns, columns, rows, P("fsdp"), columns,
        columns, rows, tokens,
    )
    out_specs = (
        tokens, tokens, P("fsdp"), columns, columns, columns, rows, P("fsdp"), columns, columns,
        rows,
    )
    return jax.shard_map(local, mesh=mesh, in_specs=in_specs, out_specs=out_specs, check_vma=False)
```

```python
import functools

import jax
import jax.numpy as jnp
from jax import lax
from jax.experimental import pallas as pl
from jax.experimental.pallas import tpu as pltpu
from jax.sharding import PartitionSpec as P

D = 640
HEADS = 4
HEAD = 256
FF = 2048
WINDOW = 512
HALF = HEAD // 2
MINE = 2 * HEAD

epsilon = 1e-06
rope_base = 10000.0
neg_fill = -1e30
score_scale = HEAD ** (-0.5)
gelu_c = 0.7978845608028654
gelu_k = 0.044715

F32 = jnp.float32
BF16 = jnp.bfloat16
MIB = 1024 * 1024


def swap(x):
    return lax.ppermute(x, "fsdp", [(0, 1), (1, 0)])


def chip_pairs(move):
    pairs = []
    for x in range(4):
        for z in range(4):
            for y in range(4):
                for c in range(2):
                    tx, tz, ty = move(x, z, y, c)
                    target = (((tx % 4) * 4 + tz % 4) * 4 + ty % 4) * 2 + c
                    pairs.append((((x * 4 + z) * 4 + y) * 2 + c, target))
    return pairs


def shift_first(by):
    return chip_pairs(lambda x, z, y, c: (x + by, z, y) if c == 0 else (x, z, y + by))


def shift_second(by):
    return chip_pairs(lambda x, z, y, c: (x, z, y + by) if c == 0 else (x + by, z, y))


def shift_z(by):
    return chip_pairs(lambda x, z, y, c: (x, z + by, y))


def after(x, *done):
    return lax.optimization_barrier((x, *done))[0]


def pair_first(z):
    return z ^ 1


def pair_second(z):
    return 3 - z


def swap_z(x, step):
    return lax.ppermute(
        x, ("ctx", "fsdp"),
        chip_pairs(lambda x, z, y, c: (x, (pair_first, pair_second)[c ^ step](z), y)),
    )


def swap_first(v, step):
    pair = (pair_first, pair_second)[step]
    return lax.ppermute(
        v, ("ctx", "fsdp"),
        chip_pairs(lambda x, z, y, c: (pair(x), z, y) if c == 0 else (x, z, pair(y))),
    )


def to_peers(parts, shift):
    return [
        lax.ppermute(part, ("ctx", "fsdp"), shift(by)) for part, by in zip(parts, (2, 1, -1))
    ]


def passed_along(shard, by):
    peers = lax.axis_size("ctx")
    pairs = [(i, i + by) for i in range(peers) if 0 <= i + by < peers]
    return lax.ppermute(shard, "ctx", pairs)


def dot(a, b):
    return lax.dot_general(a, b, (((1,), (0,)), ((), ())), preferred_element_type=F32)


def dot_nt(a, b):
    return lax.dot_general(a, b, (((1,), (1,)), ((), ())), preferred_element_type=F32)


def dot_tn(a, b):
    return lax.dot_general(a, b, (((0,), (0,)), ((), ())), preferred_element_type=F32)


def call(name, body, outs, ins, us, scalars=0, scratch=(), extra=8):
    smem = pl.BlockSpec(memory_space=pltpu.SMEM)
    whole = pl.BlockSpec(memory_space=pltpu.VMEM)
    shapes = [jax.ShapeDtypeStruct(s, t) for s, t in outs]
    held = sum(x.size * x.dtype.itemsize for x in [*ins, *shapes])
    return pl.pallas_call(
        body,
        out_shape=shapes,
        in_specs=[smem] * scalars
        + [whole] * (len(ins) - scalars),
        out_specs=[whole] * len(outs),
        scratch_shapes=scratch,
        compiler_params=pltpu.CompilerParams(vmem_limit_bytes=held + extra * MIB),
        cost_estimate=pl.CostEstimate(
            flops=int(us * 1.1e9), bytes_accessed=1024, transcendentals=0
        ),
        name=name,
    )(*ins)


def inv_rms(x):
    return lax.rsqrt(jnp.mean(x * x, axis=-1, keepdims=True) + epsilon)


def rotate_pair(a, b, c, s):
    return a * c - b * s, b * c + a * s


def allowed_pairs(pos_row):
    keys = pos_row[...].astype(F32)
    own = jnp.broadcast_to(keys[:, 512:], (128, 256)).T[:, :1]
    distance = own - keys
    return (distance >= 0) & (distance < WINDOW)


def query_body(
    where, tok, gain, wq_m, wq_o, wk_m, wk_o, wv_m, wv_o, wo, cos, sin,
    normed, query, wkv, wide, wo_near,
):
    x = tok[...].astype(F32)
    wide[...] = x
    wo_near[...] = wo[...]
    n = (x * inv_rms(x) * gain[...]).astype(BF16)
    normed[...] = n
    c, s = cos[512:, :], sin[512:, :]
    for half, w in enumerate((wq_m, wq_o)):
        raw = dot(n, w[...])
        for head in range(2):
            a = raw[:, head * HEAD : head * HEAD + HALF]
            b = raw[:, head * HEAD + HALF : (head + 1) * HEAD]
            ra, rb = rotate_pair(a, b, c, s)
            at = half * MINE + head * HEAD
            query[:, at : at + HALF] = (ra * score_scale).astype(BF16)
            query[:, at + HALF : at + HEAD] = (rb * score_scale).astype(BF16)
    for which, (a, b, c, d) in enumerate(((wk_m, wk_o, wv_m, wv_o), (wk_o, wk_m, wv_o, wv_m))):

        @pl.when(where[0] == which)
        def _(parts=(a, b, c, d)):
            for i, part in enumerate(parts):
                wkv[:, i * HALF : (i + 1) * HALF] = part[...]


def attend_body(
    far_two, far_one, normed, wide, query, wkv, gain, wo_m, wo_o, gain_two, cos, sin, pos_row,
    normed_all, query_kept, kv, ctx_m, ctx_o, lse, after, normed_two,
):
    query_kept[...] = query[...]
    normed_all[512:, :] = normed[...]
    for i, far in enumerate((far_two, far_one)):
        x = far[...].astype(F32)
        normed_all[i * 256 : (i + 1) * 256, :] = (x * inv_rms(x) * gain[...]).astype(BF16)
    raw = dot(normed_all[...], wkv[...])
    ka, kb = rotate_pair(raw[:, :HALF], raw[:, HALF:HEAD], cos[...], sin[...])
    kv[:, :HALF] = ka.astype(BF16)
    kv[:, HALF:HEAD] = kb.astype(BF16)
    kv[:, HEAD:] = raw[:, HEAD:].astype(BF16)
    ok = allowed_pairs(pos_row)
    for head in range(HEADS):
        cols = slice(head * HEAD, (head + 1) * HEAD)
        scores = jnp.where(ok, dot_nt(query[:, cols], kv[:, :HEAD]), neg_fill)
        top = jnp.max(scores, axis=-1, keepdims=True)
        exps = jnp.exp(scores - top)
        total = jnp.sum(exps, axis=-1, keepdims=True)
        lse[:, head * 128 : (head + 1) * 128] = jnp.broadcast_to(top + jnp.log(total), (256, 128))
        probs = (exps * (1.0 / total)).astype(BF16)
        context = (ctx_m, ctx_o)[head // 2]
        at = head % 2 * HEAD
        context[:, at : at + HEAD] = dot(probs, kv[:, HEAD:]).astype(BF16)
    h = wide[...] + (dot(ctx_m[...], wo_m[...]) + dot(ctx_o[...], wo_o[...]))
    after[...] = h
    normed_two[...] = (h * inv_rms(h) * gain_two[...]).astype(BF16)


FFN_STEP = 512


def ffn_half(n, y, wg, wu, wd, hid, dg, du):
    total = None
    grad_n = None
    for at in range(0, FF // 2, FFN_STEP):
        cols = slice(at, at + FFN_STEP)
        gate = dot(n, wg[:, cols])
        up = dot(n, wu[:, cols])
        grad_hidden = dot_nt(y, wd[cols, :])
        square = gate * gate
        t = jnp.tanh(gelu_c * gate * (1.0 + gelu_k * square))
        one_t = 0.5 + 0.5 * t
        act = gate * one_t
        slope = one_t + 0.5 * gate * (1.0 - t * t) * (gelu_c * (1.0 + 3.0 * gelu_k * square))
        hidden = (act * up).astype(BF16)
        grad_gate = (grad_hidden * up * slope).astype(BF16)
        grad_up = (grad_hidden * act).astype(BF16)
        hid[:, cols] = hidden
        dg[:, cols] = grad_gate
        du[:, cols] = grad_up
        part = dot(hidden, wd[cols, :])
        total = part if total is None else total + part
        part = dot_nt(grad_gate, wg[:, cols]) + dot_nt(grad_up, wu[:, cols])
        grad_n = part if grad_n is None else grad_n + part
    return total, grad_n


def ffn_other_body(normed_two, gy, wg, wu, wd, hid, dg, du, total, grad_n):
    total[...], grad_n[...] = ffn_half(normed_two[...], gy[...], wg, wu, wd, hid, dg, du)


def ffn_body(
    after, normed_two, gain_two, gy, wg, wu, wd, total_o, grad_n_o,
    out, hid, dg, du, grad_after, grad_after_low, grad_gain,
):
    y = gy[...]
    total, grad_n = ffn_half(normed_two[...], y, wg, wu, wd, hid, dg, du)
    grad_n = grad_n + grad_n_o[...]
    h = after[...]
    out[...] = (h + (total + total_o[...])).astype(BF16)
    r = inv_rms(h)
    dn = grad_n * gain_two[...]
    grad_gain[...] = jnp.sum(grad_n * h * r, axis=0, keepdims=True)
    ga = y.astype(F32) + r * dn - h * (r * r * r * jnp.mean(dn * h, axis=-1, keepdims=True))
    grad_after[...] = ga
    grad_after_low[...] = ga.astype(BF16)


ORDER = (0, 2, 1, 3)
F_ROWS = 3840
A_ROWS = 1664


def place(i, by):
    return lax.rem(i + by, 4)


def z_places(core, z):
    one = z + 1 - 2 * lax.rem(z, 2)
    other = 3 - z
    first = jnp.where(core == 0, one, other)
    second = jnp.where(core == 0, other, one)
    return z, second, first, 2 - z + 2 * lax.rem(z, 2)


def ffn_grads_body(
    where, hid_m, hid_r, dg_m, dg_r, du_m, du_r, n, n_r, gy, gy_r, out_0, out_1, out_2, out_3, turned
):
    first = where[1]
    turned[:, :256] = n[...].T
    turned[:, 256:] = n_r[...].T
    for out, by in zip((out_0, out_1, out_2, out_3), ORDER):
        j = place(first, by)
        cols = pl.ds(pl.multiple_of(j * 256, 256), 256)
        for at, left, right in ((0, dg_m, dg_r), (1280, du_m, du_r)):
            g = dot(turned[:, :256], left[:, cols]) + dot(turned[:, 256:], right[:, cols])
            out[at : at + 640, :] = g[:, :128].astype(BF16)
            out[at + 640 : at + 1280, :] = g[:, 128:].astype(BF16)
        g = dot_tn(hid_m[:, cols], gy[...]) + dot_tn(hid_r[:, cols], gy_r[...])
        for b in range(5):
            out[2560 + b * 256 : 2816 + b * 256, :] = g[:, b * 128 : (b + 1) * 128].astype(BF16)


def attend_grad_body(
    where, query, kv, lse, ga_low, wo_m, wo_o, cos, sin, pos_row,
    dq_m, dq_o, dkv, dkv_m, packed,
):
    dkv_o = packed.at[512:, :]
    ok = allowed_pairs(pos_row)
    ga = ga_low[...]
    grad_k = None
    grad_v = None
    c, s = cos[512:, :], sin[512:, :]
    for half, wo, dq in ((1, wo_o, dq_o), (0, wo_m, dq_m)):
        grad_context = dot_nt(ga, wo[...]).astype(BF16)
        for head in range(2):
            cols = slice(half * MINE + head * HEAD, half * MINE + (head + 1) * HEAD)
            q = query[:, cols]
            gc = grad_context[:, head * HEAD : (head + 1) * HEAD]
            which = half * 2 + head
            scores = jnp.where(ok, dot_nt(q, kv[:, :HEAD]), neg_fill)
            probs = jnp.exp(scores - lse[:, which * 128 : which * 128 + 1])
            part = dot_tn(probs.astype(BF16), gc)
            grad_v = part if grad_v is None else grad_v + part
            grad_probs = dot_nt(gc, kv[:, HEAD:])
            row_dot = jnp.sum(grad_probs * probs, axis=-1, keepdims=True)
            grad_scores = (probs * (grad_probs - row_dot)).astype(BF16)
            gq = dot(grad_scores, kv[:, :HEAD]) * score_scale
            a, b = rotate_pair(gq[:, :HALF], gq[:, HALF:], c, -s)
            dq[:, head * HEAD : head * HEAD + HALF] = a.astype(BF16)
            dq[:, head * HEAD + HALF : (head + 1) * HEAD] = b.astype(BF16)
            part = dot_tn(grad_scores, q)
            grad_k = part if grad_k is None else grad_k + part
    a, b = rotate_pair(grad_k[:, :HALF], grad_k[:, HALF:], cos[...], -sin[...])
    packed[:256, :] = dq_o[:, :HEAD]
    packed[256:512, :] = dq_o[:, HEAD:]
    dkv[:, :HALF] = a.astype(BF16)
    dkv[:, HALF:HEAD] = b.astype(BF16)
    dkv[:, HEAD:] = grad_v.astype(BF16)
    even = where[0] == 0
    dkv_m[:, :HALF] = jnp.where(even, a, b).astype(BF16)
    dkv_o[:, :HALF] = jnp.where(even, b, a).astype(BF16)
    va, vb = grad_v[:, :HALF], grad_v[:, HALF:]
    dkv_m[:, HALF:] = jnp.where(even, va, vb).astype(BF16)
    dkv_o[:, HALF:] = jnp.where(even, vb, va).astype(BF16)


def attend_grads_body(
    where, n, n_r, dq_m, dkv_m, packed, ctx, ctx_r, ga, ga_r, wq, wk, wv,
    gain, gain_two_grad, out_0, out_1, out_2, out_3, turned,
):
    turned[:, :768] = n[...].T
    turned[:, 768:] = n_r[...].T
    gk = dot(turned[:, :768], dkv_m[...]) + dot(turned[:, 768:], packed[512:, :])
    weighed = gk[:, :HALF] * wk[...].astype(F32) + gk[:, HALF:] * wv[...].astype(F32)
    gk = gk.astype(BF16)
    for out, j in zip((out_0, out_1, out_2, out_3), z_places(where[0], where[3])):
        cols = pl.ds(pl.multiple_of(j * 128, 128), 128)
        rows = pl.ds(pl.multiple_of(j // 2 * 256, 256), 256)
        half = pl.ds(pl.multiple_of(j % 2 * 128, 128), 128)
        g = dot(turned[:, 512:768], dq_m[:, cols]) + dot(turned[:, 1280:], packed[rows, half])
        weighed = weighed + g * wq[:, cols].astype(F32)
        out[:640, :] = g.astype(BF16)
        g = dot_tn(ctx[:, cols], ga[...]) + dot_tn(ctx_r[:, cols], ga_r[...])
        for b in range(5):
            out[960 + b * 128 : 1088 + b * 128, :] = g[:, b * 128 : (b + 1) * 128].astype(BF16)
        for at in range(4):

            @pl.when(j == at)
            def _(out=out, at=at):
                out[640:800, :] = gk[at * 160 : (at + 1) * 160, :HALF]
                out[800:960, :] = gk[at * 160 : (at + 1) * 160, HALF:]

    by_row = jnp.broadcast_to(jnp.sum(weighed, axis=1, keepdims=True), (640, 128))
    one = by_row.T[:1, :] / gain[...]
    two = gain_two_grad[...]
    rows = [v[:, b * 128 : (b + 1) * 128] for v in (one, two) for b in range(5)]
    block = jnp.concatenate([*rows, jnp.zeros((6, 128), F32)], axis=0).astype(BF16)
    for out in (out_0, out_1, out_2, out_3):
        out[1600:1616, :] = block
        out[1616:, :] = jnp.zeros((48, 128), BF16)


def token_grad_body(
    tok, gain, grad_after, dq_m, dq_o, dkv, back_one, back_two, wq_m, wq_o, wkv, out
):
    back = back_one[...].astype(F32) + back_two[...].astype(F32)
    own = (dkv[512:, :].astype(F32) + back).astype(BF16)
    gn = dot_nt(dq_m[...], wq_m[...]) + dot_nt(dq_o[...], wq_o[...]) + dot_nt(own, wkv[...])
    x = tok[...].astype(F32)
    r = inv_rms(x)
    dm = gn * gain[...]
    out[...] = grad_after[...] + r * dm - x * (
        r * r * r * jnp.mean(dm * x, axis=-1, keepdims=True)
    )


def add_low(*terms):
    total = terms[0].astype(F32)
    for term in terms[1:]:
        total = total + term.astype(F32)
    return total.astype(BF16)


F_PART, A_PART = F_ROWS // 4, A_ROWS // 4
PART = F_PART + A_PART


def split_sum_body(
    where, own, r_two, r_one, r_minus, a_own, a_one, a_last, out_0, out_1, out_2, out_3
):
    for out, by in zip((out_0, out_1, out_2, out_3), ORDER):
        j = place(where[2], by)
        at = pl.ds(pl.multiple_of(j * F_PART, F_PART), F_PART)
        total = (own[at, :].astype(F32) + r_two[at, :].astype(F32)) + (
            r_one[at, :].astype(F32) + r_minus[at, :].astype(F32)
        )
        out[:F_PART, :] = total.astype(BF16)
        at = pl.ds(pl.multiple_of(j * A_PART, A_PART), A_PART)
        total = a_own[at, :].astype(F32) + a_one[at, :].astype(F32) + a_last[at, :].astype(F32)
        out[F_PART:, :] = total.astype(BF16)


def sum_four(own, r_two, r_one, r_minus):
    total = (own.astype(F32) + r_two.astype(F32)) + (r_one.astype(F32) + r_minus.astype(F32))
    return total.astype(BF16)


def join_body(where, own, r_two, r_one, r_minus, f_out, a_out):
    for ref, by in ((own, 0), (r_two, 2), (r_one, 3), (r_minus, 1)):
        j = place(where[2], by)
        f_out[pl.ds(pl.multiple_of(j * F_PART, F_PART), F_PART), :] = ref[:F_PART, :]
        a_out[pl.ds(pl.multiple_of(j * A_PART, A_PART), A_PART), :] = ref[F_PART:, :]


def ffn_spread_body(by, fresh, where, piece, *refs):
    gate, up, down, gate_wide, up_wide, down_wide, sems = refs if fresh else refs[3:]
    j = place(where[1], by)
    copies = []
    cols = pl.ds(pl.multiple_of(j * 256, 256), 256)
    for i, (at, wide, target) in enumerate(((0, gate_wide, gate), (1280, up_wide, up))):
        for b in range(2):
            wide[:, b * 128 : (b + 1) * 128] = piece[
                at + b * 640 : at + (b + 1) * 640, :
            ].astype(F32)
        copies.append(pltpu.make_async_copy(wide, target.at[:, cols], sems.at[i]))
        copies[-1].start()
    for b in range(5):
        down_wide[:, b * 128 : (b + 1) * 128] = piece[2560 + b * 256 : 2816 + b * 256, :].astype(F32)
    copies.append(pltpu.make_async_copy(down_wide, down.at[cols, :], sems.at[2]))
    copies[-1].start()
    for copy in copies:
        copy.wait()


def ffn_spread(where, pieces):
    outs = [jax.ShapeDtypeStruct(s, F32) for s in ((D, FF // 2), (D, FF // 2), (FF // 2, D))]
    anywhere = pl.BlockSpec(memory_space=pl.ANY)
    shards = []
    for piece, by in zip(pieces, (0, 2, 3, 1)):
        shards = pl.pallas_call(
            functools.partial(ffn_spread_body, by, not shards),
            out_shape=outs,
            in_specs=[
                pl.BlockSpec(memory_space=pltpu.SMEM), pl.BlockSpec(memory_space=pltpu.VMEM),
                *[anywhere] * len(shards),
            ],
            out_specs=[anywhere] * 3,
            input_output_aliases={2 + i: i for i in range(len(shards))},
            scratch_shapes=[
                pltpu.VMEM((D, 256), F32), pltpu.VMEM((D, 256), F32), pltpu.VMEM((256, D), F32),
                pltpu.SemaphoreType.DMA((3,)),
            ],
            compiler_params=pltpu.CompilerParams(vmem_limit_bytes=8 * MIB),
            cost_estimate=pl.CostEstimate(flops=1024, bytes_accessed=1024, transcendentals=0),
            name="f_spread",
        )(where, piece, *shards)
    return shards


def attend_spread_body(where, own, r_two, r_one, r_minus, query, key, value, out, gains):
    for ref, by in ((own, 0), (r_two, 2), (r_one, 3), (r_minus, 1)):
        j = place(where[3], by)
        query[:, pl.ds(pl.multiple_of(j * 128, 128), 128)] = ref[:640, :].astype(F32)
        rows = pl.ds(pl.multiple_of(j * 160, 160), 160)
        key[rows, :] = ref[640:800, :].astype(F32)
        value[rows, :] = ref[800:960, :].astype(F32)
        rows = pl.ds(pl.multiple_of(j * 128, 128), 128)
        for b in range(5):
            out[rows, b * 128 : (b + 1) * 128] = ref[960 + b * 128 : 1088 + b * 128, :].astype(F32)
    gains[...] = own[1600:1616, :].astype(F32)


def local(
    tokens, positions, gain_attn, w_query, w_key, w_value, w_out, gain_ffn, w_gate, w_up, w_down,
    grad_out,
):
    tok = tokens[0]
    gy = grad_out[0]
    rows = tok.shape[0]
    ctx = lax.axis_index("ctx")
    core = lax.axis_index("fsdp")
    x_at, y_at = ctx // 16, ctx % 4
    where = jnp.stack(
        [core, jnp.where(core == 0, x_at, y_at), jnp.where(core == 0, y_at, x_at), ctx // 4 % 4]
    ).astype(jnp.int32)
    even = core == 0

    far_one = passed_along(tok, 1)
    far_two = passed_along(tok, 2)
    gains = jnp.concatenate([gain_attn, gain_ffn]).reshape(1, D)
    gains_other = swap(gains)
    key_other, value_other = swap(w_key), swap(w_value)
    query_other = swap(after(w_query, gains_other))
    out_other = swap(after(w_out, key_other))

    low = jnp.where(even, gains, gains_other)
    high = jnp.where(even, gains_other, gains)
    half_d = D // 2
    gain_one = jnp.concatenate([low[:, :half_d], high[:, :half_d]], axis=1).astype(F32)
    gain_two = jnp.concatenate([low[:, half_d:], high[:, half_d:]], axis=1).astype(F32)
    seq_pos = positions[0]
    key_pos = lax.dynamic_slice_in_dim(
        jnp.concatenate([jnp.full((2 * rows,), -2 * WINDOW, jnp.int32), seq_pos]), ctx * rows,
        3 * rows,
    )
    pos_row = key_pos.reshape(1, 3 * rows)
    frequency = rope_base ** (-(jnp.arange(HALF, dtype=F32) * 2.0 / HEAD))
    angles = key_pos.astype(F32)[:, None] * frequency[None, :]
    cos, sin = jnp.cos(angles), jnp.sin(angles)

    gy_r = swap(after(gy, value_other))
    normed, query, wkv, wide, wo_near = call(
        "query", query_body,
        [
            ((rows, D), BF16), ((rows, HEADS * HEAD), BF16), ((D, 2 * HEAD), BF16),
            ((rows, D), F32), ((MINE, D), BF16),
        ],
        [
            where, after(tok, gain_two, pos_row), gain_one, w_query, query_other, w_key,
            key_other, w_value, value_other, w_out, cos, sin,
        ],
        us=6, scalars=1,
    )
    first = (normed, far_one, far_two, out_other, gy_r)
    gate_other = swap(after(w_gate, *first))
    up_other = swap(after(w_up, *first))
    down_other = swap(after(w_down, *first))
    normed_all, query, kv, ctx_m, ctx_o, lse, after_attn, normed_two = call(
        "attend", attend_body,
        [
            ((3 * rows, D), BF16), ((rows, HEADS * HEAD), BF16), ((3 * rows, 2 * HEAD), BF16),
            ((rows, MINE), BF16), ((rows, MINE), BF16), ((rows, 512), F32), ((rows, D), F32),
            ((rows, D), BF16),
        ],
        [
            far_two, far_one, normed, wide, query, wkv, gain_one, wo_near, out_other, gain_two,
            cos, sin, pos_row,
        ],
        us=5,
    )
    normed_two_r = swap(normed_two)
    ctx_r, normed_r = swap(ctx_o), swap(normed_all)
    half_ffn = [((rows, FF // 2), BF16)] * 3
    hid_o, dg_o, du_o, total_o, grad_n_o = call(
        "ffn_other", ffn_other_body, [*half_ffn, ((rows, D), F32), ((rows, D), F32)],
        [normed_two, gy, gate_other, up_other, down_other],
        us=5,
    )
    gain_two = after(gain_two, normed_two_r, ctx_r, normed_r)
    hid_r, dg_r, du_r = swap(hid_o), swap(dg_o), swap(du_o)
    out, hid_m, dg_m, du_m, grad_after, ga_low, grad_gain_two = call(
        "ffn", ffn_body,
        [((rows, D), BF16), *half_ffn, ((rows, D), F32), ((rows, D), BF16), ((1, D), F32)],
        [after_attn, normed_two, gain_two, gy, w_gate, w_up, w_down, total_o, grad_n_o],
        us=4,
    )
    ga_r = swap(ga_low)
    dq_m, dq_o, dkv, dkv_m, packed = call(
        "attend_grad", attend_grad_body,
        [
            ((rows, MINE), BF16), ((rows, MINE), BF16), ((3 * rows, 2 * HEAD), BF16),
            ((3 * rows, HEAD), BF16), ((5 * rows, HEAD), BF16),
        ],
        [
            where, query, kv, lse, ga_low, w_out, out_other, cos, sin, pos_row,
        ],
        us=0, scalars=1,
    )
    packed_r = swap(packed)
    f_chunks = call(
        "ffn_grads", ffn_grads_body, [((F_ROWS, 128), BF16)] * 4,
        [where, after(hid_m, packed), hid_r, dg_m, dg_r, du_m, du_r, normed_two, normed_two_r, gy, gy_r],
        scalars=1, scratch=[pltpu.VMEM((D, 512), BF16)],
        us=3,
    )
    f_got = to_peers(f_chunks[1:], shift_first)

    a_chunks = call(
        "attend_grads", attend_grads_body, [((A_ROWS, 128), BF16)] * 4,
        [
            where, normed_all, normed_r, after(dq_m, f_chunks[0]), dkv_m, packed_r, ctx_m, ctx_r, ga_low, ga_r,
            w_query, w_key, w_value, gain_one, grad_gain_two,
        ],
        us=0, scalars=1, scratch=[pltpu.VMEM((D, 6 * rows), BF16)],
    )
    a_own, a_next, a_far_own, a_far_next = a_chunks
    a_next_r, a_own_r = swap_z(a_far_next, 0), swap_z(a_far_own, 0)
    a_last_r = swap_z(add_low(a_next, a_next_r), 1)
    parts = call(
        "split", split_sum_body, [((PART, 128), BF16)] * 4,
        [where, after(f_chunks[0], a_own), *f_got, a_own, a_own_r, a_last_r], us=0, scalars=1,
    )
    got = [parts[0], *to_peers(parts[1:], shift_second)]
    f_two = sum_four(*[part[:F_PART] for part in got])
    a_two = sum_four(*[part[F_PART:] for part in got])
    f_pair = add_low(f_two, swap_z(f_two, 0))
    a_pair = add_low(a_two, swap_first(a_two, 0))
    f_three = add_low(f_pair, swap_z(f_pair, 1))
    a_three = add_low(a_pair, swap_first(a_pair, 1))
    back_two = passed_along(after(dkv[:rows], f_two), -2)
    back_one = passed_along(after(dkv[rows : 2 * rows], f_two), -1)
    own = after(jnp.concatenate([f_three, a_three]), back_one, back_two)
    f_whole, a_whole = call(
        "join", join_body, [((F_ROWS, 128), BF16), ((A_ROWS, 128), BF16)],
        [where, own, *to_peers([own] * 3, shift_second)], us=0, scalars=1,
    )
    f_sums = [f_whole, *to_peers([f_whole] * 3, shift_first)]
    a_sums = [a_whole, *to_peers([a_whole] * 3, shift_z)]
    grad_tokens = call(
        "token_grad", token_grad_body, [((rows, D), F32)],
        [
            tok, gain_one, grad_after, dq_m, dq_o, dkv, back_one, back_two, w_query, query_other,
            wkv,
        ],
        us=2,
    )[0]

    g_query, g_key, g_value, g_out, g_gains = call(
        "a_spread", attend_spread_body,
        [((D, MINE), F32), ((D, HALF), F32), ((D, HALF), F32), ((MINE, D), F32), ((16, 128), F32)],
        [where, *a_sums], scalars=1,
        us=2.5,
    )
    g_gate, g_up, g_down = ffn_spread(where, f_sums)
    g_gains = (g_gains + swap(g_gains))[:10].reshape(2, D)
    g_gains = jnp.where(even, g_gains[:, :half_d], g_gains[:, half_d:])
    return (
        out[None], grad_tokens[None], g_gains[0], g_query, g_key, g_value, g_out, g_gains[1],
        g_gate, g_up, g_down,
    )


def solution(mesh):
    tokens = P("fsdp", "ctx", None)
    columns, rows = P(None, "fsdp"), P("fsdp", None)
    in_specs = (
        tokens, P("fsdp", None), P("fsdp"), columns, columns, columns, rows, P("fsdp"), columns,
        columns, rows, tokens,
    )
    out_specs = (
        tokens, tokens, P("fsdp"), columns, columns, columns, rows, P("fsdp"), columns, columns,
        rows,
    )
    return jax.shard_map(local, mesh=mesh, in_specs=in_specs, out_specs=out_specs, check_vma=False)
```

```python
import functools

import jax
import jax.numpy as jnp
from jax import lax
from jax.experimental import pallas as pl
from jax.experimental.pallas import tpu as pltpu
from jax.sharding import PartitionSpec as P

D = 640
HEADS = 4
HEAD = 256
FF = 2048
WINDOW = 512
HALF = HEAD // 2
MINE = 2 * HEAD

epsilon = 1e-06
rope_base = 10000.0
neg_fill = -1e30
score_scale = HEAD ** (-0.5)
gelu_c = 0.7978845608028654
gelu_k = 0.044715

F32 = jnp.float32
BF16 = jnp.bfloat16
MIB = 1024 * 1024


def swap(x):
    return lax.ppermute(x, "fsdp", [(0, 1), (1, 0)])


def chip_pairs(move):
    pairs = []
    for x in range(4):
        for z in range(4):
            for y in range(4):
                for c in range(2):
                    tx, tz, ty = move(x, z, y, c)
                    target = (((tx % 4) * 4 + tz % 4) * 4 + ty % 4) * 2 + c
                    pairs.append((((x * 4 + z) * 4 + y) * 2 + c, target))
    return pairs


def shift_first(by):
    return chip_pairs(lambda x, z, y, c: (x + by, z, y) if c == 0 else (x, z + by, y))


def shift_second(by):
    return chip_pairs(lambda x, z, y, c: (x, z + by, y) if c == 0 else (x + by, z, y))


def shift_y(by):
    return chip_pairs(lambda x, z, y, c: (x, z, y + by))


def shift_apart(by):
    return chip_pairs(lambda x, z, y, c: (x, z, y + by - 2 * by * c))


def after(x, *done):
    return lax.optimization_barrier((x, *done))[0]


def pair_first(v):
    return v ^ 1


def pair_second(v):
    return 3 - v


def swap_y(v, step):
    return lax.ppermute(
        v, ("ctx", "fsdp"),
        chip_pairs(lambda x, z, y, c: (x, z, (pair_first, pair_second)[c ^ step](y))),
    )


def swap_first(v, step):
    pair = (pair_first, pair_second)[step]
    return lax.ppermute(
        v, ("ctx", "fsdp"),
        chip_pairs(lambda x, z, y, c: (pair(x), z, y) if c == 0 else (x, pair(z), y)),
    )


def to_peers(parts, shift):
    return [
        lax.ppermute(part, ("ctx", "fsdp"), shift(by)) for part, by in zip(parts, (2, 1, -1))
    ]


def passed_along(shard, by):
    peers = lax.axis_size("ctx")
    pairs = [(i, i + by) for i in range(peers) if 0 <= i + by < peers]
    return lax.ppermute(shard, "ctx", pairs)


def dot(a, b):
    return lax.dot_general(a, b, (((1,), (0,)), ((), ())), preferred_element_type=F32)


def dot_nt(a, b):
    return lax.dot_general(a, b, (((1,), (1,)), ((), ())), preferred_element_type=F32)


def dot_tn(a, b):
    return lax.dot_general(a, b, (((0,), (0,)), ((), ())), preferred_element_type=F32)


def call(name, body, outs, ins, us, scalars=0, scratch=(), extra=8):
    smem = pl.BlockSpec(memory_space=pltpu.SMEM)
    whole = pl.BlockSpec(memory_space=pltpu.VMEM)
    shapes = [jax.ShapeDtypeStruct(s, t) for s, t in outs]
    held = sum(x.size * x.dtype.itemsize for x in [*ins, *shapes])
    return pl.pallas_call(
        body,
        out_shape=shapes,
        in_specs=[smem] * scalars
        + [whole] * (len(ins) - scalars),
        out_specs=[whole] * len(outs),
        scratch_shapes=scratch,
        compiler_params=pltpu.CompilerParams(vmem_limit_bytes=held + extra * MIB),
        cost_estimate=pl.CostEstimate(
            flops=int(us * 1.1e9), bytes_accessed=1024, transcendentals=0
        ),
        name=name,
    )(*ins)


def inv_rms(x):
    return lax.rsqrt(jnp.mean(x * x, axis=-1, keepdims=True) + epsilon)


def rotate_pair(a, b, c, s):
    return a * c - b * s, b * c + a * s


def allowed_pairs(pos_row):
    keys = pos_row[...].astype(F32)
    own = jnp.broadcast_to(keys[:, 512:], (128, 256)).T[:, :1]
    distance = own - keys
    return (distance >= 0) & (distance < WINDOW)


def query_body(
    where, tok, gain, wq_m, wq_o, wk_m, wk_o, wv_m, wv_o, wo, cos, sin,
    normed, query, wkv, wide, wo_near,
):
    x = tok[...].astype(F32)
    wide[...] = x
    wo_near[...] = wo[...]
    n = (x * inv_rms(x) * gain[...]).astype(BF16)
    normed[...] = n
    c, s = cos[512:, :], sin[512:, :]
    for half, w in enumerate((wq_m, wq_o)):
        raw = dot(n, w[...])
        for head in range(2):
            a = raw[:, head * HEAD : head * HEAD + HALF]
            b = raw[:, head * HEAD + HALF : (head + 1) * HEAD]
            ra, rb = rotate_pair(a, b, c, s)
            at = half * MINE + head * HEAD
            query[:, at : at + HALF] = (ra * score_scale).astype(BF16)
            query[:, at + HALF : at + HEAD] = (rb * score_scale).astype(BF16)
    for which, (a, b, c, d) in enumerate(((wk_m, wk_o, wv_m, wv_o), (wk_o, wk_m, wv_o, wv_m))):

        @pl.when(where[0] == which)
        def _(parts=(a, b, c, d)):
            for i, part in enumerate(parts):
                wkv[:, i * HALF : (i + 1) * HALF] = part[...]


def attend_body(
    far_two, far_one, normed, wide, query, wkv, gain, wo_m, wo_o, gain_two, cos, sin, pos_row,
    normed_all, query_kept, kv, ctx_m, ctx_o, lse, after, normed_two,
):
    query_kept[...] = query[...]
    normed_all[512:, :] = normed[...]
    for i, far in enumerate((far_two, far_one)):
        x = far[...].astype(F32)
        normed_all[i * 256 : (i + 1) * 256, :] = (x * inv_rms(x) * gain[...]).astype(BF16)
    raw = dot(normed_all[...], wkv[...])
    ka, kb = rotate_pair(raw[:, :HALF], raw[:, HALF:HEAD], cos[...], sin[...])
    kv[:, :HALF] = ka.astype(BF16)
    kv[:, HALF:HEAD] = kb.astype(BF16)
    kv[:, HEAD:] = raw[:, HEAD:].astype(BF16)
    ok = allowed_pairs(pos_row)
    for head in range(HEADS):
        cols = slice(head * HEAD, (head + 1) * HEAD)
        scores = jnp.where(ok, dot_nt(query[:, cols], kv[:, :HEAD]), neg_fill)
        top = jnp.max(scores, axis=-1, keepdims=True)
        exps = jnp.exp(scores - top)
        total = jnp.sum(exps, axis=-1, keepdims=True)
        lse[:, head * 128 : (head + 1) * 128] = jnp.broadcast_to(top + jnp.log(total), (256, 128))
        probs = (exps * (1.0 / total)).astype(BF16)
        context = (ctx_m, ctx_o)[head // 2]
        at = head % 2 * HEAD
        context[:, at : at + HEAD] = dot(probs, kv[:, HEAD:]).astype(BF16)
    h = wide[...] + (dot(ctx_m[...], wo_m[...]) + dot(ctx_o[...], wo_o[...]))
    after[...] = h
    normed_two[...] = (h * inv_rms(h) * gain_two[...]).astype(BF16)


FFN_STEP = 512


def ffn_half(n, y, wg, wu, wd, hid, dg, du):
    total = None
    grad_n = None
    for at in range(0, FF // 2, FFN_STEP):
        cols = slice(at, at + FFN_STEP)
        gate = dot(n, wg[:, cols])
        up = dot(n, wu[:, cols])
        grad_hidden = dot_nt(y, wd[cols, :])
        square = gate * gate
        t = jnp.tanh(gelu_c * gate * (1.0 + gelu_k * square))
        one_t = 0.5 + 0.5 * t
        act = gate * one_t
        slope = one_t + 0.5 * gate * (1.0 - t * t) * (gelu_c * (1.0 + 3.0 * gelu_k * square))
        hidden = (act * up).astype(BF16)
        grad_gate = (grad_hidden * up * slope).astype(BF16)
        grad_up = (grad_hidden * act).astype(BF16)
        hid[:, cols] = hidden
        dg[:, cols] = grad_gate
        du[:, cols] = grad_up
        part = dot(hidden, wd[cols, :])
        total = part if total is None else total + part
        part = dot_nt(grad_gate, wg[:, cols]) + dot_nt(grad_up, wu[:, cols])
        grad_n = part if grad_n is None else grad_n + part
    return total, grad_n


def ffn_other_body(normed_two, gy, wg, wu, wd, hid, dg, du, total, grad_n):
    total[...], grad_n[...] = ffn_half(normed_two[...], gy[...], wg, wu, wd, hid, dg, du)


def ffn_body(
    after, normed_two, gain_two, gy, wg, wu, wd, total_o, grad_n_o,
    out, hid, dg, du, grad_after, grad_after_low, grad_gain,
):
    y = gy[...]
    total, grad_n = ffn_half(normed_two[...], y, wg, wu, wd, hid, dg, du)
    grad_n = grad_n + grad_n_o[...]
    h = after[...]
    out[...] = (h + (total + total_o[...])).astype(BF16)
    r = inv_rms(h)
    dn = grad_n * gain_two[...]
    grad_gain[...] = jnp.sum(grad_n * h * r, axis=0, keepdims=True)
    ga = y.astype(F32) + r * dn - h * (r * r * r * jnp.mean(dn * h, axis=-1, keepdims=True))
    grad_after[...] = ga
    grad_after_low[...] = ga.astype(BF16)


ORDER = (0, 2, 1, 3)
F_ROWS = 3840
A_ROWS = 1664


def place(i, by):
    return lax.rem(i + by, 4)


def y_places(core, y):
    one = y + 1 - 2 * lax.rem(y, 2)
    other = 3 - y
    first = jnp.where(core == 0, one, other)
    second = jnp.where(core == 0, other, one)
    return y, second, first, 2 - y + 2 * lax.rem(y, 2)


def ffn_grads_body(
    where, hid_m, hid_r, dg_m, dg_r, du_m, du_r, n, n_r, gy, gy_r, out_0, out_1, out_2, out_3, turned
):
    first = where[1]
    turned[:, :256] = n[...].T
    turned[:, 256:] = n_r[...].T
    for out, by in zip((out_0, out_1, out_2, out_3), ORDER):
        j = place(first, by)
        cols = pl.ds(pl.multiple_of(j * 256, 256), 256)
        for at, left, right in ((0, dg_m, dg_r), (1280, du_m, du_r)):
            g = dot(turned[:, :256], left[:, cols]) + dot(turned[:, 256:], right[:, cols])
            out[at : at + 640, :] = g[:, :128].astype(BF16)
            out[at + 640 : at + 1280, :] = g[:, 128:].astype(BF16)
        g = dot_tn(hid_m[:, cols], gy[...]) + dot_tn(hid_r[:, cols], gy_r[...])
        for b in range(5):
            out[2560 + b * 256 : 2816 + b * 256, :] = g[:, b * 128 : (b + 1) * 128].astype(BF16)


def attend_grad_body(
    where, query, kv, lse, ga_low, wo_m, wo_o, cos, sin, pos_row,
    dq_m, dq_o, dkv, back_two, back_one, dkv_m, packed,
):
    dkv_o = packed.at[512:, :]
    ok = allowed_pairs(pos_row)
    ga = ga_low[...]
    grad_k = None
    grad_v = None
    c, s = cos[512:, :], sin[512:, :]
    for half, wo, dq in ((1, wo_o, dq_o), (0, wo_m, dq_m)):
        grad_context = dot_nt(ga, wo[...]).astype(BF16)
        for head in range(2):
            cols = slice(half * MINE + head * HEAD, half * MINE + (head + 1) * HEAD)
            q = query[:, cols]
            gc = grad_context[:, head * HEAD : (head + 1) * HEAD]
            which = half * 2 + head
            scores = jnp.where(ok, dot_nt(q, kv[:, :HEAD]), neg_fill)
            probs = jnp.exp(scores - lse[:, which * 128 : which * 128 + 1])
            part = dot_tn(probs.astype(BF16), gc)
            grad_v = part if grad_v is None else grad_v + part
            grad_probs = dot_nt(gc, kv[:, HEAD:])
            row_dot = jnp.sum(grad_probs * probs, axis=-1, keepdims=True)
            grad_scores = (probs * (grad_probs - row_dot)).astype(BF16)
            gq = dot(grad_scores, kv[:, :HEAD]) * score_scale
            a, b = rotate_pair(gq[:, :HALF], gq[:, HALF:], c, -s)
            dq[:, head * HEAD : head * HEAD + HALF] = a.astype(BF16)
            dq[:, head * HEAD + HALF : (head + 1) * HEAD] = b.astype(BF16)
            part = dot_tn(grad_scores, q)
            grad_k = part if grad_k is None else grad_k + part
    a, b = rotate_pair(grad_k[:, :HALF], grad_k[:, HALF:], cos[...], -sin[...])
    packed[:256, :] = dq_o[:, :HEAD]
    packed[256:512, :] = dq_o[:, HEAD:]
    for rows, out in ((0, back_two), (256, back_one), (512, dkv)):
        rows = slice(rows, rows + 256)
        out[:, :HALF] = a[rows, :].astype(BF16)
        out[:, HALF:HEAD] = b[rows, :].astype(BF16)
        out[:, HEAD:] = grad_v[rows, :].astype(BF16)
    even = where[0] == 0
    dkv_m[:, :HALF] = jnp.where(even, a, b).astype(BF16)
    dkv_o[:, :HALF] = jnp.where(even, b, a).astype(BF16)
    va, vb = grad_v[:, :HALF], grad_v[:, HALF:]
    dkv_m[:, HALF:] = jnp.where(even, va, vb).astype(BF16)
    dkv_o[:, HALF:] = jnp.where(even, vb, va).astype(BF16)


def attend_grads_body(
    where, n, n_r, dq_m, dkv_m, packed, ctx, ctx_r, ga, ga_r, wq, wk, wv,
    gain, gain_two_grad, out_0, out_1, out_2, out_3, turned,
):
    turned[:, :768] = n[...].T
    turned[:, 768:] = n_r[...].T
    gk = dot(turned[:, :768], dkv_m[...]) + dot(turned[:, 768:], packed[512:, :])
    weighed = gk[:, :HALF] * wk[...].astype(F32) + gk[:, HALF:] * wv[...].astype(F32)
    gk = gk.astype(BF16)
    for out, j in zip((out_0, out_1, out_2, out_3), y_places(where[0], where[3])):
        cols = pl.ds(pl.multiple_of(j * 128, 128), 128)
        rows = pl.ds(pl.multiple_of(j // 2 * 256, 256), 256)
        half = pl.ds(pl.multiple_of(j % 2 * 128, 128), 128)
        g = dot(turned[:, 512:768], dq_m[:, cols]) + dot(turned[:, 1280:], packed[rows, half])
        weighed = weighed + g * wq[:, cols].astype(F32)
        out[:640, :] = g.astype(BF16)
        g = dot_tn(ctx[:, cols], ga[...]) + dot_tn(ctx_r[:, cols], ga_r[...])
        for b in range(5):
            out[960 + b * 128 : 1088 + b * 128, :] = g[:, b * 128 : (b + 1) * 128].astype(BF16)
        for at in range(4):

            @pl.when(j == at)
            def _(out=out, at=at):
                out[640:800, :] = gk[at * 160 : (at + 1) * 160, :HALF]
                out[800:960, :] = gk[at * 160 : (at + 1) * 160, HALF:]

    by_row = jnp.broadcast_to(jnp.sum(weighed, axis=1, keepdims=True), (640, 128))
    one = by_row.T[:1, :] / gain[...]
    two = gain_two_grad[...]
    rows = [v[:, b * 128 : (b + 1) * 128] for v in (one, two) for b in range(5)]
    block = jnp.concatenate([*rows, jnp.zeros((6, 128), F32)], axis=0).astype(BF16)
    for out in (out_0, out_1, out_2, out_3):
        out[1600:1616, :] = block
        out[1616:, :] = jnp.zeros((48, 128), BF16)


def token_grad_body(
    tok, gain, grad_after, dq_m, dq_o, dkv, back_one, back_two, wq_m, wq_o, wkv, out
):
    back = back_one[...].astype(F32) + back_two[...].astype(F32)
    own = (dkv[...].astype(F32) + back).astype(BF16)
    gn = dot_nt(dq_m[...], wq_m[...]) + dot_nt(dq_o[...], wq_o[...]) + dot_nt(own, wkv[...])
    x = tok[...].astype(F32)
    r = inv_rms(x)
    dm = gn * gain[...]
    out[...] = grad_after[...] + r * dm - x * (
        r * r * r * jnp.mean(dm * x, axis=-1, keepdims=True)
    )


def add_low(*terms):
    total = terms[0].astype(F32)
    for term in terms[1:]:
        total = total + term.astype(F32)
    return total.astype(BF16)


F_PART, A_PART = F_ROWS // 4, A_ROWS // 4
PART = F_PART + A_PART


def split_sum_body(
    where, own, r_two, r_one, r_minus, a_own, a_one, a_last, out_0, out_1, out_2, out_3
):
    for out, by in zip((out_0, out_1, out_2, out_3), ORDER):
        j = place(where[2], by)
        at = pl.ds(pl.multiple_of(j * F_PART, F_PART), F_PART)
        total = (own[at, :].astype(F32) + r_two[at, :].astype(F32)) + (
            r_one[at, :].astype(F32) + r_minus[at, :].astype(F32)
        )
        out[:F_PART, :] = total.astype(BF16)
        at = pl.ds(pl.multiple_of(j * A_PART, A_PART), A_PART)
        total = a_own[at, :].astype(F32) + a_one[at, :].astype(F32) + a_last[at, :].astype(F32)
        out[F_PART:, :] = total.astype(BF16)


def sum_four(own, r_two, r_one, r_minus):
    total = (own.astype(F32) + r_two.astype(F32)) + (r_one.astype(F32) + r_minus.astype(F32))
    return total.astype(BF16)


def join_body(where, own, r_two, r_one, r_minus, _, f_out, a_out, small):
    for ref, by in ((own, 0), (r_two, 2), (r_one, 3), (r_minus, 1)):
        j = place(where[2], by)
        f_out[pl.ds(pl.multiple_of(j * F_PART, F_PART), F_PART), :] = ref[:F_PART, :]
        a_out[pl.ds(pl.multiple_of(j * A_PART, A_PART), A_PART), :] = ref[F_PART:, :]
    small[...] = a_out[1600:1616, :]


SHARDS = ((D, FF // 2), (D, FF // 2), (FF // 2, D), (D, MINE), (D, HALF), (D, HALF), (MINE, D))
F_WIDE = ((D, 256), (D, 256), (256, D))
A_WIDE = ((D, 128), (160, 128), (160, 128), (128, D))


def spread_body(f_places, a_places, fresh, where, *refs):
    f_count, a_count = len(f_places), len(a_places)
    f_pieces, a_pieces = refs[:f_count], refs[f_count : f_count + a_count]
    refs = refs[f_count + a_count + (0 if fresh else len(SHARDS)) :]
    gate, up, down, query, key, value, out = refs[:7]
    sems = refs[-1]
    f_wide, a_wide = refs[7:10], refs[10:14]
    copies = []

    def send(source, target):
        copies.append(pltpu.make_async_copy(source, target, sems.at[len(copies)]))
        copies[-1].start()

    for i, (piece, by) in enumerate(zip(f_pieces, f_places)):
        j = place(where[1], by)
        cols = pl.ds(pl.multiple_of(j * 256, 256), 256)
        for at, wide, target in ((0, f_wide[0], gate), (1280, f_wide[1], up)):
            for b in range(2):
                wide[i, :, b * 128 : (b + 1) * 128] = piece[
                    at + b * 640 : at + (b + 1) * 640, :
                ].astype(F32)
            send(wide.at[i], target.at[:, cols])
        for b in range(5):
            at = 2560 + b * 256
            f_wide[2][i, :, b * 128 : (b + 1) * 128] = piece[at : at + 256, :].astype(F32)
        send(f_wide[2].at[i], down.at[cols, :])
    for i, (piece, (by, apart)) in enumerate(zip(a_pieces, a_places)):
        j = place(where[3], by + apart * where[0])
        block = pl.ds(pl.multiple_of(j * 128, 128), 128)
        rows = pl.ds(pl.multiple_of(j * 160, 32), 160)
        a_wide[0][i] = piece[:640, :].astype(F32)
        send(a_wide[0].at[i], query.at[:, block])
        a_wide[1][i] = piece[640:800, :].astype(F32)
        send(a_wide[1].at[i], key.at[rows, :])
        a_wide[2][i] = piece[800:960, :].astype(F32)
        send(a_wide[2].at[i], value.at[rows, :])
        for b in range(5):
            at = 960 + b * 128
            a_wide[3][i, :, b * 128 : (b + 1) * 128] = piece[at : at + 128, :].astype(F32)
        send(a_wide[3].at[i], out.at[block, :])
    for copy in copies:
        copy.wait()


def spread(where, f_pieces, f_places, a_pieces, a_places, shards):
    f_count, a_count = len(f_pieces), len(a_pieces)
    anywhere = pl.BlockSpec(memory_space=pl.ANY)
    return pl.pallas_call(
        functools.partial(spread_body, f_places, a_places, not shards),
        out_shape=[jax.ShapeDtypeStruct(s, F32) for s in SHARDS],
        in_specs=[
            pl.BlockSpec(memory_space=pltpu.SMEM),
            *[pl.BlockSpec(memory_space=pltpu.VMEM)] * (f_count + a_count),
            *[anywhere] * len(shards),
        ],
        out_specs=[anywhere] * len(SHARDS),
        input_output_aliases={1 + f_count + a_count + i: i for i in range(len(shards))},
        scratch_shapes=[
            *[pltpu.VMEM((f_count, *s), F32) for s in F_WIDE],
            *[pltpu.VMEM((max(a_count, 1), *s), F32) for s in A_WIDE],
            pltpu.SemaphoreType.DMA((3 * f_count + 4 * a_count,)),
        ],
        compiler_params=pltpu.CompilerParams(vmem_limit_bytes=20 * MIB),
        cost_estimate=pl.CostEstimate(flops=1024, bytes_accessed=1024, transcendentals=0),
        name="spread",
    )(where, *f_pieces, *a_pieces, *shards)


def local(
    tokens, positions, gain_attn, w_query, w_key, w_value, w_out, gain_ffn, w_gate, w_up, w_down,
    grad_out,
):
    tok = tokens[0]
    gy = grad_out[0]
    rows = tok.shape[0]
    ctx = lax.axis_index("ctx")
    core = lax.axis_index("fsdp")
    x_at, z_at, y_at = ctx // 16, ctx // 4 % 4, ctx % 4
    where = jnp.stack(
        [core, jnp.where(core == 0, x_at, z_at), jnp.where(core == 0, z_at, x_at), y_at]
    ).astype(jnp.int32)
    even = core == 0

    far_one = passed_along(tok, 1)
    far_two = passed_along(tok, 2)
    gains = jnp.concatenate([gain_attn, gain_ffn]).reshape(1, D)
    gains_other = swap(gains)
    key_other, value_other = swap(w_key), swap(w_value)
    query_other = swap(after(w_query, gains_other))
    out_other = swap(after(w_out, key_other))

    low = jnp.where(even, gains, gains_other)
    high = jnp.where(even, gains_other, gains)
    half_d = D // 2
    gain_one = jnp.concatenate([low[:, :half_d], high[:, :half_d]], axis=1).astype(F32)
    gain_two = jnp.concatenate([low[:, half_d:], high[:, half_d:]], axis=1).astype(F32)
    seq_pos = positions[0]
    key_pos = lax.dynamic_slice_in_dim(
        jnp.concatenate([jnp.full((2 * rows,), -2 * WINDOW, jnp.int32), seq_pos]), ctx * rows,
        3 * rows,
    )
    pos_row = key_pos.reshape(1, 3 * rows)
    frequency = rope_base ** (-(jnp.arange(HALF, dtype=F32) * 2.0 / HEAD))
    angles = key_pos.astype(F32)[:, None] * frequency[None, :]
    cos, sin = jnp.cos(angles), jnp.sin(angles)

    gy_r = swap(after(gy, value_other))
    normed, query, wkv, wide, wo_near = call(
        "query", query_body,
        [
            ((rows, D), BF16), ((rows, HEADS * HEAD), BF16), ((D, 2 * HEAD), BF16),
            ((rows, D), F32), ((MINE, D), BF16),
        ],
        [
            where, after(tok, gain_two, pos_row), gain_one, w_query, query_other, w_key,
            key_other, w_value, value_other, w_out, cos, sin,
        ],
        us=6, scalars=1,
    )
    first = (normed, far_one, far_two, out_other, gy_r)
    gate_other = swap(after(w_gate, *first))
    up_other = swap(after(w_up, *first))
    down_other = swap(after(w_down, *first))
    normed_all, query, kv, ctx_m, ctx_o, lse, after_attn, normed_two = call(
        "attend", attend_body,
        [
            ((3 * rows, D), BF16), ((rows, HEADS * HEAD), BF16), ((3 * rows, 2 * HEAD), BF16),
            ((rows, MINE), BF16), ((rows, MINE), BF16), ((rows, 512), F32), ((rows, D), F32),
            ((rows, D), BF16),
        ],
        [
            far_two, far_one, normed, wide, query, wkv, gain_one, wo_near, out_other, gain_two,
            cos, sin, pos_row,
        ],
        us=5,
    )
    normed_two_r = swap(normed_two)
    half_ffn = [((rows, FF // 2), BF16)] * 3
    hid_o, dg_o, du_o, total_o, grad_n_o = call(
        "ffn_other", ffn_other_body, [*half_ffn, ((rows, D), F32), ((rows, D), F32)],
        [normed_two, gy, gate_other, up_other, down_other],
        us=5,
    )
    gain_two = after(gain_two, normed_two_r)
    hid_r, dg_r, du_r = swap(hid_o), swap(dg_o), swap(du_o)
    ctx_r, normed_r = swap(after(ctx_o, hid_o)), swap(after(normed_all, hid_o))
    out, hid_m, dg_m, du_m, grad_after, ga_low, grad_gain_two = call(
        "ffn", ffn_body,
        [((rows, D), BF16), *half_ffn, ((rows, D), F32), ((rows, D), BF16), ((1, D), F32)],
        [after_attn, normed_two, gain_two, gy, w_gate, w_up, w_down, total_o, grad_n_o],
        us=4,
    )
    ga_r = swap(ga_low)
    dq_m, dq_o, dkv, back_two, back_one, dkv_m, packed = call(
        "attend_grad", attend_grad_body,
        [
            ((rows, MINE), BF16), ((rows, MINE), BF16), *[((rows, 2 * HEAD), BF16)] * 3,
            ((3 * rows, HEAD), BF16), ((5 * rows, HEAD), BF16),
        ],
        [
            where, query, kv, lse, ga_low, w_out, out_other, cos, sin, pos_row,
        ],
        us=0, scalars=1,
    )
    packed_r = swap(packed)
    f_chunks = call(
        "ffn_grads", ffn_grads_body, [((F_ROWS, 128), BF16)] * 4,
        [where, after(hid_m, packed), hid_r, dg_m, dg_r, du_m, du_r, normed_two, normed_two_r, gy, gy_r],
        scalars=1, scratch=[pltpu.VMEM((D, 512), BF16)],
        us=3,
    )
    f_got = to_peers(f_chunks[1:], shift_first)

    a_chunks = call(
        "attend_grads", attend_grads_body, [((A_ROWS, 128), BF16)] * 4,
        [
            where, normed_all, normed_r, after(dq_m, f_chunks[0]), dkv_m, packed_r, ctx_m, ctx_r, ga_low, ga_r,
            w_query, w_key, w_value, gain_one, grad_gain_two,
        ],
        us=0, scalars=1, scratch=[pltpu.VMEM((D, 6 * rows), BF16)],
    )
    a_own, a_next, a_far_own, a_far_next = a_chunks
    a_next_r, a_own_r = swap_y(a_far_next, 0), swap_y(a_far_own, 0)
    a_last_r = swap_y(add_low(a_next, a_next_r), 1)
    parts = call(
        "split", split_sum_body, [((PART, 128), BF16)] * 4,
        [where, after(f_chunks[0], a_own), *f_got, a_own, a_own_r, a_last_r], us=0, scalars=1,
    )
    got = [parts[0], *to_peers(parts[1:], shift_second)]
    f_two = sum_four(*[part[:F_PART] for part in got])
    a_two = sum_four(*[part[F_PART:] for part in got])
    f_pair = add_low(f_two, swap_y(f_two, 0))
    a_pair = add_low(a_two, swap_first(a_two, 0))
    f_three = add_low(f_pair, swap_y(f_pair, 1))
    back_two = passed_along(after(back_two, f_two), -2)
    back_one = passed_along(after(back_one, f_two), -1)
    turn = swap(after(swap(after(grad_gain_two, back_one, back_two)), f_pair))
    a_three = add_low(a_pair, swap_first(after(a_pair, f_pair), 1))
    own, turn = lax.optimization_barrier((jnp.concatenate([f_three, a_three]), turn))
    f_whole, a_whole, small = call(
        "join", join_body,
        [((F_ROWS, 128), BF16), ((A_ROWS, 128), BF16), ((16, 128), BF16)],
        [where, own, *to_peers([own] * 3, shift_second), turn], us=0, scalars=1,
    )
    small_r = swap(small)
    everywhere = ("ctx", "fsdp")
    f_send, a_send = after(f_whole, small_r), after(a_whole, small_r)
    f_got = to_peers([f_send] * 3, shift_first)
    a_two = lax.ppermute(a_send, everywhere, shift_y(2))
    a_one = lax.ppermute(a_send, everywhere, shift_apart(1))
    grad_tokens = call(
        "token_grad", token_grad_body, [((rows, D), F32)],
        [
            tok, gain_one, grad_after, dq_m, dq_o, dkv, back_one, back_two, w_query, query_other,
            wkv,
        ],
        us=2,
    )[0]

    shards = spread(where, [after(f_whole, grad_tokens)], (0,), [a_whole], ((0, 0),), [])
    a_other = lax.ppermute(after(a_send, f_got[0]), everywhere, shift_apart(-1))
    shards = spread(where, f_got[:1], (2,), [], (), shards)
    g_gate, g_up, g_down, g_query, g_key, g_value, g_out = spread(
        where, f_got[1:], (3, 1), [a_two, a_one, a_other], ((2, 0), (3, -2), (1, 2)), shards
    )
    g_gains = (after(small, g_key).astype(F32) + small_r.astype(F32))[:10].reshape(2, D)
    g_gains = jnp.where(even, g_gains[:, :half_d], g_gains[:, half_d:])
    return (
        out[None], grad_tokens[None], g_gains[0], g_query, g_key, g_value, g_out, g_gains[1],
        g_gate, g_up, g_down,
    )


def solution(mesh):
    tokens = P("fsdp", "ctx", None)
    columns, rows = P(None, "fsdp"), P("fsdp", None)
    in_specs = (
        tokens, P("fsdp", None), P("fsdp"), columns, columns, columns, rows, P("fsdp"), columns,
        columns, rows, tokens,
    )
    out_specs = (
        tokens, tokens, P("fsdp"), columns, columns, columns, rows, P("fsdp"), columns, columns,
        rows,
    )
    return jax.shard_map(local, mesh=mesh, in_specs=in_specs, out_specs=out_specs, check_vma=False)
```

```python
import functools

import jax
import jax.numpy as jnp
from jax import lax
from jax.experimental import pallas as pl
from jax.experimental.pallas import tpu as pltpu
from jax.sharding import PartitionSpec as P

D = 640
HEADS = 4
HEAD = 256
FF = 2048
WINDOW = 512
HALF = HEAD // 2
MINE = 2 * HEAD

epsilon = 1e-06
rope_base = 10000.0
neg_fill = -1e30
score_scale = HEAD ** (-0.5)
gelu_c = 0.7978845608028654
gelu_k = 0.044715

F32 = jnp.float32
BF16 = jnp.bfloat16
MIB = 1024 * 1024


def swap(x):
    return lax.ppermute(x, "fsdp", [(0, 1), (1, 0)])


def chip_pairs(move):
    pairs = []
    for x in range(4):
        for z in range(4):
            for y in range(4):
                for c in range(2):
                    tx, tz, ty = move(x, z, y, c)
                    target = (((tx % 4) * 4 + tz % 4) * 4 + ty % 4) * 2 + c
                    pairs.append((((x * 4 + z) * 4 + y) * 2 + c, target))
    return pairs


def shift_first(by):
    return chip_pairs(lambda x, z, y, c: (x + by, z, y) if c == 0 else (x, z + by, y))


def shift_second(by):
    return chip_pairs(lambda x, z, y, c: (x, z + by, y) if c == 0 else (x + by, z, y))


def shift_y(by):
    return chip_pairs(lambda x, z, y, c: (x, z, y + by))


def shift_apart(by):
    return chip_pairs(lambda x, z, y, c: (x, z, y + by - 2 * by * c))


def after(x, *done):
    return lax.optimization_barrier((x, *done))[0]


def pair_first(v):
    return v ^ 1


def pair_second(v):
    return 3 - v


def swap_y(v, step):
    return lax.ppermute(
        v, ("ctx", "fsdp"),
        chip_pairs(lambda x, z, y, c: (x, z, (pair_first, pair_second)[c ^ step](y))),
    )


def swap_first(v, step):
    pair = (pair_first, pair_second)[step]
    return lax.ppermute(
        v, ("ctx", "fsdp"),
        chip_pairs(lambda x, z, y, c: (pair(x), z, y) if c == 0 else (x, pair(z), y)),
    )


def to_peers(parts, shift):
    return [
        lax.ppermute(part, ("ctx", "fsdp"), shift(by)) for part, by in zip(parts, (2, 1, -1))
    ]


def passed_along(shard, by):
    peers = lax.axis_size("ctx")
    pairs = [(i, i + by) for i in range(peers) if 0 <= i + by < peers]
    return lax.ppermute(shard, "ctx", pairs)


def dot(a, b):
    return lax.dot_general(a, b, (((1,), (0,)), ((), ())), preferred_element_type=F32)


def dot_nt(a, b):
    return lax.dot_general(a, b, (((1,), (1,)), ((), ())), preferred_element_type=F32)


def dot_tn(a, b):
    return lax.dot_general(a, b, (((0,), (0,)), ((), ())), preferred_element_type=F32)


def call(name, body, outs, ins, us, scalars=0, scratch=(), extra=8):
    smem = pl.BlockSpec(memory_space=pltpu.SMEM)
    whole = pl.BlockSpec(memory_space=pltpu.VMEM)
    shapes = [jax.ShapeDtypeStruct(s, t) for s, t in outs]
    held = sum(x.size * x.dtype.itemsize for x in [*ins, *shapes])
    return pl.pallas_call(
        body,
        out_shape=shapes,
        in_specs=[smem] * scalars
        + [whole] * (len(ins) - scalars),
        out_specs=[whole] * len(outs),
        scratch_shapes=scratch,
        compiler_params=pltpu.CompilerParams(vmem_limit_bytes=held + extra * MIB),
        cost_estimate=pl.CostEstimate(
            flops=int(us * 1.1e9), bytes_accessed=1024, transcendentals=0
        ),
        name=name,
    )(*ins)


def inv_rms(x):
    return lax.rsqrt(jnp.mean(x * x, axis=-1, keepdims=True) + epsilon)


def rotate_pair(a, b, c, s):
    return a * c - b * s, b * c + a * s


def allowed_pairs(pos_row):
    keys = pos_row[...].astype(F32)
    own = jnp.broadcast_to(keys[:, 512:], (128, 256)).T[:, :1]
    distance = own - keys
    return (distance >= 0) & (distance < WINDOW)


def query_body(
    where, tok, gain, wq_m, wq_o, wk_m, wk_o, wv_m, wv_o, wo, cos, sin,
    normed, query, wkv, wide, wo_near,
):
    x = tok[...].astype(F32)
    wide[...] = x
    wo_near[...] = wo[...]
    n = (x * inv_rms(x) * gain[...]).astype(BF16)
    normed[...] = n
    c, s = cos[512:, :], sin[512:, :]
    for half, w in enumerate((wq_m, wq_o)):
        raw = dot(n, w[...])
        for head in range(2):
            a = raw[:, head * HEAD : head * HEAD + HALF]
            b = raw[:, head * HEAD + HALF : (head + 1) * HEAD]
            ra, rb = rotate_pair(a, b, c, s)
            at = half * MINE + head * HEAD
            query[:, at : at + HALF] = (ra * score_scale).astype(BF16)
            query[:, at + HALF : at + HEAD] = (rb * score_scale).astype(BF16)
    for which, (a, b, c, d) in enumerate(((wk_m, wk_o, wv_m, wv_o), (wk_o, wk_m, wv_o, wv_m))):

        @pl.when(where[0] == which)
        def _(parts=(a, b, c, d)):
            for i, part in enumerate(parts):
                wkv[:, i * HALF : (i + 1) * HALF] = part[...]


def attend_body(
    far_two, far_one, normed, wide, query, wkv, gain, wo_m, wo_o, gain_two, cos, sin, pos_row,
    normed_all, query_kept, kv, ctx_m, ctx_o, kept, after, normed_two,
):
    query_kept[...] = query[...]
    normed_all[512:, :] = normed[...]
    for i, far in enumerate((far_two, far_one)):
        x = far[...].astype(F32)
        normed_all[i * 256 : (i + 1) * 256, :] = (x * inv_rms(x) * gain[...]).astype(BF16)
    raw = dot(normed_all[...], wkv[...])
    ka, kb = rotate_pair(raw[:, :HALF], raw[:, HALF:HEAD], cos[...], sin[...])
    kv[:, :HALF] = ka.astype(BF16)
    kv[:, HALF:HEAD] = kb.astype(BF16)
    kv[:, HEAD:] = raw[:, HEAD:].astype(BF16)
    ok = allowed_pairs(pos_row)
    for head in range(HEADS):
        cols = slice(head * HEAD, (head + 1) * HEAD)
        scores = jnp.where(ok, dot_nt(query[:, cols], kv[:, :HEAD]), neg_fill)
        top = jnp.max(scores, axis=-1, keepdims=True)
        exps = jnp.exp(scores - top)
        total = jnp.sum(exps, axis=-1, keepdims=True)
        probs = exps * (1.0 / total)
        kept[head] = probs
        probs = probs.astype(BF16)
        context = (ctx_m, ctx_o)[head // 2]
        at = head % 2 * HEAD
        context[:, at : at + HEAD] = dot(probs, kv[:, HEAD:]).astype(BF16)
    h = wide[...] + (dot(ctx_m[...], wo_m[...]) + dot(ctx_o[...], wo_o[...]))
    after[...] = h
    normed_two[...] = (h * inv_rms(h) * gain_two[...]).astype(BF16)


FFN_STEP = 512


def ffn_half(n, y, wg, wu, wd, hid, dg, du):
    total = None
    grad_n = None
    for at in range(0, FF // 2, FFN_STEP):
        cols = slice(at, at + FFN_STEP)
        gate = dot(n, wg[:, cols])
        up = dot(n, wu[:, cols])
        grad_hidden = dot_nt(y, wd[cols, :])
        square = gate * gate
        t = jnp.tanh(gelu_c * gate * (1.0 + gelu_k * square))
        one_t = 0.5 + 0.5 * t
        act = gate * one_t
        slope = one_t + 0.5 * gate * (1.0 - t * t) * (gelu_c * (1.0 + 3.0 * gelu_k * square))
        hidden = (act * up).astype(BF16)
        grad_gate = (grad_hidden * up * slope).astype(BF16)
        grad_up = (grad_hidden * act).astype(BF16)
        hid[:, cols] = hidden
        dg[:, cols] = grad_gate
        du[:, cols] = grad_up
        part = dot(hidden, wd[cols, :])
        total = part if total is None else total + part
        part = dot_nt(grad_gate, wg[:, cols]) + dot_nt(grad_up, wu[:, cols])
        grad_n = part if grad_n is None else grad_n + part
    return total, grad_n


def ffn_other_body(normed_two, gy, wg, wu, wd, hid, dg, du, total, grad_n):
    total[...], grad_n[...] = ffn_half(normed_two[...], gy[...], wg, wu, wd, hid, dg, du)


def ffn_body(
    after, normed_two, gain_two, gy, wg, wu, wd, total_o, grad_n_o,
    out, hid, dg, du, grad_after, grad_after_low, grad_gain,
):
    y = gy[...]
    total, grad_n = ffn_half(normed_two[...], y, wg, wu, wd, hid, dg, du)
    grad_n = grad_n + grad_n_o[...]
    h = after[...]
    out[...] = (h + (total + total_o[...])).astype(BF16)
    r = inv_rms(h)
    dn = grad_n * gain_two[...]
    grad_gain[...] = jnp.sum(grad_n * h * r, axis=0, keepdims=True)
    ga = y.astype(F32) + r * dn - h * (r * r * r * jnp.mean(dn * h, axis=-1, keepdims=True))
    grad_after[...] = ga
    grad_after_low[...] = ga.astype(BF16)


ORDER = (0, 2, 1, 3)
F_ROWS = 3840
A_ROWS = 1664


def place(i, by):
    return lax.rem(i + by, 4)


def y_places(core, y):
    one = y + 1 - 2 * lax.rem(y, 2)
    other = 3 - y
    first = jnp.where(core == 0, one, other)
    second = jnp.where(core == 0, other, one)
    return y, second, first, 2 - y + 2 * lax.rem(y, 2)


def ffn_grads_body(
    where, hid_m, hid_r, dg_m, dg_r, du_m, du_r, n, n_r, gy, gy_r, out_0, out_1, out_2, out_3, turned
):
    first = where[1]
    turned[:, :256] = n[...].T
    turned[:, 256:] = n_r[...].T
    for out, by in zip((out_0, out_1, out_2, out_3), ORDER):
        j = place(first, by)
        cols = pl.ds(pl.multiple_of(j * 256, 256), 256)
        for at, left, right in ((0, dg_m, dg_r), (1280, du_m, du_r)):
            g = dot(turned[:, :256], left[:, cols]) + dot(turned[:, 256:], right[:, cols])
            out[at : at + 640, :] = g[:, :128].astype(BF16)
            out[at + 640 : at + 1280, :] = g[:, 128:].astype(BF16)
        g = dot_tn(hid_m[:, cols], gy[...]) + dot_tn(hid_r[:, cols], gy_r[...])
        for b in range(5):
            out[2560 + b * 256 : 2816 + b * 256, :] = g[:, b * 128 : (b + 1) * 128].astype(BF16)


def attend_grad_body(
    where, query, kv, kept, ga_low, wo_m, wo_o, cos, sin,
    dq_m, dq_o, dkv, back_two, back_one, dkv_m, packed,
):
    dkv_o = packed.at[512:, :]
    ga = ga_low[...]
    grad_k = None
    grad_v = None
    c, s = cos[512:, :], sin[512:, :]
    for half, wo, dq in ((1, wo_o, dq_o), (0, wo_m, dq_m)):
        grad_context = dot_nt(ga, wo[...]).astype(BF16)
        for head in range(2):
            cols = slice(half * MINE + head * HEAD, half * MINE + (head + 1) * HEAD)
            q = query[:, cols]
            gc = grad_context[:, head * HEAD : (head + 1) * HEAD]
            which = half * 2 + head
            probs = kept[which]
            part = dot_tn(probs.astype(BF16), gc)
            grad_v = part if grad_v is None else grad_v + part
            grad_probs = dot_nt(gc, kv[:, HEAD:])
            row_dot = jnp.sum(grad_probs * probs, axis=-1, keepdims=True)
            grad_scores = (probs * (grad_probs - row_dot)).astype(BF16)
            gq = dot(grad_scores, kv[:, :HEAD]) * score_scale
            a, b = rotate_pair(gq[:, :HALF], gq[:, HALF:], c, -s)
            dq[:, head * HEAD : head * HEAD + HALF] = a.astype(BF16)
            dq[:, head * HEAD + HALF : (head + 1) * HEAD] = b.astype(BF16)
            part = dot_tn(grad_scores, q)
            grad_k = part if grad_k is None else grad_k + part
    a, b = rotate_pair(grad_k[:, :HALF], grad_k[:, HALF:], cos[...], -sin[...])
    packed[:256, :] = dq_o[:, :HEAD]
    packed[256:512, :] = dq_o[:, HEAD:]
    for rows, out in ((0, back_two), (256, back_one), (512, dkv)):
        rows = slice(rows, rows + 256)
        out[:, :HALF] = a[rows, :].astype(BF16)
        out[:, HALF:HEAD] = b[rows, :].astype(BF16)
        out[:, HEAD:] = grad_v[rows, :].astype(BF16)
    even = where[0] == 0
    dkv_m[:, :HALF] = jnp.where(even, a, b).astype(BF16)
    dkv_o[:, :HALF] = jnp.where(even, b, a).astype(BF16)
    va, vb = grad_v[:, :HALF], grad_v[:, HALF:]
    dkv_m[:, HALF:] = jnp.where(even, va, vb).astype(BF16)
    dkv_o[:, HALF:] = jnp.where(even, vb, va).astype(BF16)


def attend_grads_body(
    where, n, n_r, dq_m, dkv_m, packed, ctx, ctx_r, ga, ga_r, wq, wk, wv,
    gain, gain_two_grad, out_0, out_1, out_2, out_3, turned,
):
    turned[:, :768] = n[...].T
    turned[:, 768:] = n_r[...].T
    gk = dot(turned[:, :768], dkv_m[...]) + dot(turned[:, 768:], packed[512:, :])
    weighed = gk[:, :HALF] * wk[...].astype(F32) + gk[:, HALF:] * wv[...].astype(F32)
    gk = gk.astype(BF16)
    for out, j in zip((out_0, out_1, out_2, out_3), y_places(where[0], where[3])):
        cols = pl.ds(pl.multiple_of(j * 128, 128), 128)
        rows = pl.ds(pl.multiple_of(j // 2 * 256, 256), 256)
        half = pl.ds(pl.multiple_of(j % 2 * 128, 128), 128)
        g = dot(turned[:, 512:768], dq_m[:, cols]) + dot(turned[:, 1280:], packed[rows, half])
        weighed = weighed + g * wq[:, cols].astype(F32)
        out[:640, :] = g.astype(BF16)
        g = dot_tn(ctx[:, cols], ga[...]) + dot_tn(ctx_r[:, cols], ga_r[...])
        for b in range(5):
            out[960 + b * 128 : 1088 + b * 128, :] = g[:, b * 128 : (b + 1) * 128].astype(BF16)
        for at in range(4):

            @pl.when(j == at)
            def _(out=out, at=at):
                out[640:800, :] = gk[at * 160 : (at + 1) * 160, :HALF]
                out[800:960, :] = gk[at * 160 : (at + 1) * 160, HALF:]

    by_row = jnp.broadcast_to(jnp.sum(weighed, axis=1, keepdims=True), (640, 128))
    one = by_row.T[:1, :] / gain[...]
    two = gain_two_grad[...]
    rows = [v[:, b * 128 : (b + 1) * 128] for v in (one, two) for b in range(5)]
    block = jnp.concatenate([*rows, jnp.zeros((6, 128), F32)], axis=0).astype(BF16)
    for out in (out_0, out_1, out_2, out_3):
        out[1600:1616, :] = block
        out[1616:, :] = jnp.zeros((48, 128), BF16)


def token_grad_body(
    tok, gain, grad_after, dq_m, dq_o, dkv, back_one, back_two, wq_m, wq_o, wkv, out
):
    back = back_one[...].astype(F32) + back_two[...].astype(F32)
    own = (dkv[...].astype(F32) + back).astype(BF16)
    gn = dot_nt(dq_m[...], wq_m[...]) + dot_nt(dq_o[...], wq_o[...]) + dot_nt(own, wkv[...])
    x = tok[...].astype(F32)
    r = inv_rms(x)
    dm = gn * gain[...]
    out[...] = grad_after[...] + r * dm - x * (
        r * r * r * jnp.mean(dm * x, axis=-1, keepdims=True)
    )


def add_low(*terms):
    total = terms[0].astype(F32)
    for term in terms[1:]:
        total = total + term.astype(F32)
    return total.astype(BF16)


F_PART, A_PART = F_ROWS // 4, A_ROWS // 4
PART = F_PART + A_PART


def split_sum_body(
    where, own, r_two, r_one, r_minus, a_own, a_one, a_last, out_0, out_1, out_2, out_3
):
    for out, by in zip((out_0, out_1, out_2, out_3), ORDER):
        j = place(where[2], by)
        at = pl.ds(pl.multiple_of(j * F_PART, F_PART), F_PART)
        total = (own[at, :].astype(F32) + r_two[at, :].astype(F32)) + (
            r_one[at, :].astype(F32) + r_minus[at, :].astype(F32)
        )
        out[:F_PART, :] = total.astype(BF16)
        at = pl.ds(pl.multiple_of(j * A_PART, A_PART), A_PART)
        total = a_own[at, :].astype(F32) + a_one[at, :].astype(F32) + a_last[at, :].astype(F32)
        out[F_PART:, :] = total.astype(BF16)


def sum_four(own, r_two, r_one, r_minus):
    total = (own.astype(F32) + r_two.astype(F32)) + (r_one.astype(F32) + r_minus.astype(F32))
    return total.astype(BF16)


def join_body(where, own, r_two, r_one, r_minus, _, f_out, a_out, small):
    for ref, by in ((own, 0), (r_two, 2), (r_one, 3), (r_minus, 1)):
        j = place(where[2], by)
        f_out[pl.ds(pl.multiple_of(j * F_PART, F_PART), F_PART), :] = ref[:F_PART, :]
        a_out[pl.ds(pl.multiple_of(j * A_PART, A_PART), A_PART), :] = ref[F_PART:, :]
    small[...] = a_out[1600:1616, :]


SHARDS = ((D, FF // 2), (D, FF // 2), (FF // 2, D), (D, MINE), (D, HALF), (D, HALF), (MINE, D))
F_WIDE = ((D, 256), (D, 256), (256, D))
A_WIDE = ((D, 128), (160, 128), (160, 128), (128, D))


def spread_body(f_places, a_places, fresh, where, *refs):
    f_count, a_count = len(f_places), len(a_places)
    f_pieces, a_pieces = refs[:f_count], refs[f_count : f_count + a_count]
    refs = refs[f_count + a_count + (0 if fresh else len(SHARDS)) :]
    gate, up, down, query, key, value, out = refs[:7]
    sems = refs[-1]
    f_wide, a_wide = refs[7:10], refs[10:14]
    copies = []

    def send(source, target):
        copies.append(pltpu.make_async_copy(source, target, sems.at[len(copies)]))
        copies[-1].start()

    for i, (piece, by) in enumerate(zip(f_pieces, f_places)):
        j = place(where[1], by)
        cols = pl.ds(pl.multiple_of(j * 256, 256), 256)
        for at, wide, target in ((0, f_wide[0], gate), (1280, f_wide[1], up)):
            for b in range(2):
                wide[i, :, b * 128 : (b + 1) * 128] = piece[
                    at + b * 640 : at + (b + 1) * 640, :
                ].astype(F32)
            send(wide.at[i], target.at[:, cols])
        for b in range(5):
            at = 2560 + b * 256
            f_wide[2][i, :, b * 128 : (b + 1) * 128] = piece[at : at + 256, :].astype(F32)
        send(f_wide[2].at[i], down.at[cols, :])
    for i, (piece, (by, apart)) in enumerate(zip(a_pieces, a_places)):
        j = place(where[3], by + apart * where[0])
        block = pl.ds(pl.multiple_of(j * 128, 128), 128)
        rows = pl.ds(pl.multiple_of(j * 160, 32), 160)
        a_wide[0][i] = piece[:640, :].astype(F32)
        send(a_wide[0].at[i], query.at[:, block])
        a_wide[1][i] = piece[640:800, :].astype(F32)
        send(a_wide[1].at[i], key.at[rows, :])
        a_wide[2][i] = piece[800:960, :].astype(F32)
        send(a_wide[2].at[i], value.at[rows, :])
        for b in range(5):
            at = 960 + b * 128
            a_wide[3][i, :, b * 128 : (b + 1) * 128] = piece[at : at + 128, :].astype(F32)
        send(a_wide[3].at[i], out.at[block, :])
    for copy in copies:
        copy.wait()


def spread(where, f_pieces, f_places, a_pieces, a_places, shards):
    f_count, a_count = len(f_pieces), len(a_pieces)
    anywhere = pl.BlockSpec(memory_space=pl.ANY)
    return pl.pallas_call(
        functools.partial(spread_body, f_places, a_places, not shards),
        out_shape=[jax.ShapeDtypeStruct(s, F32) for s in SHARDS],
        in_specs=[
            pl.BlockSpec(memory_space=pltpu.SMEM),
            *[pl.BlockSpec(memory_space=pltpu.VMEM)] * (f_count + a_count),
            *[anywhere] * len(shards),
        ],
        out_specs=[anywhere] * len(SHARDS),
        input_output_aliases={1 + f_count + a_count + i: i for i in range(len(shards))},
        scratch_shapes=[
            *[pltpu.VMEM((f_count, *s), F32) for s in F_WIDE],
            *[pltpu.VMEM((max(a_count, 1), *s), F32) for s in A_WIDE],
            pltpu.SemaphoreType.DMA((3 * f_count + 4 * a_count,)),
        ],
        compiler_params=pltpu.CompilerParams(vmem_limit_bytes=20 * MIB),
        cost_estimate=pl.CostEstimate(flops=1024, bytes_accessed=1024, transcendentals=0),
        name="spread",
    )(where, *f_pieces, *a_pieces, *shards)


def local(
    tokens, positions, gain_attn, w_query, w_key, w_value, w_out, gain_ffn, w_gate, w_up, w_down,
    grad_out,
):
    tok = tokens[0]
    gy = grad_out[0]
    rows = tok.shape[0]
    ctx = lax.axis_index("ctx")
    core = lax.axis_index("fsdp")
    x_at, z_at, y_at = ctx // 16, ctx // 4 % 4, ctx % 4
    where = jnp.stack(
        [core, jnp.where(core == 0, x_at, z_at), jnp.where(core == 0, z_at, x_at), y_at]
    ).astype(jnp.int32)
    even = core == 0

    far_one = passed_along(tok, 1)
    far_two = passed_along(tok, 2)
    gains = jnp.concatenate([gain_attn, gain_ffn]).reshape(1, D)
    gains_other = swap(gains)
    key_other, value_other = swap(w_key), swap(w_value)
    query_other = swap(after(w_query, gains_other))
    out_other = swap(after(w_out, key_other))

    low = jnp.where(even, gains, gains_other)
    high = jnp.where(even, gains_other, gains)
    half_d = D // 2
    gain_one = jnp.concatenate([low[:, :half_d], high[:, :half_d]], axis=1).astype(F32)
    gain_two = jnp.concatenate([low[:, half_d:], high[:, half_d:]], axis=1).astype(F32)
    seq_pos = positions[0]
    key_pos = lax.dynamic_slice_in_dim(
        jnp.concatenate([jnp.full((2 * rows,), -2 * WINDOW, jnp.int32), seq_pos]), ctx * rows,
        3 * rows,
    )
    pos_row = key_pos.reshape(1, 3 * rows)
    frequency = rope_base ** (-(jnp.arange(HALF, dtype=F32) * 2.0 / HEAD))
    angles = key_pos.astype(F32)[:, None] * frequency[None, :]
    cos, sin = jnp.cos(angles), jnp.sin(angles)

    gy_r = swap(after(gy, value_other))
    normed, query, wkv, wide, wo_near = call(
        "query", query_body,
        [
            ((rows, D), BF16), ((rows, HEADS * HEAD), BF16), ((D, 2 * HEAD), BF16),
            ((rows, D), F32), ((MINE, D), BF16),
        ],
        [
            where, after(tok, gain_two, pos_row), gain_one, w_query, query_other, w_key,
            key_other, w_value, value_other, w_out, cos, sin,
        ],
        us=6, scalars=1,
    )
    first = (normed, far_one, far_two, out_other, gy_r)
    gate_other = swap(after(w_gate, out_other, query_other))
    up_other = swap(after(w_up, *first))
    down_other = swap(after(w_down, *first))
    normed_all, query, kv, ctx_m, ctx_o, kept, after_attn, normed_two = call(
        "attend", attend_body,
        [
            ((3 * rows, D), BF16), ((rows, HEADS * HEAD), BF16), ((3 * rows, 2 * HEAD), BF16),
            ((rows, MINE), BF16), ((rows, MINE), BF16), ((HEADS, rows, 3 * rows), F32), ((rows, D), F32),
            ((rows, D), BF16),
        ],
        [
            far_two, far_one, normed, wide, query, wkv, after(gain_one, gate_other), wo_near,
            out_other, gain_two,
            cos, sin, pos_row,
        ],
        us=5,
    )
    half_ffn = [((rows, FF // 2), BF16)] * 3
    hid_o, dg_o, du_o, total_o, grad_n_o = call(
        "ffn_other", ffn_other_body, [*half_ffn, ((rows, D), F32), ((rows, D), F32)],
        [normed_two, gy, gate_other, up_other, down_other],
        us=5,
    )
    hid_r, dg_r, du_r = swap(hid_o), swap(dg_o), swap(du_o)
    normed_two_r, normed_r = swap(after(normed_two, hid_o)), swap(after(normed_all, hid_o))
    ctx_r = swap(after(ctx_o, hid_r))
    out, hid_m, dg_m, du_m, grad_after, ga_low, grad_gain_two = call(
        "ffn", ffn_body,
        [((rows, D), BF16), *half_ffn, ((rows, D), F32), ((rows, D), BF16), ((1, D), F32)],
        [after_attn, normed_two, gain_two, gy, w_gate, w_up, w_down, total_o, grad_n_o],
        us=4,
    )
    ga_r = swap(ga_low)
    dq_m, dq_o, dkv, back_two, back_one, dkv_m, packed = call(
        "attend_grad", attend_grad_body,
        [
            ((rows, MINE), BF16), ((rows, MINE), BF16), *[((rows, 2 * HEAD), BF16)] * 3,
            ((3 * rows, HEAD), BF16), ((5 * rows, HEAD), BF16),
        ],
        [
            where, query, kv, kept, ga_low, w_out, out_other, cos, sin,
        ],
        us=0, scalars=1,
    )
    packed_r = swap(packed)
    f_chunks = call(
        "ffn_grads", ffn_grads_body, [((F_ROWS, 128), BF16)] * 4,
        [where, after(hid_m, packed), hid_r, dg_m, dg_r, du_m, du_r, normed_two, normed_two_r, gy, gy_r],
        scalars=1, scratch=[pltpu.VMEM((D, 512), BF16)],
        us=3,
    )
    f_got = to_peers(f_chunks[1:], shift_first)

    a_chunks = call(
        "attend_grads", attend_grads_body, [((A_ROWS, 128), BF16)] * 4,
        [
            where, normed_all, normed_r, after(dq_m, f_chunks[0]), dkv_m, packed_r, ctx_m, ctx_r, ga_low, ga_r,
            w_query, w_key, w_value, gain_one, grad_gain_two,
        ],
        us=0, scalars=1, scratch=[pltpu.VMEM((D, 6 * rows), BF16)],
    )
    a_own, a_next, a_far_own, a_far_next = a_chunks
    a_next_r, a_own_r = swap_y(a_far_next, 0), swap_y(a_far_own, 0)
    a_last_r = swap_y(add_low(a_next, a_next_r), 1)
    parts = call(
        "split", split_sum_body, [((PART, 128), BF16)] * 4,
        [where, after(f_chunks[0], a_own), *f_got, a_own, a_own_r, a_last_r], us=0, scalars=1,
    )
    got = [parts[0], *to_peers(parts[1:], shift_second)]
    f_two = sum_four(*[part[:F_PART] for part in got])
    a_two = sum_four(*[part[F_PART:] for part in got])
    f_pair = add_low(f_two, swap_y(f_two, 0))
    a_pair = add_low(a_two, swap_first(a_two, 0))
    f_three = add_low(f_pair, swap_y(f_pair, 1))
    back_two = passed_along(after(back_two, f_two), -2)
    back_one = passed_along(after(back_one, f_two), -1)
    turn = swap(after(swap(after(grad_gain_two, back_one, back_two)), f_pair))
    a_three = add_low(a_pair, swap_first(after(a_pair, f_pair), 1))
    own, turn = lax.optimization_barrier((jnp.concatenate([f_three, a_three]), turn))
    f_whole, a_whole, small = call(
        "join", join_body,
        [((F_ROWS, 128), BF16), ((A_ROWS, 128), BF16), ((16, 128), BF16)],
        [where, own, *to_peers([own] * 3, shift_second), turn], us=0, scalars=1,
    )
    small_r = swap(small)
    everywhere = ("ctx", "fsdp")
    f_send, a_send = after(f_whole, small_r), after(a_whole, small_r)
    f_got = to_peers([f_send] * 3, shift_first)
    a_two = lax.ppermute(a_send, everywhere, shift_y(2))
    a_one = lax.ppermute(a_send, everywhere, shift_apart(1))
    grad_tokens = call(
        "token_grad", token_grad_body, [((rows, D), F32)],
        [
            tok, gain_one, grad_after, dq_m, dq_o, dkv, back_one, back_two, w_query, query_other,
            wkv,
        ],
        us=2,
    )[0]

    shards = spread(where, [after(f_whole, grad_tokens)], (0,), [a_whole], ((0, 0),), [])
    a_other = lax.ppermute(after(a_send, f_got[0]), everywhere, shift_apart(-1))
    shards = spread(where, f_got[:1], (2,), [], (), shards)
    g_gate, g_up, g_down, g_query, g_key, g_value, g_out = spread(
        where, f_got[1:], (3, 1), [a_two, a_one, a_other], ((2, 0), (3, -2), (1, 2)), shards
    )
    g_gains = (after(small, g_key).astype(F32) + small_r.astype(F32))[:10].reshape(2, D)
    g_gains = jnp.where(even, g_gains[:, :half_d], g_gains[:, half_d:])
    return (
        out[None], grad_tokens[None], g_gains[0], g_query, g_key, g_value, g_out, g_gains[1],
        g_gate, g_up, g_down,
    )


def solution(mesh):
    tokens = P("fsdp", "ctx", None)
    columns, rows = P(None, "fsdp"), P("fsdp", None)
    in_specs = (
        tokens, P("fsdp", None), P("fsdp"), columns, columns, columns, rows, P("fsdp"), columns,
        columns, rows, tokens,
    )
    out_specs = (
        tokens, tokens, P("fsdp"), columns, columns, columns, rows, P("fsdp"), columns, columns,
        rows,
    )
    return jax.shard_map(local, mesh=mesh, in_specs=in_specs, out_specs=out_specs, check_vma=False)
```

```python
import functools

import jax
import jax.numpy as jnp
from jax import lax
from jax.experimental import pallas as pl
from jax.experimental.pallas import tpu as pltpu
from jax.sharding import PartitionSpec as P

D = 640
HEADS = 4
HEAD = 256
FF = 2048
WINDOW = 512
HALF = HEAD // 2
MINE = 2 * HEAD

epsilon = 1e-06
rope_base = 10000.0
neg_fill = -1e30
score_scale = HEAD ** (-0.5)
gelu_c = 0.7978845608028654
gelu_k = 0.044715

F32 = jnp.float32
BF16 = jnp.bfloat16
MIB = 1024 * 1024


def swap(x):
    return lax.ppermute(x, "fsdp", [(0, 1), (1, 0)])


def chip_pairs(move):
    pairs = []
    for x in range(4):
        for z in range(4):
            for y in range(4):
                for c in range(2):
                    tx, tz, ty = move(x, z, y, c)
                    target = (((tx % 4) * 4 + tz % 4) * 4 + ty % 4) * 2 + c
                    pairs.append((((x * 4 + z) * 4 + y) * 2 + c, target))
    return pairs


def shift_first(by):
    return chip_pairs(lambda x, z, y, c: (x + by, z, y) if c == 0 else (x, z + by, y))


def shift_second(by):
    return chip_pairs(lambda x, z, y, c: (x, z + by, y) if c == 0 else (x + by, z, y))


def shift_y(by):
    return chip_pairs(lambda x, z, y, c: (x, z, y + by))


def shift_apart(by):
    return chip_pairs(lambda x, z, y, c: (x, z, y + by - 2 * by * c))


def after(x, *done):
    return lax.optimization_barrier((x, *done))[0]


def pair_first(v):
    return v ^ 1


def pair_second(v):
    return 3 - v


def swap_y(v, step):
    return lax.ppermute(
        v, ("ctx", "fsdp"),
        chip_pairs(lambda x, z, y, c: (x, z, (pair_first, pair_second)[c ^ step](y))),
    )


def swap_first(v, step):
    pair = (pair_first, pair_second)[step]
    return lax.ppermute(
        v, ("ctx", "fsdp"),
        chip_pairs(lambda x, z, y, c: (pair(x), z, y) if c == 0 else (x, pair(z), y)),
    )


def to_peers(parts, shift):
    return [
        lax.ppermute(part, ("ctx", "fsdp"), shift(by)) for part, by in zip(parts, (2, 1, -1))
    ]


def passed_along(shard, by):
    peers = lax.axis_size("ctx")
    pairs = [(i, i + by) for i in range(peers) if 0 <= i + by < peers]
    return lax.ppermute(shard, "ctx", pairs)


def dot(a, b):
    return lax.dot_general(a, b, (((1,), (0,)), ((), ())), preferred_element_type=F32)


def dot_nt(a, b):
    return lax.dot_general(a, b, (((1,), (1,)), ((), ())), preferred_element_type=F32)


def dot_tn(a, b):
    return lax.dot_general(a, b, (((0,), (0,)), ((), ())), preferred_element_type=F32)


def call(name, body, outs, ins, us, scalars=0, scratch=(), extra=8):
    smem = pl.BlockSpec(memory_space=pltpu.SMEM)
    whole = pl.BlockSpec(memory_space=pltpu.VMEM)
    shapes = [jax.ShapeDtypeStruct(s, t) for s, t in outs]
    held = sum(x.size * x.dtype.itemsize for x in [*ins, *shapes])
    return pl.pallas_call(
        body,
        out_shape=shapes,
        in_specs=[smem] * scalars
        + [whole] * (len(ins) - scalars),
        out_specs=[whole] * len(outs),
        scratch_shapes=scratch,
        compiler_params=pltpu.CompilerParams(vmem_limit_bytes=held + extra * MIB),
        cost_estimate=pl.CostEstimate(
            flops=int(us * 1.1e9), bytes_accessed=1024, transcendentals=0
        ),
        name=name,
    )(*ins)


def inv_rms(x):
    return lax.rsqrt(jnp.mean(x * x, axis=-1, keepdims=True) + epsilon)


def rotate_pair(a, b, c, s):
    return a * c - b * s, b * c + a * s


def allowed_pairs(pos_row):
    keys = pos_row[...].astype(F32)
    own = jnp.broadcast_to(keys[:, 512:], (128, 256)).T[:, :1]
    distance = own - keys
    return (distance >= 0) & (distance < WINDOW)


def query_body(
    where, tok, gain, wq_m, wq_o, wk_m, wk_o, wv_m, wv_o, wo, cos, sin,
    normed, query, wkv, wide, wo_near,
):
    x = tok[...].astype(F32)
    wide[...] = x
    wo_near[...] = wo[...]
    n = (x * inv_rms(x) * gain[...]).astype(BF16)
    normed[...] = n
    c, s = cos[512:, :], sin[512:, :]
    for half, w in enumerate((wq_m, wq_o)):
        raw = dot(n, w[...])
        for head in range(2):
            a = raw[:, head * HEAD : head * HEAD + HALF]
            b = raw[:, head * HEAD + HALF : (head + 1) * HEAD]
            ra, rb = rotate_pair(a, b, c, s)
            at = half * MINE + head * HEAD
            query[:, at : at + HALF] = (ra * score_scale).astype(BF16)
            query[:, at + HALF : at + HEAD] = (rb * score_scale).astype(BF16)
    for which, (a, b, c, d) in enumerate(((wk_m, wk_o, wv_m, wv_o), (wk_o, wk_m, wv_o, wv_m))):

        @pl.when(where[0] == which)
        def _(parts=(a, b, c, d)):
            for i, part in enumerate(parts):
                wkv[:, i * HALF : (i + 1) * HALF] = part[...]


def attend_body(
    far_two, far_one, normed, wide, query, wkv, gain, wo_m, wo_o, gain_two, cos, sin, pos_row,
    normed_all, query_kept, kv, ctx_m, ctx_o, kept, after, normed_two,
):
    query_kept[...] = query[...]
    normed_all[512:, :] = normed[...]
    for i, far in enumerate((far_two, far_one)):
        x = far[...].astype(F32)
        normed_all[i * 256 : (i + 1) * 256, :] = (x * inv_rms(x) * gain[...]).astype(BF16)
    raw = dot(normed_all[...], wkv[...])
    ka, kb = rotate_pair(raw[:, :HALF], raw[:, HALF:HEAD], cos[...], sin[...])
    kv[:, :HALF] = ka.astype(BF16)
    kv[:, HALF:HEAD] = kb.astype(BF16)
    kv[:, HEAD:] = raw[:, HEAD:].astype(BF16)
    ok = allowed_pairs(pos_row)
    for head in range(HEADS):
        cols = slice(head * HEAD, (head + 1) * HEAD)
        scores = jnp.where(ok, dot_nt(query[:, cols], kv[:, :HEAD]), neg_fill)
        top = jnp.max(scores, axis=-1, keepdims=True)
        exps = jnp.exp(scores - top)
        total = jnp.sum(exps, axis=-1, keepdims=True)
        probs = exps * (1.0 / total)
        kept[head] = probs
        probs = probs.astype(BF16)
        context = (ctx_m, ctx_o)[head // 2]
        at = head % 2 * HEAD
        context[:, at : at + HEAD] = dot(probs, kv[:, HEAD:]).astype(BF16)
    h = wide[...] + (dot(ctx_m[...], wo_m[...]) + dot(ctx_o[...], wo_o[...]))
    after[...] = h
    normed_two[...] = (h * inv_rms(h) * gain_two[...]).astype(BF16)


FFN_STEP = 512


def ffn_half(n, y, wg, wu, wd, hid, dg, du):
    total = None
    grad_n = None
    for at in range(0, FF // 2, FFN_STEP):
        cols = slice(at, at + FFN_STEP)
        gate = dot(n, wg[:, cols])
        up = dot(n, wu[:, cols])
        grad_hidden = dot_nt(y, wd[cols, :])
        square = gate * gate
        t = jnp.tanh(gelu_c * gate * (1.0 + gelu_k * square))
        one_t = 0.5 + 0.5 * t
        act = gate * one_t
        slope = one_t + 0.5 * gate * (1.0 - t * t) * (gelu_c * (1.0 + 3.0 * gelu_k * square))
        hidden = (act * up).astype(BF16)
        grad_gate = (grad_hidden * up * slope).astype(BF16)
        grad_up = (grad_hidden * act).astype(BF16)
        hid[:, cols] = hidden
        dg[:, cols] = grad_gate
        du[:, cols] = grad_up
        part = dot(hidden, wd[cols, :])
        total = part if total is None else total + part
        part = dot_nt(grad_gate, wg[:, cols]) + dot_nt(grad_up, wu[:, cols])
        grad_n = part if grad_n is None else grad_n + part
    return total, grad_n


def ffn_other_body(normed_two, gy, wg, wu, wd, hid, dg, du, total, grad_n):
    total[...], grad_n[...] = ffn_half(normed_two[...], gy[...], wg, wu, wd, hid, dg, du)


def ffn_body(
    after, normed_two, gain_two, gy, wg, wu, wd, total_o, grad_n_o,
    out, hid, dg, du, grad_after, grad_after_low, grad_gain,
):
    y = gy[...]
    total, grad_n = ffn_half(normed_two[...], y, wg, wu, wd, hid, dg, du)
    grad_n = grad_n + grad_n_o[...]
    h = after[...]
    out[...] = (h + (total + total_o[...])).astype(BF16)
    r = inv_rms(h)
    dn = grad_n * gain_two[...]
    grad_gain[...] = jnp.sum(grad_n * h * r, axis=0, keepdims=True)
    ga = y.astype(F32) + r * dn - h * (r * r * r * jnp.mean(dn * h, axis=-1, keepdims=True))
    grad_after[...] = ga
    grad_after_low[...] = ga.astype(BF16)


ORDER = (0, 2, 1, 3)
F_ROWS = 3840
A_ROWS = 1664


def place(i, by):
    return lax.rem(i + by, 4)


def y_places(core, y):
    one = y + 1 - 2 * lax.rem(y, 2)
    other = 3 - y
    first = jnp.where(core == 0, one, other)
    second = jnp.where(core == 0, other, one)
    return y, second, first, 2 - y + 2 * lax.rem(y, 2)


def ffn_grads_body(
    where, hid_m, hid_r, dg_m, dg_r, du_m, du_r, n, n_r, gy, gy_r, out_0, out_1, out_2, out_3, turned
):
    first = where[1]
    turned[:, :256] = n[...].T
    turned[:, 256:] = n_r[...].T
    for out, by in zip((out_0, out_1, out_2, out_3), ORDER):
        j = place(first, by)
        cols = pl.ds(pl.multiple_of(j * 256, 256), 256)
        for at, left, right in ((0, dg_m, dg_r), (1280, du_m, du_r)):
            g = dot(turned[:, :256], left[:, cols]) + dot(turned[:, 256:], right[:, cols])
            out[at : at + 640, :] = g[:, :128].astype(BF16)
            out[at + 640 : at + 1280, :] = g[:, 128:].astype(BF16)
        g = dot_tn(hid_m[:, cols], gy[...]) + dot_tn(hid_r[:, cols], gy_r[...])
        for b in range(5):
            out[2560 + b * 256 : 2816 + b * 256, :] = g[:, b * 128 : (b + 1) * 128].astype(BF16)


def attend_grad_body(
    where, query, kv, kept, ga_low, wo_m, wo_o, cos, sin,
    dq_m, dq_o, dkv, back_two, back_one, dkv_m, packed,
):
    dkv_o = packed.at[512:, :]
    ga = ga_low[...]
    grad_k = None
    grad_v = None
    c, s = cos[512:, :], sin[512:, :]
    for half, wo, dq in ((1, wo_o, dq_o), (0, wo_m, dq_m)):
        grad_context = dot_nt(ga, wo[...]).astype(BF16)
        for head in range(2):
            cols = slice(half * MINE + head * HEAD, half * MINE + (head + 1) * HEAD)
            q = query[:, cols]
            gc = grad_context[:, head * HEAD : (head + 1) * HEAD]
            which = half * 2 + head
            probs = kept[which]
            part = dot_tn(probs.astype(BF16), gc)
            grad_v = part if grad_v is None else grad_v + part
            grad_probs = dot_nt(gc, kv[:, HEAD:])
            row_dot = jnp.sum(grad_probs * probs, axis=-1, keepdims=True)
            grad_scores = (probs * (grad_probs - row_dot)).astype(BF16)
            gq = dot(grad_scores, kv[:, :HEAD]) * score_scale
            a, b = rotate_pair(gq[:, :HALF], gq[:, HALF:], c, -s)
            dq[:, head * HEAD : head * HEAD + HALF] = a.astype(BF16)
            dq[:, head * HEAD + HALF : (head + 1) * HEAD] = b.astype(BF16)
            part = dot_tn(grad_scores, q)
            grad_k = part if grad_k is None else grad_k + part
    a, b = rotate_pair(grad_k[:, :HALF], grad_k[:, HALF:], cos[...], -sin[...])
    packed[:256, :] = dq_o[:, :HEAD]
    packed[256:512, :] = dq_o[:, HEAD:]
    for rows, out in ((0, back_two), (256, back_one), (512, dkv)):
        rows = slice(rows, rows + 256)
        out[:, :HALF] = a[rows, :].astype(BF16)
        out[:, HALF:HEAD] = b[rows, :].astype(BF16)
        out[:, HEAD:] = grad_v[rows, :].astype(BF16)
    even = where[0] == 0
    dkv_m[:, :HALF] = jnp.where(even, a, b).astype(BF16)
    dkv_o[:, :HALF] = jnp.where(even, b, a).astype(BF16)
    va, vb = grad_v[:, :HALF], grad_v[:, HALF:]
    dkv_m[:, HALF:] = jnp.where(even, va, vb).astype(BF16)
    dkv_o[:, HALF:] = jnp.where(even, vb, va).astype(BF16)


def attend_grads_body(
    where, n, n_r, dq_m, dkv_m, packed, ctx, ctx_r, ga, ga_r, wq, wk, wv,
    gain, gain_two_grad, out_0, out_1, out_2, out_3, turned,
):
    turned[:, :768] = n[...].T
    turned[:, 768:] = n_r[...].T
    gk = dot(turned[:, :768], dkv_m[...]) + dot(turned[:, 768:], packed[512:, :])
    weighed = gk[:, :HALF] * wk[...].astype(F32) + gk[:, HALF:] * wv[...].astype(F32)
    gk = gk.astype(BF16)
    for out, j in zip((out_0, out_1, out_2, out_3), y_places(where[0], where[3])):
        cols = pl.ds(pl.multiple_of(j * 128, 128), 128)
        rows = pl.ds(pl.multiple_of(j // 2 * 256, 256), 256)
        half = pl.ds(pl.multiple_of(j % 2 * 128, 128), 128)
        g = dot(turned[:, 512:768], dq_m[:, cols]) + dot(turned[:, 1280:], packed[rows, half])
        weighed = weighed + g * wq[:, cols].astype(F32)
        out[:640, :] = g.astype(BF16)
        g = dot_tn(ctx[:, cols], ga[...]) + dot_tn(ctx_r[:, cols], ga_r[...])
        for b in range(5):
            out[960 + b * 128 : 1088 + b * 128, :] = g[:, b * 128 : (b + 1) * 128].astype(BF16)
        for at in range(4):

            @pl.when(j == at)
            def _(out=out, at=at):
                out[640:800, :] = gk[at * 160 : (at + 1) * 160, :HALF]
                out[800:960, :] = gk[at * 160 : (at + 1) * 160, HALF:]

    by_row = jnp.broadcast_to(jnp.sum(weighed, axis=1, keepdims=True), (640, 128))
    one = by_row.T[:1, :] / gain[...]
    two = gain_two_grad[...]
    rows = [v[:, b * 128 : (b + 1) * 128] for v in (one, two) for b in range(5)]
    block = jnp.concatenate([*rows, jnp.zeros((6, 128), F32)], axis=0).astype(BF16)
    for out in (out_0, out_1, out_2, out_3):
        out[1600:1616, :] = block
        out[1616:, :] = jnp.zeros((48, 128), BF16)


def token_grad_body(
    where, tok, gain, grad_after, dq_m, dq_o, dkv, back_one, back_two, wq_m, wq_o, wkv, small,
    small_r, out, gain_one_out, gain_two_out,
):
    sums = small[...].astype(F32) + small_r[...].astype(F32)
    for at, target in ((0, gain_one_out), (5, gain_two_out)):
        whole = jnp.concatenate([sums[at + b : at + b + 1, :] for b in range(5)], axis=1)
        half = jnp.where(where[0] == 0, whole[:, : D // 2], whole[:, D // 2 :])
        target[...] = half.reshape(D // 2)
    back = back_one[...].astype(F32) + back_two[...].astype(F32)
    own = (dkv[...].astype(F32) + back).astype(BF16)
    gn = dot_nt(dq_m[...], wq_m[...]) + dot_nt(dq_o[...], wq_o[...]) + dot_nt(own, wkv[...])
    x = tok[...].astype(F32)
    r = inv_rms(x)
    dm = gn * gain[...]
    out[...] = grad_after[...] + r * dm - x * (
        r * r * r * jnp.mean(dm * x, axis=-1, keepdims=True)
    )


def add_low(*terms):
    total = terms[0].astype(F32)
    for term in terms[1:]:
        total = total + term.astype(F32)
    return total.astype(BF16)


F_PART, A_PART = F_ROWS // 4, A_ROWS // 4
PART = F_PART + A_PART


def split_sum_body(
    where, own, r_two, r_one, r_minus, a_own, a_one, a_last, out_0, out_1, out_2, out_3
):
    for out, by in zip((out_0, out_1, out_2, out_3), ORDER):
        j = place(where[2], by)
        at = pl.ds(pl.multiple_of(j * F_PART, F_PART), F_PART)
        total = (own[at, :].astype(F32) + r_two[at, :].astype(F32)) + (
            r_one[at, :].astype(F32) + r_minus[at, :].astype(F32)
        )
        out[:F_PART, :] = total.astype(BF16)
        at = pl.ds(pl.multiple_of(j * A_PART, A_PART), A_PART)
        total = a_own[at, :].astype(F32) + a_one[at, :].astype(F32) + a_last[at, :].astype(F32)
        out[F_PART:, :] = total.astype(BF16)


def sum_four(own, r_two, r_one, r_minus):
    total = (own.astype(F32) + r_two.astype(F32)) + (r_one.astype(F32) + r_minus.astype(F32))
    return total.astype(BF16)


def join_body(where, own, r_two, r_one, r_minus, _, f_out, a_out, small):
    for ref, by in ((own, 0), (r_two, 2), (r_one, 3), (r_minus, 1)):
        j = place(where[2], by)
        f_out[pl.ds(pl.multiple_of(j * F_PART, F_PART), F_PART), :] = ref[:F_PART, :]
        a_out[pl.ds(pl.multiple_of(j * A_PART, A_PART), A_PART), :] = ref[F_PART:, :]
    small[...] = a_out[1600:1616, :]


SHARDS = ((D, FF // 2), (D, FF // 2), (FF // 2, D), (D, MINE), (D, HALF), (D, HALF), (MINE, D))
F_WIDE = ((D, 256), (D, 256), (256, D))
A_WIDE = ((D, 128), (160, 128), (160, 128), (128, D))


def spread_body(f_places, a_places, fresh, where, *refs):
    f_count, a_count = len(f_places), len(a_places)
    f_pieces, a_pieces = refs[:f_count], refs[f_count : f_count + a_count]
    refs = refs[f_count + a_count + (0 if fresh else len(SHARDS)) :]
    gate, up, down, query, key, value, out = refs[:7]
    sems = refs[-1]
    f_wide, a_wide = refs[7:10], refs[10:14]
    copies = []

    def send(source, target):
        copies.append(pltpu.make_async_copy(source, target, sems.at[len(copies)]))
        copies[-1].start()

    for i, (piece, by) in enumerate(zip(f_pieces, f_places)):
        j = place(where[1], by)
        cols = pl.ds(pl.multiple_of(j * 256, 256), 256)
        for at, wide, target in ((0, f_wide[0], gate), (1280, f_wide[1], up)):
            for b in range(2):
                wide[i, :, b * 128 : (b + 1) * 128] = piece[
                    at + b * 640 : at + (b + 1) * 640, :
                ].astype(F32)
            send(wide.at[i], target.at[:, cols])
        for b in range(5):
            at = 2560 + b * 256
            f_wide[2][i, :, b * 128 : (b + 1) * 128] = piece[at : at + 256, :].astype(F32)
        send(f_wide[2].at[i], down.at[cols, :])
    for i, (piece, (by, apart)) in enumerate(zip(a_pieces, a_places)):
        j = place(where[3], by + apart * where[0])
        block = pl.ds(pl.multiple_of(j * 128, 128), 128)
        rows = pl.ds(pl.multiple_of(j * 160, 32), 160)
        a_wide[0][i] = piece[:640, :].astype(F32)
        send(a_wide[0].at[i], query.at[:, block])
        a_wide[1][i] = piece[640:800, :].astype(F32)
        send(a_wide[1].at[i], key.at[rows, :])
        a_wide[2][i] = piece[800:960, :].astype(F32)
        send(a_wide[2].at[i], value.at[rows, :])
        for b in range(5):
            at = 960 + b * 128
            a_wide[3][i, :, b * 128 : (b + 1) * 128] = piece[at : at + 128, :].astype(F32)
        send(a_wide[3].at[i], out.at[block, :])
    for copy in copies:
        copy.wait()


def spread(where, f_pieces, f_places, a_pieces, a_places, shards):
    f_count, a_count = len(f_pieces), len(a_pieces)
    anywhere = pl.BlockSpec(memory_space=pl.ANY)
    return pl.pallas_call(
        functools.partial(spread_body, f_places, a_places, not shards),
        out_shape=[jax.ShapeDtypeStruct(s, F32) for s in SHARDS],
        in_specs=[
            pl.BlockSpec(memory_space=pltpu.SMEM),
            *[pl.BlockSpec(memory_space=pltpu.VMEM)] * (f_count + a_count),
            *[anywhere] * len(shards),
        ],
        out_specs=[anywhere] * len(SHARDS),
        input_output_aliases={1 + f_count + a_count + i: i for i in range(len(shards))},
        scratch_shapes=[
            *[pltpu.VMEM((f_count, *s), F32) for s in F_WIDE],
            *[pltpu.VMEM((max(a_count, 1), *s), F32) for s in A_WIDE],
            pltpu.SemaphoreType.DMA((3 * f_count + 4 * a_count,)),
        ],
        compiler_params=pltpu.CompilerParams(vmem_limit_bytes=20 * MIB),
        cost_estimate=pl.CostEstimate(flops=1024, bytes_accessed=1024, transcendentals=0),
        name="spread",
    )(where, *f_pieces, *a_pieces, *shards)


def local(
    tokens, positions, gain_attn, w_query, w_key, w_value, w_out, gain_ffn, w_gate, w_up, w_down,
    grad_out,
):
    tok = tokens[0]
    gy = grad_out[0]
    rows = tok.shape[0]
    ctx = lax.axis_index("ctx")
    core = lax.axis_index("fsdp")
    x_at, z_at, y_at = ctx // 16, ctx // 4 % 4, ctx % 4
    where = jnp.stack(
        [core, jnp.where(core == 0, x_at, z_at), jnp.where(core == 0, z_at, x_at), y_at]
    ).astype(jnp.int32)
    even = core == 0

    far_one = passed_along(tok, 1)
    far_two = passed_along(tok, 2)
    gains = jnp.concatenate([gain_attn, gain_ffn]).reshape(1, D)
    gains_other = swap(gains)
    key_other, value_other = swap(w_key), swap(w_value)
    query_other = swap(after(w_query, gains_other))
    out_other = swap(after(w_out, key_other))

    low = jnp.where(even, gains, gains_other)
    high = jnp.where(even, gains_other, gains)
    half_d = D // 2
    gain_one = jnp.concatenate([low[:, :half_d], high[:, :half_d]], axis=1).astype(F32)
    gain_two = jnp.concatenate([low[:, half_d:], high[:, half_d:]], axis=1).astype(F32)
    seq_pos = positions[0]
    key_pos = lax.dynamic_slice_in_dim(
        jnp.concatenate([jnp.full((2 * rows,), -2 * WINDOW, jnp.int32), seq_pos]), ctx * rows,
        3 * rows,
    )
    pos_row = key_pos.reshape(1, 3 * rows)
    frequency = rope_base ** (-(jnp.arange(HALF, dtype=F32) * 2.0 / HEAD))
    angles = key_pos.astype(F32)[:, None] * frequency[None, :]
    cos, sin = jnp.cos(angles), jnp.sin(angles)

    gy_r = swap(after(gy, value_other))
    normed, query, wkv, wide, wo_near = call(
        "query", query_body,
        [
            ((rows, D), BF16), ((rows, HEADS * HEAD), BF16), ((D, 2 * HEAD), BF16),
            ((rows, D), F32), ((MINE, D), BF16),
        ],
        [
            where, after(tok, gain_two, pos_row), gain_one, w_query, query_other, w_key,
            key_other, w_value, value_other, w_out, cos, sin,
        ],
        us=6, scalars=1,
    )
    first = (normed, far_one, far_two, out_other, gy_r)
    gate_other = swap(after(w_gate, out_other, query_other))
    up_other = swap(after(w_up, *first))
    down_other = swap(after(w_down, *first))
    normed_all, query, kv, ctx_m, ctx_o, kept, after_attn, normed_two = call(
        "attend", attend_body,
        [
            ((3 * rows, D), BF16), ((rows, HEADS * HEAD), BF16), ((3 * rows, 2 * HEAD), BF16),
            ((rows, MINE), BF16), ((rows, MINE), BF16), ((HEADS, rows, 3 * rows), F32), ((rows, D), F32),
            ((rows, D), BF16),
        ],
        [
            far_two, far_one, normed, wide, query, wkv, after(gain_one, gate_other), wo_near,
            out_other, gain_two,
            cos, sin, pos_row,
        ],
        us=5,
    )
    half_ffn = [((rows, FF // 2), BF16)] * 3
    hid_o, dg_o, du_o, total_o, grad_n_o = call(
        "ffn_other", ffn_other_body, [*half_ffn, ((rows, D), F32), ((rows, D), F32)],
        [normed_two, gy, gate_other, up_other, down_other],
        us=5,
    )
    hid_r, dg_r, du_r = swap(hid_o), swap(dg_o), swap(du_o)
    normed_two_r, normed_r = swap(after(normed_two, hid_o)), swap(after(normed_all, hid_o))
    ctx_r = swap(after(ctx_o, hid_r))
    out, hid_m, dg_m, du_m, grad_after, ga_low, grad_gain_two = call(
        "ffn", ffn_body,
        [((rows, D), BF16), *half_ffn, ((rows, D), F32), ((rows, D), BF16), ((1, D), F32)],
        [after_attn, normed_two, gain_two, gy, w_gate, w_up, w_down, total_o, grad_n_o],
        us=4,
    )
    ga_r = swap(ga_low)
    dq_m, dq_o, dkv, back_two, back_one, dkv_m, packed = call(
        "attend_grad", attend_grad_body,
        [
            ((rows, MINE), BF16), ((rows, MINE), BF16), *[((rows, 2 * HEAD), BF16)] * 3,
            ((3 * rows, HEAD), BF16), ((5 * rows, HEAD), BF16),
        ],
        [
            where, query, kv, kept, ga_low, w_out, out_other, cos, sin,
        ],
        us=0, scalars=1,
    )
    packed_r = swap(packed)
    f_chunks = call(
        "ffn_grads", ffn_grads_body, [((F_ROWS, 128), BF16)] * 4,
        [where, after(hid_m, packed), hid_r, dg_m, dg_r, du_m, du_r, normed_two, normed_two_r, gy, gy_r],
        scalars=1, scratch=[pltpu.VMEM((D, 512), BF16)],
        us=3,
    )
    f_got = to_peers(f_chunks[1:], shift_first)

    a_chunks = call(
        "attend_grads", attend_grads_body, [((A_ROWS, 128), BF16)] * 4,
        [
            where, normed_all, normed_r, after(dq_m, f_chunks[0]), dkv_m, packed_r, ctx_m, ctx_r, ga_low, ga_r,
            w_query, w_key, w_value, gain_one, grad_gain_two,
        ],
        us=0, scalars=1, scratch=[pltpu.VMEM((D, 6 * rows), BF16)],
    )
    a_own, a_next, a_far_own, a_far_next = a_chunks
    a_next_r, a_own_r = swap_y(a_far_next, 0), swap_y(a_far_own, 0)
    a_last_r = swap_y(add_low(a_next, a_next_r), 1)
    parts = call(
        "split", split_sum_body, [((PART, 128), BF16)] * 4,
        [where, after(f_chunks[0], a_own), *f_got, a_own, a_own_r, a_last_r], us=0, scalars=1,
    )
    got = [parts[0], *to_peers(parts[1:], shift_second)]
    f_two = sum_four(*[part[:F_PART] for part in got])
    a_two = sum_four(*[part[F_PART:] for part in got])
    f_pair = add_low(f_two, swap_y(f_two, 0))
    a_pair = add_low(a_two, swap_first(a_two, 0))
    f_three = add_low(f_pair, swap_y(f_pair, 1))
    back_two = passed_along(after(back_two, f_two), -2)
    back_one = passed_along(after(back_one, f_two), -1)
    turn = swap(after(swap(after(grad_gain_two, back_one, back_two)), f_pair))
    a_three = add_low(a_pair, swap_first(after(a_pair, f_pair), 1))
    own, turn = lax.optimization_barrier((jnp.concatenate([f_three, a_three]), turn))
    f_whole, a_whole, small = call(
        "join", join_body,
        [((F_ROWS, 128), BF16), ((A_ROWS, 128), BF16), ((16, 128), BF16)],
        [where, own, *to_peers([own] * 3, shift_second), turn], us=0, scalars=1,
    )
    small_r = swap(small)
    everywhere = ("ctx", "fsdp")
    f_send, a_send = after(f_whole, small_r), after(a_whole, small_r)
    f_got = to_peers([f_send] * 3, shift_first)
    a_two = lax.ppermute(a_send, everywhere, shift_y(2))
    a_one = lax.ppermute(a_send, everywhere, shift_apart(1))
    grad_tokens, g_gain_one, g_gain_two = call(
        "token_grad", token_grad_body, [((rows, D), F32), ((half_d,), F32), ((half_d,), F32)],
        [
            where, tok, gain_one, grad_after, dq_m, dq_o, dkv, back_one, back_two, w_query,
            query_other, wkv, small, small_r,
        ],
        us=2, scalars=1,
    )

    shards = spread(where, [after(f_whole, grad_tokens)], (0,), [a_whole], ((0, 0),), [])
    a_other = lax.ppermute(after(a_send, f_got[0]), everywhere, shift_apart(-1))
    shards = spread(where, f_got[:1], (2,), [a_two], ((2, 0),), shards)
    g_gate, g_up, g_down, g_query, g_key, g_value, g_out = spread(
        where, f_got[1:], (3, 1), [a_one, a_other], ((3, -2), (1, 2)), shards
    )
    return (
        out[None], grad_tokens[None], g_gain_one, g_query, g_key, g_value, g_out, g_gain_two,
        g_gate, g_up, g_down,
    )


def solution(mesh):
    tokens = P("fsdp", "ctx", None)
    columns, rows = P(None, "fsdp"), P("fsdp", None)
    in_specs = (
        tokens, P("fsdp", None), P("fsdp"), columns, columns, columns, rows, P("fsdp"), columns,
        columns, rows, tokens,
    )
    out_specs = (
        tokens, tokens, P("fsdp"), columns, columns, columns, rows, P("fsdp"), columns, columns,
        rows,
    )
    return jax.shard_map(local, mesh=mesh, in_specs=in_specs, out_specs=out_specs, check_vma=False)
```

```python
import functools

import jax
import jax.numpy as jnp
from jax import lax
from jax.experimental import pallas as pl
from jax.experimental.pallas import tpu as pltpu
from jax.sharding import PartitionSpec as P

D = 640
HEADS = 4
HEAD = 256
FF = 2048
WINDOW = 512
HALF = HEAD // 2
MINE = 2 * HEAD

epsilon = 1e-06
rope_base = 10000.0
neg_fill = -1e30
score_scale = HEAD ** (-0.5)
gelu_c = 0.7978845608028654
gelu_k = 0.044715

F32 = jnp.float32
BF16 = jnp.bfloat16
MIB = 1024 * 1024


def swap(x):
    return lax.ppermute(x, "fsdp", [(0, 1), (1, 0)])


def chip_pairs(move):
    pairs = []
    for x in range(4):
        for z in range(4):
            for y in range(4):
                for c in range(2):
                    tx, tz, ty = move(x, z, y, c)
                    target = (((tx % 4) * 4 + tz % 4) * 4 + ty % 4) * 2 + c
                    pairs.append((((x * 4 + z) * 4 + y) * 2 + c, target))
    return pairs


def shift_first(by):
    return chip_pairs(lambda x, z, y, c: (x + by, z, y) if c == 0 else (x, z + by, y))


def shift_second(by):
    return chip_pairs(lambda x, z, y, c: (x, z + by, y) if c == 0 else (x + by, z, y))


def shift_y(by):
    return chip_pairs(lambda x, z, y, c: (x, z, y + by))


def shift_apart(by):
    return chip_pairs(lambda x, z, y, c: (x, z, y + by - 2 * by * c))


def after(x, *done):
    return lax.optimization_barrier((x, *done))[0]


def pair_first(v):
    return v ^ 1


def pair_second(v):
    return 3 - v


def swap_y(v, step):
    return lax.ppermute(
        v, ("ctx", "fsdp"),
        chip_pairs(lambda x, z, y, c: (x, z, (pair_first, pair_second)[c ^ step](y))),
    )


def swap_first(v, step):
    pair = (pair_first, pair_second)[step]
    return lax.ppermute(
        v, ("ctx", "fsdp"),
        chip_pairs(lambda x, z, y, c: (pair(x), z, y) if c == 0 else (x, pair(z), y)),
    )


def to_peers(parts, shift):
    return [
        lax.ppermute(part, ("ctx", "fsdp"), shift(by)) for part, by in zip(parts, (2, 1, -1))
    ]


def passed_along(shard, by):
    peers = lax.axis_size("ctx")
    pairs = [(i, i + by) for i in range(peers) if 0 <= i + by < peers]
    return lax.ppermute(shard, "ctx", pairs)


def dot(a, b):
    return lax.dot_general(a, b, (((1,), (0,)), ((), ())), preferred_element_type=F32)


def dot_nt(a, b):
    return lax.dot_general(a, b, (((1,), (1,)), ((), ())), preferred_element_type=F32)


def dot_tn(a, b):
    return lax.dot_general(a, b, (((0,), (0,)), ((), ())), preferred_element_type=F32)


def call(name, body, outs, ins, us, scalars=0, scratch=(), extra=8):
    smem = pl.BlockSpec(memory_space=pltpu.SMEM)
    whole = pl.BlockSpec(memory_space=pltpu.VMEM)
    shapes = [jax.ShapeDtypeStruct(s, t) for s, t in outs]
    held = sum(x.size * x.dtype.itemsize for x in [*ins, *shapes])
    return pl.pallas_call(
        body,
        out_shape=shapes,
        in_specs=[smem] * scalars
        + [whole] * (len(ins) - scalars),
        out_specs=[whole] * len(outs),
        scratch_shapes=scratch,
        compiler_params=pltpu.CompilerParams(vmem_limit_bytes=held + extra * MIB),
        cost_estimate=pl.CostEstimate(
            flops=int(us * 1.1e9), bytes_accessed=1024, transcendentals=0
        ),
        name=name,
    )(*ins)


def inv_rms(x):
    return lax.rsqrt(jnp.mean(x * x, axis=-1, keepdims=True) + epsilon)


def rotate_pair(a, b, c, s):
    return a * c - b * s, b * c + a * s


def allowed_pairs(pos_row):
    keys = pos_row[...].astype(F32)
    own = jnp.broadcast_to(keys[:, 512:], (128, 256)).T[:, :1]
    distance = own - keys
    return (distance >= 0) & (distance < WINDOW)


def query_body(
    where, tok, gain, wq_m, wq_o, wk_m, wk_o, wv_m, wv_o, wo, cos, sin,
    normed, query, wkv, wide, wo_near,
):
    x = tok[...].astype(F32)
    wide[...] = x
    wo_near[...] = wo[...]
    n = (x * inv_rms(x) * gain[...]).astype(BF16)
    normed[...] = n
    c, s = cos[512:, :], sin[512:, :]
    for half, w in enumerate((wq_m, wq_o)):
        raw = dot(n, w[...])
        for head in range(2):
            a = raw[:, head * HEAD : head * HEAD + HALF]
            b = raw[:, head * HEAD + HALF : (head + 1) * HEAD]
            ra, rb = rotate_pair(a, b, c, s)
            at = half * MINE + head * HEAD
            query[:, at : at + HALF] = (ra * score_scale).astype(BF16)
            query[:, at + HALF : at + HEAD] = (rb * score_scale).astype(BF16)
    for which, (a, b, c, d) in enumerate(((wk_m, wk_o, wv_m, wv_o), (wk_o, wk_m, wv_o, wv_m))):

        @pl.when(where[0] == which)
        def _(parts=(a, b, c, d)):
            for i, part in enumerate(parts):
                wkv[:, i * HALF : (i + 1) * HALF] = part[...]


def attend_body(
    far_two, far_one, normed, wide, query, wkv, gain, wo_m, wo_o, gain_two, cos, sin, pos_row,
    normed_all, query_kept, kv, ctx_m, ctx_o, kept, after, normed_two,
):
    query_kept[...] = query[...]
    normed_all[512:, :] = normed[...]
    for i, far in enumerate((far_two, far_one)):
        x = far[...].astype(F32)
        normed_all[i * 256 : (i + 1) * 256, :] = (x * inv_rms(x) * gain[...]).astype(BF16)
    raw = dot(normed_all[...], wkv[...])
    ka, kb = rotate_pair(raw[:, :HALF], raw[:, HALF:HEAD], cos[...], sin[...])
    kv[:, :HALF] = ka.astype(BF16)
    kv[:, HALF:HEAD] = kb.astype(BF16)
    kv[:, HEAD:] = raw[:, HEAD:].astype(BF16)
    ok = allowed_pairs(pos_row)
    for head in range(HEADS):
        cols = slice(head * HEAD, (head + 1) * HEAD)
        scores = jnp.where(ok, dot_nt(query[:, cols], kv[:, :HEAD]), neg_fill)
        top = jnp.max(scores, axis=-1, keepdims=True)
        exps = jnp.exp(scores - top)
        total = jnp.sum(exps, axis=-1, keepdims=True)
        probs = exps * (1.0 / total)
        kept[head] = probs
        probs = probs.astype(BF16)
        context = (ctx_m, ctx_o)[head // 2]
        at = head % 2 * HEAD
        context[:, at : at + HEAD] = dot(probs, kv[:, HEAD:]).astype(BF16)
    h = wide[...] + (dot(ctx_m[...], wo_m[...]) + dot(ctx_o[...], wo_o[...]))
    after[...] = h
    normed_two[...] = (h * inv_rms(h) * gain_two[...]).astype(BF16)


FFN_STEP = 1024


def ffn_half(n, y, wg, wu, wd, hid, dg, du):
    total = None
    grad_n = None
    for at in range(0, FF // 2, FFN_STEP):
        cols = slice(at, at + FFN_STEP)
        gate = dot(n, wg[:, cols])
        up = dot(n, wu[:, cols])
        grad_hidden = dot_nt(y, wd[cols, :])
        square = gate * gate
        t = jnp.tanh(gelu_c * gate * (1.0 + gelu_k * square))
        one_t = 0.5 + 0.5 * t
        act = gate * one_t
        slope = one_t + 0.5 * gate * (1.0 - t * t) * (gelu_c * (1.0 + 3.0 * gelu_k * square))
        hidden = (act * up).astype(BF16)
        grad_gate = (grad_hidden * up * slope).astype(BF16)
        grad_up = (grad_hidden * act).astype(BF16)
        hid[:, cols] = hidden
        dg[:, cols] = grad_gate
        du[:, cols] = grad_up
        part = dot(hidden, wd[cols, :])
        total = part if total is None else total + part
        part = dot_nt(grad_gate, wg[:, cols]) + dot_nt(grad_up, wu[:, cols])
        grad_n = part if grad_n is None else grad_n + part
    return total, grad_n


def ffn_other_body(normed_two, gy, wg, wu, wd, hid, dg, du, total, grad_n):
    total[...], grad_n[...] = ffn_half(normed_two[...], gy[...], wg, wu, wd, hid, dg, du)


def ffn_body(
    after, normed_two, gain_two, gy, wg, wu, wd, total_o, grad_n_o,
    out, hid, dg, du, grad_after, grad_after_low, grad_gain,
):
    y = gy[...]
    total, grad_n = ffn_half(normed_two[...], y, wg, wu, wd, hid, dg, du)
    grad_n = grad_n + grad_n_o[...]
    h = after[...]
    out[...] = (h + (total + total_o[...])).astype(BF16)
    r = inv_rms(h)
    dn = grad_n * gain_two[...]
    grad_gain[...] = jnp.sum(grad_n * h * r, axis=0, keepdims=True)
    ga = y.astype(F32) + r * dn - h * (r * r * r * jnp.mean(dn * h, axis=-1, keepdims=True))
    grad_after[...] = ga
    grad_after_low[...] = ga.astype(BF16)


ORDER = (0, 2, 1, 3)
F_ROWS = 3840
A_ROWS = 1664


def place(i, by):
    return lax.rem(i + by, 4)


def y_places(core, y):
    one = y + 1 - 2 * lax.rem(y, 2)
    other = 3 - y
    first = jnp.where(core == 0, one, other)
    second = jnp.where(core == 0, other, one)
    return y, second, first, 2 - y + 2 * lax.rem(y, 2)


def ffn_grads_body(
    where, hid_m, hid_r, dg_m, dg_r, du_m, du_r, n, n_r, gy, gy_r, out_0, out_1, out_2, out_3, turned
):
    first = where[1]
    turned[:, :256] = n[...].T
    turned[:, 256:] = n_r[...].T
    for out, by in zip((out_0, out_1, out_2, out_3), ORDER):
        j = place(first, by)
        cols = pl.ds(pl.multiple_of(j * 256, 256), 256)
        for at, left, right in ((0, dg_m, dg_r), (1280, du_m, du_r)):
            g = dot(turned[:, :256], left[:, cols]) + dot(turned[:, 256:], right[:, cols])
            out[at : at + 640, :] = g[:, :128].astype(BF16)
            out[at + 640 : at + 1280, :] = g[:, 128:].astype(BF16)
        g = dot_tn(hid_m[:, cols], gy[...]) + dot_tn(hid_r[:, cols], gy_r[...])
        for b in range(5):
            out[2560 + b * 256 : 2816 + b * 256, :] = g[:, b * 128 : (b + 1) * 128].astype(BF16)


def attend_grad_body(
    where, query, kv, kept, ga_low, wo_m, wo_o, cos, sin,
    dq_m, dq_o, dkv, back_two, back_one, dkv_m, packed,
):
    dkv_o = packed.at[512:, :]
    ga = ga_low[...]
    grad_k = None
    grad_v = None
    c, s = cos[512:, :], sin[512:, :]
    for half, wo, dq in ((1, wo_o, dq_o), (0, wo_m, dq_m)):
        grad_context = dot_nt(ga, wo[...]).astype(BF16)
        for head in range(2):
            cols = slice(half * MINE + head * HEAD, half * MINE + (head + 1) * HEAD)
            q = query[:, cols]
            gc = grad_context[:, head * HEAD : (head + 1) * HEAD]
            which = half * 2 + head
            probs = kept[which]
            part = dot_tn(probs.astype(BF16), gc)
            grad_v = part if grad_v is None else grad_v + part
            grad_probs = dot_nt(gc, kv[:, HEAD:])
            row_dot = jnp.sum(grad_probs * probs, axis=-1, keepdims=True)
            grad_scores = (probs * (grad_probs - row_dot)).astype(BF16)
            gq = dot(grad_scores, kv[:, :HEAD]) * score_scale
            a, b = rotate_pair(gq[:, :HALF], gq[:, HALF:], c, -s)
            dq[:, head * HEAD : head * HEAD + HALF] = a.astype(BF16)
            dq[:, head * HEAD + HALF : (head + 1) * HEAD] = b.astype(BF16)
            part = dot_tn(grad_scores, q)
            grad_k = part if grad_k is None else grad_k + part
    a, b = rotate_pair(grad_k[:, :HALF], grad_k[:, HALF:], cos[...], -sin[...])
    packed[:256, :] = dq_o[:, :HEAD]
    packed[256:512, :] = dq_o[:, HEAD:]
    for rows, out in ((0, back_two), (256, back_one), (512, dkv)):
        rows = slice(rows, rows + 256)
        out[:, :HALF] = a[rows, :].astype(BF16)
        out[:, HALF:HEAD] = b[rows, :].astype(BF16)
        out[:, HEAD:] = grad_v[rows, :].astype(BF16)
    even = where[0] == 0
    dkv_m[:, :HALF] = jnp.where(even, a, b).astype(BF16)
    dkv_o[:, :HALF] = jnp.where(even, b, a).astype(BF16)
    va, vb = grad_v[:, :HALF], grad_v[:, HALF:]
    dkv_m[:, HALF:] = jnp.where(even, va, vb).astype(BF16)
    dkv_o[:, HALF:] = jnp.where(even, vb, va).astype(BF16)


def attend_grads_body(
    where, n, n_r, dq_m, dkv_m, packed, ctx, ctx_r, ga, ga_r, wq, wk, wv,
    gain, gain_two_grad, out_0, out_1, out_2, out_3, turned,
):
    turned[:, :768] = n[...].T
    turned[:, 768:] = n_r[...].T
    gk = dot(turned[:, :768], dkv_m[...]) + dot(turned[:, 768:], packed[512:, :])
    weighed = gk[:, :HALF] * wk[...].astype(F32) + gk[:, HALF:] * wv[...].astype(F32)
    gk = gk.astype(BF16)
    for out, j in zip((out_0, out_1, out_2, out_3), y_places(where[0], where[3])):
        cols = pl.ds(pl.multiple_of(j * 128, 128), 128)
        rows = pl.ds(pl.multiple_of(j // 2 * 256, 256), 256)
        half = pl.ds(pl.multiple_of(j % 2 * 128, 128), 128)
        g = dot(turned[:, 512:768], dq_m[:, cols]) + dot(turned[:, 1280:], packed[rows, half])
        weighed = weighed + g * wq[:, cols].astype(F32)
        out[:640, :] = g.astype(BF16)
        g = dot_tn(ctx[:, cols], ga[...]) + dot_tn(ctx_r[:, cols], ga_r[...])
        for b in range(5):
            out[960 + b * 128 : 1088 + b * 128, :] = g[:, b * 128 : (b + 1) * 128].astype(BF16)
        for at in range(4):

            @pl.when(j == at)
            def _(out=out, at=at):
                out[640:800, :] = gk[at * 160 : (at + 1) * 160, :HALF]
                out[800:960, :] = gk[at * 160 : (at + 1) * 160, HALF:]

    by_row = jnp.broadcast_to(jnp.sum(weighed, axis=1, keepdims=True), (640, 128))
    one = by_row.T[:1, :] / gain[...]
    two = gain_two_grad[...]
    rows = [v[:, b * 128 : (b + 1) * 128] for v in (one, two) for b in range(5)]
    block = jnp.concatenate([*rows, jnp.zeros((6, 128), F32)], axis=0).astype(BF16)
    for out in (out_0, out_1, out_2, out_3):
        out[1600:1616, :] = block
        out[1616:, :] = jnp.zeros((48, 128), BF16)


def token_grad_body(
    where, tok, gain, grad_after, dq_m, dq_o, dkv, back_one, back_two, wq_m, wq_o, wkv, small,
    small_r, out, gain_one_out, gain_two_out,
):
    sums = small[...].astype(F32) + small_r[...].astype(F32)
    for at, target in ((0, gain_one_out), (5, gain_two_out)):
        whole = jnp.concatenate([sums[at + b : at + b + 1, :] for b in range(5)], axis=1)
        half = jnp.where(where[0] == 0, whole[:, : D // 2], whole[:, D // 2 :])
        target[...] = half.reshape(D // 2)
    back = back_one[...].astype(F32) + back_two[...].astype(F32)
    own = (dkv[...].astype(F32) + back).astype(BF16)
    gn = dot_nt(dq_m[...], wq_m[...]) + dot_nt(dq_o[...], wq_o[...]) + dot_nt(own, wkv[...])
    x = tok[...].astype(F32)
    r = inv_rms(x)
    dm = gn * gain[...]
    out[...] = grad_after[...] + r * dm - x * (
        r * r * r * jnp.mean(dm * x, axis=-1, keepdims=True)
    )


def add_low(*terms):
    total = terms[0].astype(F32)
    for term in terms[1:]:
        total = total + term.astype(F32)
    return total.astype(BF16)


F_PART, A_PART = F_ROWS // 4, A_ROWS // 4
PART = F_PART + A_PART


def split_sum_body(
    where, own, r_two, r_one, r_minus, a_own, a_one, a_last, out_0, out_1, out_2, out_3
):
    for out, by in zip((out_0, out_1, out_2, out_3), ORDER):
        j = place(where[2], by)
        at = pl.ds(pl.multiple_of(j * F_PART, F_PART), F_PART)
        total = (own[at, :].astype(F32) + r_two[at, :].astype(F32)) + (
            r_one[at, :].astype(F32) + r_minus[at, :].astype(F32)
        )
        out[:F_PART, :] = total.astype(BF16)
        at = pl.ds(pl.multiple_of(j * A_PART, A_PART), A_PART)
        total = a_own[at, :].astype(F32) + a_one[at, :].astype(F32) + a_last[at, :].astype(F32)
        out[F_PART:, :] = total.astype(BF16)


def sum_four(own, r_two, r_one, r_minus):
    total = (own.astype(F32) + r_two.astype(F32)) + (r_one.astype(F32) + r_minus.astype(F32))
    return total.astype(BF16)


def join_body(where, own, r_two, r_one, r_minus, _, f_out, a_out, small):
    for ref, by in ((own, 0), (r_two, 2), (r_one, 3), (r_minus, 1)):
        j = place(where[2], by)
        f_out[pl.ds(pl.multiple_of(j * F_PART, F_PART), F_PART), :] = ref[:F_PART, :]
        a_out[pl.ds(pl.multiple_of(j * A_PART, A_PART), A_PART), :] = ref[F_PART:, :]
    small[...] = a_out[1600:1616, :]


SHARDS = ((D, FF // 2), (D, FF // 2), (FF // 2, D), (D, MINE), (D, HALF), (D, HALF), (MINE, D))
F_WIDE = ((D, 256), (D, 256), (256, D))
A_WIDE = ((D, 128), (160, 128), (160, 128), (128, D))


def spread_body(f_places, a_places, fresh, where, *refs):
    f_count, a_count = len(f_places), len(a_places)
    f_pieces, a_pieces = refs[:f_count], refs[f_count : f_count + a_count]
    refs = refs[f_count + a_count + (0 if fresh else len(SHARDS)) :]
    gate, up, down, query, key, value, out = refs[:7]
    sems = refs[-1]
    f_wide, a_wide = refs[7:10], refs[10:14]
    copies = []

    def send(source, target):
        copies.append(pltpu.make_async_copy(source, target, sems.at[len(copies)]))
        copies[-1].start()

    for i, (piece, by) in enumerate(zip(f_pieces, f_places)):
        j = place(where[1], by)
        cols = pl.ds(pl.multiple_of(j * 256, 256), 256)
        for at, wide, target in ((0, f_wide[0], gate), (1280, f_wide[1], up)):
            for b in range(2):
                wide[i, :, b * 128 : (b + 1) * 128] = piece[
                    at + b * 640 : at + (b + 1) * 640, :
                ].astype(F32)
            send(wide.at[i], target.at[:, cols])
        for b in range(5):
            at = 2560 + b * 256
            f_wide[2][i, :, b * 128 : (b + 1) * 128] = piece[at : at + 256, :].astype(F32)
        send(f_wide[2].at[i], down.at[cols, :])
    for i, (piece, (by, apart)) in enumerate(zip(a_pieces, a_places)):
        j = place(where[3], by + apart * where[0])
        block = pl.ds(pl.multiple_of(j * 128, 128), 128)
        rows = pl.ds(pl.multiple_of(j * 160, 32), 160)
        a_wide[0][i] = piece[:640, :].astype(F32)
        send(a_wide[0].at[i], query.at[:, block])
        a_wide[1][i] = piece[640:800, :].astype(F32)
        send(a_wide[1].at[i], key.at[rows, :])
        a_wide[2][i] = piece[800:960, :].astype(F32)
        send(a_wide[2].at[i], value.at[rows, :])
        for b in range(5):
            at = 960 + b * 128
            a_wide[3][i, :, b * 128 : (b + 1) * 128] = piece[at : at + 128, :].astype(F32)
        send(a_wide[3].at[i], out.at[block, :])
    for copy in copies:
        copy.wait()


def spread(where, f_pieces, f_places, a_pieces, a_places, shards):
    f_count, a_count = len(f_pieces), len(a_pieces)
    anywhere = pl.BlockSpec(memory_space=pl.ANY)
    return pl.pallas_call(
        functools.partial(spread_body, f_places, a_places, not shards),
        out_shape=[jax.ShapeDtypeStruct(s, F32) for s in SHARDS],
        in_specs=[
            pl.BlockSpec(memory_space=pltpu.SMEM),
            *[pl.BlockSpec(memory_space=pltpu.VMEM)] * (f_count + a_count),
            *[anywhere] * len(shards),
        ],
        out_specs=[anywhere] * len(SHARDS),
        input_output_aliases={1 + f_count + a_count + i: i for i in range(len(shards))},
        scratch_shapes=[
            *[pltpu.VMEM((f_count, *s), F32) for s in F_WIDE],
            *[pltpu.VMEM((max(a_count, 1), *s), F32) for s in A_WIDE],
            pltpu.SemaphoreType.DMA((3 * f_count + 4 * a_count,)),
        ],
        compiler_params=pltpu.CompilerParams(vmem_limit_bytes=20 * MIB),
        cost_estimate=pl.CostEstimate(flops=1024, bytes_accessed=1024, transcendentals=0),
        name="spread",
    )(where, *f_pieces, *a_pieces, *shards)


def local(
    tokens, positions, gain_attn, w_query, w_key, w_value, w_out, gain_ffn, w_gate, w_up, w_down,
    grad_out,
):
    tok = tokens[0]
    gy = grad_out[0]
    rows = tok.shape[0]
    ctx = lax.axis_index("ctx")
    core = lax.axis_index("fsdp")
    x_at, z_at, y_at = ctx // 16, ctx // 4 % 4, ctx % 4
    where = jnp.stack(
        [core, jnp.where(core == 0, x_at, z_at), jnp.where(core == 0, z_at, x_at), y_at]
    ).astype(jnp.int32)
    even = core == 0

    far_one = passed_along(tok, 1)
    far_two = passed_along(tok, 2)
    gains = jnp.concatenate([gain_attn, gain_ffn]).reshape(1, D)
    gains_other = swap(gains)
    key_other, value_other = swap(w_key), swap(w_value)
    query_other = swap(after(w_query, gains_other))
    out_other = swap(after(w_out, key_other))

    low = jnp.where(even, gains, gains_other)
    high = jnp.where(even, gains_other, gains)
    half_d = D // 2
    gain_one = jnp.concatenate([low[:, :half_d], high[:, :half_d]], axis=1).astype(F32)
    gain_two = jnp.concatenate([low[:, half_d:], high[:, half_d:]], axis=1).astype(F32)
    seq_pos = positions[0]
    key_pos = lax.dynamic_slice_in_dim(
        jnp.concatenate([jnp.full((2 * rows,), -2 * WINDOW, jnp.int32), seq_pos]), ctx * rows,
        3 * rows,
    )
    pos_row = key_pos.reshape(1, 3 * rows)
    frequency = rope_base ** (-(jnp.arange(HALF, dtype=F32) * 2.0 / HEAD))
    angles = key_pos.astype(F32)[:, None] * frequency[None, :]
    cos, sin = jnp.cos(angles), jnp.sin(angles)

    gy_r = swap(after(gy, value_other))
    normed, query, wkv, wide, wo_near = call(
        "query", query_body,
        [
            ((rows, D), BF16), ((rows, HEADS * HEAD), BF16), ((D, 2 * HEAD), BF16),
            ((rows, D), F32), ((MINE, D), BF16),
        ],
        [
            where, after(tok, gain_two, pos_row), gain_one, w_query, query_other, w_key,
            key_other, w_value, value_other, w_out, cos, sin,
        ],
        us=6, scalars=1,
    )
    first = (normed, far_one, far_two, out_other, gy_r)
    gate_other = swap(after(w_gate, out_other, query_other))
    up_other = swap(after(w_up, *first))
    down_other = swap(after(w_down, *first))
    normed_all, query, kv, ctx_m, ctx_o, kept, after_attn, normed_two = call(
        "attend", attend_body,
        [
            ((3 * rows, D), BF16), ((rows, HEADS * HEAD), BF16), ((3 * rows, 2 * HEAD), BF16),
            ((rows, MINE), BF16), ((rows, MINE), BF16), ((HEADS, rows, 3 * rows), F32), ((rows, D), F32),
            ((rows, D), BF16),
        ],
        [
            far_two, far_one, normed, wide, query, wkv, after(gain_one, gate_other), wo_near,
            out_other, gain_two,
            cos, sin, pos_row,
        ],
        us=5,
    )
    half_ffn = [((rows, FF // 2), BF16)] * 3
    hid_o, dg_o, du_o, total_o, grad_n_o = call(
        "ffn_other", ffn_other_body, [*half_ffn, ((rows, D), F32), ((rows, D), F32)],
        [normed_two, gy, gate_other, up_other, down_other],
        us=5,
    )
    hid_r, dg_r, du_r = swap(hid_o), swap(dg_o), swap(du_o)
    normed_two_r, normed_r = swap(after(normed_two, hid_o)), swap(after(normed_all, hid_o))
    ctx_r = swap(after(ctx_o, hid_r))
    out, hid_m, dg_m, du_m, grad_after, ga_low, grad_gain_two = call(
        "ffn", ffn_body,
        [((rows, D), BF16), *half_ffn, ((rows, D), F32), ((rows, D), BF16), ((1, D), F32)],
        [after_attn, normed_two, gain_two, gy, w_gate, w_up, w_down, total_o, grad_n_o],
        us=4,
    )
    ga_r = swap(ga_low)
    dq_m, dq_o, dkv, back_two, back_one, dkv_m, packed = call(
        "attend_grad", attend_grad_body,
        [
            ((rows, MINE), BF16), ((rows, MINE), BF16), *[((rows, 2 * HEAD), BF16)] * 3,
            ((3 * rows, HEAD), BF16), ((5 * rows, HEAD), BF16),
        ],
        [
            where, query, kv, kept, ga_low, w_out, out_other, cos, sin,
        ],
        us=0, scalars=1,
    )
    packed_r = swap(packed)
    f_chunks = call(
        "ffn_grads", ffn_grads_body, [((F_ROWS, 128), BF16)] * 4,
        [where, after(hid_m, packed), hid_r, dg_m, dg_r, du_m, du_r, normed_two, normed_two_r, gy, gy_r],
        scalars=1, scratch=[pltpu.VMEM((D, 512), BF16)],
        us=3,
    )
    f_got = to_peers(f_chunks[1:], shift_first)

    a_chunks = call(
        "attend_grads", attend_grads_body, [((A_ROWS, 128), BF16)] * 4,
        [
            where, normed_all, normed_r, after(dq_m, f_chunks[0]), dkv_m, packed_r, ctx_m, ctx_r, ga_low, ga_r,
            w_query, w_key, w_value, gain_one, grad_gain_two,
        ],
        us=0, scalars=1, scratch=[pltpu.VMEM((D, 6 * rows), BF16)],
    )
    a_own, a_next, a_far_own, a_far_next = a_chunks
    a_next_r, a_own_r = swap_y(a_far_next, 0), swap_y(a_far_own, 0)
    a_last_r = swap_y(add_low(a_next, a_next_r), 1)
    parts = call(
        "split", split_sum_body, [((PART, 128), BF16)] * 4,
        [where, after(f_chunks[0], a_own), *f_got, a_own, a_own_r, a_last_r], us=0, scalars=1,
    )
    got = [parts[0], *to_peers(parts[1:], shift_second)]
    f_two = sum_four(*[part[:F_PART] for part in got])
    a_two = sum_four(*[part[F_PART:] for part in got])
    f_pair = add_low(f_two, swap_y(f_two, 0))
    a_pair = add_low(a_two, swap_first(a_two, 0))
    f_three = add_low(f_pair, swap_y(f_pair, 1))
    back_two = passed_along(after(back_two, f_two), -2)
    back_one = passed_along(after(back_one, f_two), -1)
    turn = swap(after(swap(after(grad_gain_two, back_one, back_two)), f_pair))
    a_three = add_low(a_pair, swap_first(after(a_pair, f_pair), 1))
    own, turn = lax.optimization_barrier((jnp.concatenate([f_three, a_three]), turn))
    f_whole, a_whole, small = call(
        "join", join_body,
        [((F_ROWS, 128), BF16), ((A_ROWS, 128), BF16), ((16, 128), BF16)],
        [where, own, *to_peers([own] * 3, shift_second), turn], us=0, scalars=1,
    )
    small_r = swap(small)
    everywhere = ("ctx", "fsdp")
    f_send, a_send = after(f_whole, small_r), after(a_whole, small_r)
    f_got = to_peers([f_send] * 3, shift_first)
    a_two = lax.ppermute(a_send, everywhere, shift_y(2))
    a_one = lax.ppermute(a_send, everywhere, shift_apart(1))
    grad_tokens, g_gain_one, g_gain_two = call(
        "token_grad", token_grad_body, [((rows, D), F32), ((half_d,), F32), ((half_d,), F32)],
        [
            where, tok, gain_one, grad_after, dq_m, dq_o, dkv, back_one, back_two, w_query,
            query_other, wkv, small, small_r,
        ],
        us=2, scalars=1,
    )

    shards = spread(where, [after(f_whole, grad_tokens)], (0,), [a_whole], ((0, 0),), [])
    a_other = lax.ppermute(after(a_send, f_got[0]), everywhere, shift_apart(-1))
    shards = spread(where, f_got[:1], (2,), [a_two], ((2, 0),), shards)
    g_gate, g_up, g_down, g_query, g_key, g_value, g_out = spread(
        where, f_got[1:], (3, 1), [a_one, a_other], ((3, -2), (1, 2)), shards
    )
    return (
        out[None], grad_tokens[None], g_gain_one, g_query, g_key, g_value, g_out, g_gain_two,
        g_gate, g_up, g_down,
    )


def solution(mesh):
    tokens = P("fsdp", "ctx", None)
    columns, rows = P(None, "fsdp"), P("fsdp", None)
    in_specs = (
        tokens, P("fsdp", None), P("fsdp"), columns, columns, columns, rows, P("fsdp"), columns,
        columns, rows, tokens,
    )
    out_specs = (
        tokens, tokens, P("fsdp"), columns, columns, columns, rows, P("fsdp"), columns, columns,
        rows,
    )
    return jax.shard_map(local, mesh=mesh, in_specs=in_specs, out_specs=out_specs, check_vma=False)
```

```python
import functools

import jax
import jax.numpy as jnp
from jax import lax
from jax.experimental import pallas as pl
from jax.experimental.pallas import tpu as pltpu
from jax.sharding import PartitionSpec as P

D = 640
HEADS = 4
HEAD = 256
FF = 2048
WINDOW = 512
HALF = HEAD // 2
MINE = 2 * HEAD

epsilon = 1e-06
rope_base = 10000.0
neg_fill = -1e30
score_scale = HEAD ** (-0.5)
gelu_c = 0.7978845608028654
gelu_k = 0.044715

F32 = jnp.float32
BF16 = jnp.bfloat16
MIB = 1024 * 1024


def swap(x):
    return lax.ppermute(x, "fsdp", [(0, 1), (1, 0)])


def chip_pairs(move):
    pairs = []
    for x in range(4):
        for z in range(4):
            for y in range(4):
                for c in range(2):
                    tx, tz, ty = move(x, z, y, c)
                    target = (((tx % 4) * 4 + tz % 4) * 4 + ty % 4) * 2 + c
                    pairs.append((((x * 4 + z) * 4 + y) * 2 + c, target))
    return pairs


def shift_first(by):
    return chip_pairs(lambda x, z, y, c: (x + by, z, y) if c == 0 else (x, z + by, y))


def shift_second(by):
    return chip_pairs(lambda x, z, y, c: (x, z + by, y) if c == 0 else (x + by, z, y))


def shift_y(by):
    return chip_pairs(lambda x, z, y, c: (x, z, y + by))


def shift_apart(by):
    return chip_pairs(lambda x, z, y, c: (x, z, y + by - 2 * by * c))


def after(x, *done):
    return lax.optimization_barrier((x, *done))[0]


def pair_first(v):
    return v ^ 1


def pair_second(v):
    return 3 - v


def swap_y(v, step):
    return lax.ppermute(
        v, ("ctx", "fsdp"),
        chip_pairs(lambda x, z, y, c: (x, z, (pair_first, pair_second)[c ^ step](y))),
    )


def swap_first(v, step):
    pair = (pair_first, pair_second)[step]
    return lax.ppermute(
        v, ("ctx", "fsdp"),
        chip_pairs(lambda x, z, y, c: (pair(x), z, y) if c == 0 else (x, pair(z), y)),
    )


def to_peers(parts, shift):
    return [
        lax.ppermute(part, ("ctx", "fsdp"), shift(by)) for part, by in zip(parts, (2, 1, -1))
    ]


def passed_along(shard, by):
    peers = lax.axis_size("ctx")
    pairs = [(i, i + by) for i in range(peers) if 0 <= i + by < peers]
    return lax.ppermute(shard, "ctx", pairs)


def dot(a, b):
    return lax.dot_general(a, b, (((1,), (0,)), ((), ())), preferred_element_type=F32)


def dot_nt(a, b):
    return lax.dot_general(a, b, (((1,), (1,)), ((), ())), preferred_element_type=F32)


def dot_tn(a, b):
    return lax.dot_general(a, b, (((0,), (0,)), ((), ())), preferred_element_type=F32)


def call(name, body, outs, ins, us, scalars=0, scratch=(), extra=8):
    smem = pl.BlockSpec(memory_space=pltpu.SMEM)
    whole = pl.BlockSpec(memory_space=pltpu.VMEM)
    shapes = [jax.ShapeDtypeStruct(s, t) for s, t in outs]
    held = sum(x.size * x.dtype.itemsize for x in [*ins, *shapes])
    return pl.pallas_call(
        body,
        out_shape=shapes,
        in_specs=[smem] * scalars
        + [whole] * (len(ins) - scalars),
        out_specs=[whole] * len(outs),
        scratch_shapes=scratch,
        compiler_params=pltpu.CompilerParams(vmem_limit_bytes=held + extra * MIB),
        cost_estimate=pl.CostEstimate(
            flops=int(us * 1.1e9), bytes_accessed=1024, transcendentals=0
        ),
        name=name,
    )(*ins)


def inv_rms(x):
    return lax.rsqrt(jnp.mean(x * x, axis=-1, keepdims=True) + epsilon)


def rotate_pair(a, b, c, s):
    return a * c - b * s, b * c + a * s


def allowed_pairs(pos_row):
    keys = pos_row[...].astype(F32)
    own = jnp.broadcast_to(keys[:, 512:], (128, 256)).T[:, :1]
    distance = own - keys
    return (distance >= 0) & (distance < WINDOW)


def query_body(
    where, tok, gain, wq_m, wq_o, wk_m, wk_o, wv_m, wv_o, wo, cos, sin,
    normed, query, wkv, wide, wo_near,
):
    x = tok[...].astype(F32)
    wide[...] = x
    wo_near[...] = wo[...]
    n = (x * inv_rms(x) * gain[...]).astype(BF16)
    normed[...] = n
    c, s = cos[512:, :], sin[512:, :]
    for half, w in enumerate((wq_m, wq_o)):
        raw = dot(n, w[...])
        for head in range(2):
            a = raw[:, head * HEAD : head * HEAD + HALF]
            b = raw[:, head * HEAD + HALF : (head + 1) * HEAD]
            ra, rb = rotate_pair(a, b, c, s)
            at = half * MINE + head * HEAD
            query[:, at : at + HALF] = (ra * score_scale).astype(BF16)
            query[:, at + HALF : at + HEAD] = (rb * score_scale).astype(BF16)
    for which, (a, b, c, d) in enumerate(((wk_m, wk_o, wv_m, wv_o), (wk_o, wk_m, wv_o, wv_m))):

        @pl.when(where[0] == which)
        def _(parts=(a, b, c, d)):
            for i, part in enumerate(parts):
                wkv[:, i * HALF : (i + 1) * HALF] = part[...]


def attend_body(
    far_two, far_one, normed, wide, query, wkv, gain, wo_m, wo_o, gain_two, cos, sin, pos_row,
    normed_all, query_kept, kv, ctx_m, ctx_o, kept, after, normed_two,
):
    query_kept[...] = query[...]
    normed_all[512:, :] = normed[...]
    for i, far in enumerate((far_two, far_one)):
        x = far[...].astype(F32)
        normed_all[i * 256 : (i + 1) * 256, :] = (x * inv_rms(x) * gain[...]).astype(BF16)
    raw = dot(normed_all[...], wkv[...])
    ka, kb = rotate_pair(raw[:, :HALF], raw[:, HALF:HEAD], cos[...], sin[...])
    kv[:, :HALF] = ka.astype(BF16)
    kv[:, HALF:HEAD] = kb.astype(BF16)
    kv[:, HEAD:] = raw[:, HEAD:].astype(BF16)
    ok = allowed_pairs(pos_row)
    for head in range(HEADS):
        cols = slice(head * HEAD, (head + 1) * HEAD)
        scores = jnp.where(ok, dot_nt(query[:, cols], kv[:, :HEAD]), neg_fill)
        top = jnp.max(scores, axis=-1, keepdims=True)
        exps = jnp.exp(scores - top)
        total = jnp.sum(exps, axis=-1, keepdims=True)
        probs = exps * (1.0 / total)
        kept[head] = probs
        probs = probs.astype(BF16)
        context = (ctx_m, ctx_o)[head // 2]
        at = head % 2 * HEAD
        context[:, at : at + HEAD] = dot(probs, kv[:, HEAD:]).astype(BF16)
    h = wide[...] + (dot(ctx_m[...], wo_m[...]) + dot(ctx_o[...], wo_o[...]))
    after[...] = h
    normed_two[...] = (h * inv_rms(h) * gain_two[...]).astype(BF16)


FFN_STEP = 1024


def ffn_half(n, y, wg, wu, wd, hid, dg, du):
    total = None
    grad_n = None
    for at in range(0, FF // 2, FFN_STEP):
        cols = slice(at, at + FFN_STEP)
        gate = dot(n, wg[:, cols])
        up = dot(n, wu[:, cols])
        grad_hidden = dot_nt(y, wd[cols, :])
        square = gate * gate
        t = jnp.tanh(gelu_c * gate * (1.0 + gelu_k * square))
        one_t = 0.5 + 0.5 * t
        act = gate * one_t
        slope = one_t + 0.5 * gate * (1.0 - t * t) * (gelu_c * (1.0 + 3.0 * gelu_k * square))
        hidden = (act * up).astype(BF16)
        grad_gate = (grad_hidden * up * slope).astype(BF16)
        grad_up = (grad_hidden * act).astype(BF16)
        hid[:, cols] = hidden
        dg[:, cols] = grad_gate
        du[:, cols] = grad_up
        part = dot(hidden, wd[cols, :])
        total = part if total is None else total + part
        part = dot_nt(grad_gate, wg[:, cols]) + dot_nt(grad_up, wu[:, cols])
        grad_n = part if grad_n is None else grad_n + part
    return total, grad_n


def ffn_other_body(normed_two, gy, wg, wu, wd, hid, dg, du, total, grad_n):
    total[...], grad_n[...] = ffn_half(normed_two[...], gy[...], wg, wu, wd, hid, dg, du)


def ffn_body(
    after, normed_two, gain_two, gy, wg, wu, wd, total_o, grad_n_o,
    out, hid, dg, du, grad_after, grad_after_low, grad_gain,
):
    y = gy[...]
    total, grad_n = ffn_half(normed_two[...], y, wg, wu, wd, hid, dg, du)
    grad_n = grad_n + grad_n_o[...]
    h = after[...]
    out[...] = (h + (total + total_o[...])).astype(BF16)
    r = inv_rms(h)
    dn = grad_n * gain_two[...]
    grad_gain[...] = jnp.sum(grad_n * h * r, axis=0, keepdims=True)
    ga = y.astype(F32) + r * dn - h * (r * r * r * jnp.mean(dn * h, axis=-1, keepdims=True))
    grad_after[...] = ga
    grad_after_low[...] = ga.astype(BF16)


ORDER = (0, 2, 1, 3)
F_ROWS = 3840
A_ROWS = 1664


def place(i, by):
    return lax.rem(i + by, 4)


def y_places(core, y):
    one = y + 1 - 2 * lax.rem(y, 2)
    other = 3 - y
    first = jnp.where(core == 0, one, other)
    second = jnp.where(core == 0, other, one)
    return y, second, first, 2 - y + 2 * lax.rem(y, 2)


def ffn_grads_body(
    where, hid_m, hid_r, dg_m, dg_r, du_m, du_r, n, n_r, gy, gy_r, out_0, out_1, out_2, out_3, turned
):
    first = where[1]
    turned[:, :256] = n[...].T
    turned[:, 256:] = n_r[...].T
    for out, by in zip((out_0, out_1, out_2, out_3), ORDER):
        j = place(first, by)
        cols = pl.ds(pl.multiple_of(j * 256, 256), 256)
        for at, left, right in ((0, dg_m, dg_r), (1280, du_m, du_r)):
            g = dot(turned[:, :256], left[:, cols]) + dot(turned[:, 256:], right[:, cols])
            out[at : at + 640, :] = g[:, :128].astype(BF16)
            out[at + 640 : at + 1280, :] = g[:, 128:].astype(BF16)
        g = dot_tn(hid_m[:, cols], gy[...]) + dot_tn(hid_r[:, cols], gy_r[...])
        for b in range(5):
            out[2560 + b * 256 : 2816 + b * 256, :] = g[:, b * 128 : (b + 1) * 128].astype(BF16)


def attend_grad_body(
    where, query, kv, kept, ga_low, wo_m, wo_o, cos, sin,
    dq_m, dq_o, dkv, back_two, back_one, dkv_m, packed,
):
    dkv_o = packed.at[512:, :]
    ga = ga_low[...]
    grad_k = None
    grad_v = None
    c, s = cos[512:, :], sin[512:, :]
    for half, wo, dq in ((1, wo_o, dq_o), (0, wo_m, dq_m)):
        grad_context = dot_nt(ga, wo[...]).astype(BF16)
        for head in range(2):
            cols = slice(half * MINE + head * HEAD, half * MINE + (head + 1) * HEAD)
            q = query[:, cols]
            gc = grad_context[:, head * HEAD : (head + 1) * HEAD]
            which = half * 2 + head
            probs = kept[which]
            part = dot_tn(probs.astype(BF16), gc)
            grad_v = part if grad_v is None else grad_v + part
            grad_probs = dot_nt(gc, kv[:, HEAD:])
            row_dot = jnp.sum(grad_probs * probs, axis=-1, keepdims=True)
            grad_scores = (probs * (grad_probs - row_dot)).astype(BF16)
            gq = dot(grad_scores, kv[:, :HEAD]) * score_scale
            a, b = rotate_pair(gq[:, :HALF], gq[:, HALF:], c, -s)
            dq[:, head * HEAD : head * HEAD + HALF] = a.astype(BF16)
            dq[:, head * HEAD + HALF : (head + 1) * HEAD] = b.astype(BF16)
            part = dot_tn(grad_scores, q)
            grad_k = part if grad_k is None else grad_k + part
    a, b = rotate_pair(grad_k[:, :HALF], grad_k[:, HALF:], cos[...], -sin[...])
    packed[:256, :] = dq_o[:, :HEAD]
    packed[256:512, :] = dq_o[:, HEAD:]
    for rows, out in ((0, back_two), (256, back_one), (512, dkv)):
        rows = slice(rows, rows + 256)
        out[:, :HALF] = a[rows, :].astype(BF16)
        out[:, HALF:HEAD] = b[rows, :].astype(BF16)
        out[:, HEAD:] = grad_v[rows, :].astype(BF16)
    even = where[0] == 0
    dkv_m[:, :HALF] = jnp.where(even, a, b).astype(BF16)
    dkv_o[:, :HALF] = jnp.where(even, b, a).astype(BF16)
    va, vb = grad_v[:, :HALF], grad_v[:, HALF:]
    dkv_m[:, HALF:] = jnp.where(even, va, vb).astype(BF16)
    dkv_o[:, HALF:] = jnp.where(even, vb, va).astype(BF16)


def attend_grads_body(
    where, n, n_r, dq_m, dkv_m, packed, ctx, ctx_r, ga, ga_r, wq, wk, wv,
    gain, gain_two_grad, out_0, out_1, out_2, out_3, turned,
):
    turned[:, :768] = n[...].T
    turned[:, 768:] = n_r[...].T
    gk = dot(turned[:, :768], dkv_m[...]) + dot(turned[:, 768:], packed[512:, :])
    weighed = gk[:, :HALF] * wk[...].astype(F32) + gk[:, HALF:] * wv[...].astype(F32)
    gk = gk.astype(BF16)
    for out, j in zip((out_0, out_1, out_2, out_3), y_places(where[0], where[3])):
        cols = pl.ds(pl.multiple_of(j * 128, 128), 128)
        rows = pl.ds(pl.multiple_of(j // 2 * 256, 256), 256)
        half = pl.ds(pl.multiple_of(j % 2 * 128, 128), 128)
        g = dot(turned[:, 512:768], dq_m[:, cols]) + dot(turned[:, 1280:], packed[rows, half])
        weighed = weighed + g * wq[:, cols].astype(F32)
        out[:640, :] = g.astype(BF16)
        g = dot_tn(ctx[:, cols], ga[...]) + dot_tn(ctx_r[:, cols], ga_r[...])
        for b in range(5):
            out[960 + b * 128 : 1088 + b * 128, :] = g[:, b * 128 : (b + 1) * 128].astype(BF16)
        for at in range(4):

            @pl.when(j == at)
            def _(out=out, at=at):
                out[640:800, :] = gk[at * 160 : (at + 1) * 160, :HALF]
                out[800:960, :] = gk[at * 160 : (at + 1) * 160, HALF:]

    by_row = jnp.broadcast_to(jnp.sum(weighed, axis=1, keepdims=True), (640, 128))
    one = by_row.T[:1, :] / gain[...]
    two = gain_two_grad[...]
    rows = [v[:, b * 128 : (b + 1) * 128] for v in (one, two) for b in range(5)]
    block = jnp.concatenate([*rows, jnp.zeros((6, 128), F32)], axis=0).astype(BF16)
    for out in (out_0, out_1, out_2, out_3):
        out[1600:1616, :] = block
        out[1616:, :] = jnp.zeros((48, 128), BF16)


def token_grad_body(
    where, tok, gain, grad_after, dq_m, dq_o, dkv, back_one, back_two, wq_m, wq_o, wkv, small,
    small_r, out, gain_one_out, gain_two_out,
):
    sums = small[...].astype(F32) + small_r[...].astype(F32)
    for at, target in ((0, gain_one_out), (5, gain_two_out)):
        whole = jnp.concatenate([sums[at + b : at + b + 1, :] for b in range(5)], axis=1)
        half = jnp.where(where[0] == 0, whole[:, : D // 2], whole[:, D // 2 :])
        target[...] = half.reshape(D // 2)
    back = back_one[...].astype(F32) + back_two[...].astype(F32)
    own = (dkv[...].astype(F32) + back).astype(BF16)
    gn = dot_nt(dq_m[...], wq_m[...]) + dot_nt(dq_o[...], wq_o[...]) + dot_nt(own, wkv[...])
    x = tok[...].astype(F32)
    r = inv_rms(x)
    dm = gn * gain[...]
    out[...] = grad_after[...] + r * dm - x * (
        r * r * r * jnp.mean(dm * x, axis=-1, keepdims=True)
    )


def add_low(*terms):
    total = terms[0].astype(F32)
    for term in terms[1:]:
        total = total + term.astype(F32)
    return total.astype(BF16)


F_PART, A_PART = F_ROWS // 4, A_ROWS // 4
PART = F_PART + A_PART


def split_sum_body(
    where, own, r_two, r_one, r_minus, a_own, a_one, a_last, out_0, out_1, out_2, out_3
):
    for out, by in zip((out_0, out_1, out_2, out_3), ORDER):
        j = place(where[2], by)
        at = pl.ds(pl.multiple_of(j * F_PART, F_PART), F_PART)
        total = (own[at, :].astype(F32) + r_two[at, :].astype(F32)) + (
            r_one[at, :].astype(F32) + r_minus[at, :].astype(F32)
        )
        out[:F_PART, :] = total.astype(BF16)
        at = pl.ds(pl.multiple_of(j * A_PART, A_PART), A_PART)
        total = a_own[at, :].astype(F32) + a_one[at, :].astype(F32) + a_last[at, :].astype(F32)
        out[F_PART:, :] = total.astype(BF16)


def sum_four(own, r_two, r_one, r_minus):
    total = (own.astype(F32) + r_two.astype(F32)) + (r_one.astype(F32) + r_minus.astype(F32))
    return total.astype(BF16)


def join_body(where, own, r_two, r_one, r_minus, _, f_out, a_out, small):
    for ref, by in ((own, 0), (r_two, 2), (r_one, 3), (r_minus, 1)):
        j = place(where[2], by)
        f_out[pl.ds(pl.multiple_of(j * F_PART, F_PART), F_PART), :] = ref[:F_PART, :]
        a_out[pl.ds(pl.multiple_of(j * A_PART, A_PART), A_PART), :] = ref[F_PART:, :]
    small[...] = a_out[1600:1616, :]


SHARDS = ((D, FF // 2), (D, FF // 2), (FF // 2, D), (D, MINE), (D, HALF), (D, HALF), (MINE, D))
F_WIDE = ((D, 256), (D, 256), (256, D))
A_WIDE = ((D, 128), (160, 128), (160, 128), (128, D))


def spread_body(f_places, a_places, fresh, where, *refs):
    f_count, a_count = len(f_places), len(a_places)
    f_pieces, a_pieces = refs[:f_count], refs[f_count : f_count + a_count]
    refs = refs[f_count + a_count + (0 if fresh else len(SHARDS)) :]
    gate, up, down, query, key, value, out = refs[:7]
    sems = refs[-1]
    f_wide, a_wide = refs[7:10], refs[10:14]
    copies = []

    def send(source, target):
        copies.append(pltpu.make_async_copy(source, target, sems.at[len(copies)]))
        copies[-1].start()

    for i, (piece, by) in enumerate(zip(f_pieces, f_places)):
        j = place(where[1], by)
        cols = pl.ds(pl.multiple_of(j * 256, 256), 256)
        for at, wide, target in ((0, f_wide[0], gate), (1280, f_wide[1], up)):
            for b in range(2):
                wide[i, :, b * 128 : (b + 1) * 128] = piece[
                    at + b * 640 : at + (b + 1) * 640, :
                ].astype(F32)
            send(wide.at[i], target.at[:, cols])
        for b in range(5):
            at = 2560 + b * 256
            f_wide[2][i, :, b * 128 : (b + 1) * 128] = piece[at : at + 256, :].astype(F32)
        send(f_wide[2].at[i], down.at[cols, :])
    for i, (piece, (by, apart)) in enumerate(zip(a_pieces, a_places)):
        j = place(where[3], by + apart * where[0])
        block = pl.ds(pl.multiple_of(j * 128, 128), 128)
        rows = pl.ds(pl.multiple_of(j * 160, 32), 160)
        a_wide[0][i] = piece[:640, :].astype(F32)
        send(a_wide[0].at[i], query.at[:, block])
        a_wide[1][i] = piece[640:800, :].astype(F32)
        send(a_wide[1].at[i], key.at[rows, :])
        a_wide[2][i] = piece[800:960, :].astype(F32)
        send(a_wide[2].at[i], value.at[rows, :])
        for b in range(5):
            at = 960 + b * 128
            a_wide[3][i, :, b * 128 : (b + 1) * 128] = piece[at : at + 128, :].astype(F32)
        send(a_wide[3].at[i], out.at[block, :])
    for copy in copies:
        copy.wait()


def spread(where, f_pieces, f_places, a_pieces, a_places, shards):
    f_count, a_count = len(f_pieces), len(a_pieces)
    anywhere = pl.BlockSpec(memory_space=pl.ANY)
    return pl.pallas_call(
        functools.partial(spread_body, f_places, a_places, not shards),
        out_shape=[jax.ShapeDtypeStruct(s, F32) for s in SHARDS],
        in_specs=[
            pl.BlockSpec(memory_space=pltpu.SMEM),
            *[pl.BlockSpec(memory_space=pltpu.VMEM)] * (f_count + a_count),
            *[anywhere] * len(shards),
        ],
        out_specs=[anywhere] * len(SHARDS),
        input_output_aliases={1 + f_count + a_count + i: i for i in range(len(shards))},
        scratch_shapes=[
            *[pltpu.VMEM((f_count, *s), F32) for s in F_WIDE],
            *[pltpu.VMEM((max(a_count, 1), *s), F32) for s in A_WIDE],
            pltpu.SemaphoreType.DMA((3 * f_count + 4 * a_count,)),
        ],
        compiler_params=pltpu.CompilerParams(vmem_limit_bytes=20 * MIB),
        cost_estimate=pl.CostEstimate(flops=1024, bytes_accessed=1024, transcendentals=0),
        name="spread",
    )(where, *f_pieces, *a_pieces, *shards)


def local(
    tokens, positions, gain_attn, w_query, w_key, w_value, w_out, gain_ffn, w_gate, w_up, w_down,
    grad_out,
):
    tok = tokens[0]
    gy = grad_out[0]
    rows = tok.shape[0]
    ctx = lax.axis_index("ctx")
    core = lax.axis_index("fsdp")
    x_at, z_at, y_at = ctx // 16, ctx // 4 % 4, ctx % 4
    where = jnp.stack(
        [core, jnp.where(core == 0, x_at, z_at), jnp.where(core == 0, z_at, x_at), y_at]
    ).astype(jnp.int32)
    even = core == 0

    far_one = passed_along(tok, 1)
    far_two = passed_along(tok, 2)
    gains = jnp.concatenate([gain_attn, gain_ffn]).reshape(1, D)
    gains_other = swap(gains)
    key_other, value_other = swap(w_key), swap(w_value)
    query_other = swap(after(w_query, gains_other))
    out_other = swap(after(w_out, key_other))

    low = jnp.where(even, gains, gains_other)
    high = jnp.where(even, gains_other, gains)
    half_d = D // 2
    gain_one = jnp.concatenate([low[:, :half_d], high[:, :half_d]], axis=1).astype(F32)
    gain_two = jnp.concatenate([low[:, half_d:], high[:, half_d:]], axis=1).astype(F32)
    seq_pos = positions[0]
    key_pos = lax.dynamic_slice_in_dim(
        jnp.concatenate([jnp.full((2 * rows,), -2 * WINDOW, jnp.int32), seq_pos]), ctx * rows,
        3 * rows,
    )
    pos_row = key_pos.reshape(1, 3 * rows)
    frequency = rope_base ** (-(jnp.arange(HALF, dtype=F32) * 2.0 / HEAD))
    angles = key_pos.astype(F32)[:, None] * frequency[None, :]
    cos, sin = jnp.cos(angles), jnp.sin(angles)

    gy_r = swap(after(gy, value_other))
    normed, query, wkv, wide, wo_near = call(
        "query", query_body,
        [
            ((rows, D), BF16), ((rows, HEADS * HEAD), BF16), ((D, 2 * HEAD), BF16),
            ((rows, D), F32), ((MINE, D), BF16),
        ],
        [
            where, after(tok, gain_two, pos_row), gain_one, w_query, query_other, w_key,
            key_other, w_value, value_other, w_out, cos, sin,
        ],
        us=6, scalars=1,
    )
    first = (normed, far_one, far_two, out_other, gy_r)
    gate_other = swap(after(w_gate, out_other, query_other))
    up_other = swap(after(w_up, *first))
    down_other = swap(after(w_down, *first))
    normed_all, query, kv, ctx_m, ctx_o, kept, after_attn, normed_two = call(
        "attend", attend_body,
        [
            ((3 * rows, D), BF16), ((rows, HEADS * HEAD), BF16), ((3 * rows, 2 * HEAD), BF16),
            ((rows, MINE), BF16), ((rows, MINE), BF16), ((HEADS, rows, 3 * rows), F32), ((rows, D), F32),
            ((rows, D), BF16),
        ],
        [
            far_two, far_one, normed, wide, query, wkv, after(gain_one, gate_other), wo_near,
            out_other, gain_two,
            cos, sin, pos_row,
        ],
        us=5,
    )
    half_ffn = [((rows, FF // 2), BF16)] * 3
    hid_o, dg_o, du_o, total_o, grad_n_o = call(
        "ffn_other", ffn_other_body, [*half_ffn, ((rows, D), F32), ((rows, D), F32)],
        [normed_two, gy, gate_other, up_other, down_other],
        us=5,
    )
    hid_r, dg_r, du_r = swap(hid_o), swap(dg_o), swap(du_o)
    normed_two_r, normed_r = swap(after(normed_two, hid_o)), swap(after(normed_all, hid_o))
    ctx_r = swap(after(ctx_o, hid_r))
    out, hid_m, dg_m, du_m, grad_after, ga_low, grad_gain_two = call(
        "ffn", ffn_body,
        [((rows, D), BF16), *half_ffn, ((rows, D), F32), ((rows, D), BF16), ((1, D), F32)],
        [after_attn, normed_two, gain_two, gy, w_gate, w_up, w_down, total_o, grad_n_o],
        us=4,
    )
    ga_r = swap(ga_low)
    dq_m, dq_o, dkv, back_two, back_one, dkv_m, packed = call(
        "attend_grad", attend_grad_body,
        [
            ((rows, MINE), BF16), ((rows, MINE), BF16), *[((rows, 2 * HEAD), BF16)] * 3,
            ((3 * rows, HEAD), BF16), ((5 * rows, HEAD), BF16),
        ],
        [
            where, query, kv, kept, ga_low, w_out, out_other, cos, sin,
        ],
        us=0, scalars=1,
    )
    packed_r = swap(packed)
    f_chunks = call(
        "ffn_grads", ffn_grads_body, [((F_ROWS, 128), BF16)] * 4,
        [where, after(hid_m, packed), hid_r, dg_m, dg_r, du_m, du_r, normed_two, normed_two_r, gy, gy_r],
        scalars=1, scratch=[pltpu.VMEM((D, 512), BF16)],
        us=3,
    )
    f_got = [
        lax.ppermute(f_chunks[i], ("ctx", "fsdp"), shift_first(by)) for i, by in ((2, 1), (3, -1), (1, 2))
    ]
    f_got = [f_got[2], f_got[0], f_got[1]]

    a_chunks = call(
        "attend_grads", attend_grads_body, [((A_ROWS, 128), BF16)] * 4,
        [
            where, normed_all, normed_r, after(dq_m, f_chunks[0]), dkv_m, packed_r, ctx_m, ctx_r, ga_low, ga_r,
            w_query, w_key, w_value, gain_one, grad_gain_two,
        ],
        us=0, scalars=1, scratch=[pltpu.VMEM((D, 6 * rows), BF16)],
    )
    a_own, a_next, a_far_own, a_far_next = a_chunks
    a_next_r, a_own_r = swap_y(a_far_next, 0), swap_y(a_far_own, 0)
    a_last_r = swap_y(add_low(a_next, a_next_r), 1)
    parts = call(
        "split", split_sum_body, [((PART, 128), BF16)] * 4,
        [where, after(f_chunks[0], a_own), *f_got, a_own, a_own_r, a_last_r], us=0, scalars=1,
    )
    got = [parts[0], *to_peers(parts[1:], shift_second)]
    f_two = sum_four(*[part[:F_PART] for part in got])
    a_two = sum_four(*[part[F_PART:] for part in got])
    f_pair = add_low(f_two, swap_y(f_two, 0))
    a_pair = add_low(a_two, swap_first(a_two, 0))
    f_three = add_low(f_pair, swap_y(f_pair, 1))
    back_two = passed_along(after(back_two, f_two), -2)
    back_one = passed_along(after(back_one, f_two), -1)
    turn = swap(after(swap(after(grad_gain_two, back_one, back_two)), f_pair))
    a_three = add_low(a_pair, swap_first(after(a_pair, f_pair), 1))
    own, turn = lax.optimization_barrier((jnp.concatenate([f_three, a_three]), turn))
    f_whole, a_whole, small = call(
        "join", join_body,
        [((F_ROWS, 128), BF16), ((A_ROWS, 128), BF16), ((16, 128), BF16)],
        [where, own, *to_peers([own] * 3, shift_second), turn], us=0, scalars=1,
    )
    small_r = swap(small)
    everywhere = ("ctx", "fsdp")
    f_send, a_send = after(f_whole, small_r), after(a_whole, small_r)
    f_got = to_peers([f_send] * 3, shift_first)
    a_two = lax.ppermute(a_send, everywhere, shift_y(2))
    a_one = lax.ppermute(a_send, everywhere, shift_apart(1))
    grad_tokens, g_gain_one, g_gain_two = call(
        "token_grad", token_grad_body, [((rows, D), F32), ((half_d,), F32), ((half_d,), F32)],
        [
            where, tok, gain_one, grad_after, dq_m, dq_o, dkv, back_one, back_two, w_query,
            query_other, wkv, small, small_r,
        ],
        us=2, scalars=1,
    )

    shards = spread(where, [after(f_whole, grad_tokens)], (0,), [a_whole], ((0, 0),), [])
    a_other = lax.ppermute(after(a_send, f_got[0]), everywhere, shift_apart(-1))
    shards = spread(where, f_got[:1], (2,), [a_two], ((2, 0),), shards)
    g_gate, g_up, g_down, g_query, g_key, g_value, g_out = spread(
        where, f_got[1:], (3, 1), [a_one, a_other], ((3, -2), (1, 2)), shards
    )
    return (
        out[None], grad_tokens[None], g_gain_one, g_query, g_key, g_value, g_out, g_gain_two,
        g_gate, g_up, g_down,
    )


def solution(mesh):
    tokens = P("fsdp", "ctx", None)
    columns, rows = P(None, "fsdp"), P("fsdp", None)
    in_specs = (
        tokens, P("fsdp", None), P("fsdp"), columns, columns, columns, rows, P("fsdp"), columns,
        columns, rows, tokens,
    )
    out_specs = (
        tokens, tokens, P("fsdp"), columns, columns, columns, rows, P("fsdp"), columns, columns,
        rows,
    )
    return jax.shard_map(local, mesh=mesh, in_specs=in_specs, out_specs=out_specs, check_vma=False)
```
